128 devices in a mesh: lat: 32 (over y, x, core), lon: 4 (over z).
Axes of the slice: x: 4, y: 4, z: 4, core: 2. Of those that a mesh axis runs over, the one named last changes fastest.
Arguments:
- terminal: float32 [2, 256, 100, 2048], P(None, 'lat', None, 'lon'), may hold values from -6 to 6
- courant: float32 [4, 256, 100, 2048], P(None, 'lat', None, 'lon'), may hold values from 0.02 to 0.24
- inverse: float32 [256, 100, 100], P('lat'), may hold values from -1.5 to 1.5
- land_mask: int32 [256, 2048], P('lat', 'lon'), may hold values 0 or 1
- obs_values: float32 [262144, 128], P(('lat', 'lon')), may hold values from -6 to 6
- obs_owner: int32 [262144, 1], P(('lat', 'lon')), may hold values from 0 to 127; in each aligned block of 2048 rows (0 to 2047, 2048 to 4095, ...) at most 32 rows name the same one
- obs_cell: int32 [262144], P(('lat', 'lon')), may hold values from 0 to 6399
Outputs:
- adjoint: float32 [2, 256, 100, 2048], P(None, 'lat', None, 'lon')
The draws below stay inside these ranges and needn't reach their ends.
Inputs may be any that keep to these rules, and one draw needn't show every extreme that they name: `obs_owner`: among the 2048 blocks of one device at most 32 name the same tile, a bound that some block reaches of them.
All inputs are finite; a program needn't handle non-finite values. No bound on the sum of `land_mask` on one device may be relied on, other than what follows from the above.
Results may differ from the reference program's by a relative error of at most 0.0001.
Values sent between devices are 32-bit elements; how exact they have to be, the bound alone decides.
No kernel may reach another device: no remote copies, remote signals or barrier semaphores. Data moves between devices by JAX's collectives and lax.ppermute only.
A program may use at most 128 MiB of HBM per device.

```python
import math
import jax
import jax.numpy as jnp
import numpy as np
from jax import lax

NZ = 100
VALS = 128
STEPS = 2
LAT_DEV = 8
LON_DEV = 512
OBS_DEV = 2048
NLAT = 256
NLON = 2048
OBS_ALL = 262144
CAP = 32
CELLS = 6400
N_LAT = 32
N_LON = 4
DEVICES = 128


def draw_inverse(key, part):
    key = jax.random.fold_in(key, 7)
    diag_key, spread_key = jax.random.split(key)
    diagonal = jax.random.uniform(diag_key, (NLAT, NZ), jnp.float32, 0.6, 1.0)
    spread = jnp.clip(jax.random.normal(spread_key, (NLAT, NZ, NZ), jnp.float32), -4.0, 4.0) * (0.45 / math.sqrt(NZ))
    return spread + diagonal[:, :, None] * jnp.eye(NZ, dtype=jnp.float32)[None, :, :]


def set_ends(values, key, smallest, top_value):
    longest = values.shape.index(max(values.shape))
    spots = []
    for shift in (0, 1):
        where = [jax.random.randint(jax.random.fold_in(key, axis), (), 0, length) for axis, length in enumerate(values.shape)]
        where[longest] = (where[longest] + shift) % values.shape[longest]
        spots.append(tuple(where))
    return values.at[spots[0]].set(smallest).at[spots[1]].set(top_value)


def level_of(own_key, extent, cuts, least, largest):
    level = 1.0
    for dim, parts in cuts:
        heights = jax.random.uniform(jax.random.fold_in(jax.random.fold_in(own_key, 6), dim), (parts,), jnp.float32, least / len(cuts), largest / len(cuts))
        level = level * jnp.repeat(jnp.exp(heights), extent[dim] // parts).reshape((-1,) + (1,) * (len(extent) - 1 - dim))
    return level


def routed_block(key, own, number, rows, amount, top, most, lean):
    sequence = jax.random.permutation(key, amount)
    packed, common = load_shares(amount, rows * top, most, lean, True), load_shares(amount, rows * top, most, lean, False)
    places = jnp.arange(amount)

    def named(sizes, offset_by):
        used = int((sizes > 0).sum())
        fixed = max(1, used // 4)
        passed = fixed + (places - fixed + offset_by * (used - fixed)) % max(1, amount - fixed)
        return jnp.zeros((amount,), jnp.int32).at[sequence[jnp.where(places < fixed, places, passed)]].set(jnp.asarray(sizes, jnp.int32))

    sizes = jnp.where(number % 4 == 0, named(packed, number // 4), named(common, number - number // 4 - 1))
    mixed = jax.random.permutation(jax.random.fold_in(own, 3), amount)
    donor, receiver = mixed[0:amount // 2 * 2:2], mixed[1:amount // 2 * 2:2]
    margin = jnp.minimum(sizes[donor] - 1, most - sizes[receiver]) // 2
    margin = jnp.where((donor == sequence[0]) | (receiver == sequence[0]) | (sizes[receiver] == 0), 0, jnp.maximum(margin, 0))
    passed = jax.random.randint(jax.random.fold_in(own, 4), (amount // 2,), 0, 1 << 20) % (margin + 1)
    sizes = sizes.at[donor].add(-passed).at[receiver].add(passed)
    members = jnp.searchsorted(jnp.cumsum(sizes), jnp.arange(rows * top), side="right").astype(jnp.int32)
    grid = members.reshape(top, rows).T
    grid = grid[jax.random.permutation(jax.random.fold_in(own, 1), rows)]
    offset_by = jax.random.randint(jax.random.fold_in(own, 2), (rows, 1), 0, top)
    return jnp.take_along_axis(grid, (jnp.arange(top)[None, :] + offset_by) % top, axis=1)


def load_shares(count, total, reach, slope, full):
    portions = [(1 << 20) // math.isqrt(standing ** slope) + 1 for standing in range(1, count + 1)]
    largest = reach if full else min(reach, max(-(-total // count), total * portions[0] // sum(portions)))
    least = 1 if total - largest >= count - 1 else 0
    counts, surplus = [largest] + [least] * (count - 1), total - largest - least * (count - 1)
    while surplus > 0:
        free = [i for i in range(1, count) if counts[i] < largest] or [i for i in range(1, count) if counts[i] < reach]
        whole, budget = sum([portions[i] for i in free]), surplus
        for i in free:
            more = min(reach - counts[i], max(1, budget * portions[i] // whole), surplus)
            counts[i] = counts[i] + more
            surplus = surplus - more
    return np.array(counts)


def noise(rng, extent, scale, bound, pieces=(), held_as=jnp.bfloat16):
    values = scale * jax.random.normal(rng, extent, jnp.float32)
    if pieces:
        values = values * level_of(rng, extent, pieces, -0.22, 0.18)
    return jnp.clip(values, -bound, bound).astype(held_as)


def setup_inputs(seed: int = 0) -> dict:
    key_list = jax.random.split(jax.random.key(seed), 8)
    terminal = noise(key_list[0], (2, NLAT, NZ, NLON), 1.0, 6.0, ((1, 32), (3, 4)), jnp.float32)
    courant = jnp.clip(jnp.exp(math.log(0.24) - 2.4849066 * jax.random.uniform(key_list[1], (4, NLAT, NZ, NLON), jnp.float32) ** level_of(key_list[1], (4, NLAT, NZ, NLON), ((1, 32), (3, 4)), -0.2, 0.2)), 0.02, 0.24)
    inverse = draw_inverse(jax.random.fold_in(key_list[7], 71), 0)
    land_mask = set_ends((jax.random.randint(key_list[3], (NLAT, NLON), 0, 5) < 4).astype(jnp.int32), jax.random.fold_in(key_list[3], 1), 0, 1)
    obs_values = noise(key_list[4], (OBS_ALL, VALS), 1.0, 6.0, ((0, 128),), jnp.float32)
    obs_owner_keys = jax.random.split(jax.random.fold_in(key_list[5], 1), OBS_ALL // OBS_DEV)
    obs_owner_turns = jax.random.permutation(jax.random.fold_in(key_list[5], 3), OBS_ALL // OBS_DEV)
    obs_owner = jax.vmap(lambda own, number: routed_block(jax.random.fold_in(key_list[5], 2), own, number, OBS_DEV, DEVICES, 1, CAP, 2))(obs_owner_keys, obs_owner_turns).reshape((OBS_ALL, 1))
    obs_cell = set_ends(jax.random.randint(key_list[6], (OBS_ALL,), 0, CELLS), jax.random.fold_in(key_list[6], 1), 0, CELLS - 1).astype(jnp.int32)
    return {"terminal": terminal, "courant": courant, "inverse": inverse, "land_mask": land_mask, "obs_values": obs_values, "obs_owner": obs_owner, "obs_cell": obs_cell}


def transport(vertical, courant):
    zero_row = jnp.zeros_like(vertical[:, :1])
    north_side = jnp.concatenate([vertical[:, 1:], zero_row], axis=1)
    south_side = jnp.concatenate([zero_row, vertical[:, :-1]], axis=1)
    east_side = jnp.roll(vertical, -1, axis=3)
    west_side = jnp.roll(vertical, 1, axis=3)
    return (vertical + courant[0] * (east_side - vertical) + courant[1] * (west_side - vertical)
            + courant[2] * (north_side - vertical) + courant[3] * (south_side - vertical))


def reference(terminal, courant, inverse, land_mask, obs_values, obs_owner, obs_cell):
    owners = obs_owner[:, 0].astype(jnp.int32)
    global_rows = owners * CELLS + obs_cell.astype(jnp.int32)
    flat_forcing = jnp.zeros((DEVICES * CELLS, VALS), jnp.float32).at[global_rows].add(obs_values)
    tiled = flat_forcing.reshape(N_LAT, N_LON, 2, LAT_DEV, NZ, LON_DEV)
    forcing = jnp.transpose(tiled, (2, 0, 3, 4, 1, 5)).reshape(2, NLAT, NZ, NLON)
    state = terminal + forcing
    ocean = land_mask.astype(jnp.float32)[None, :, None, :]
    for repeat in range(STEPS):
        vertical = jnp.einsum("jmk,tjmx->tjkx", inverse, state, precision=lax.Precision.HIGHEST)
        state = ocean * transport(vertical, courant)
    return state
```

```python
import functools

import jax
import jax.numpy as jnp
from jax import lax
from jax.experimental import pallas as pl
from jax.experimental.pallas import tpu as pltpu
from jax.sharding import PartitionSpec as P

STEPS = 2
LANES = 128
SLOTS = 33
BANKS = 4
MIB = 1 << 20


def padded_levels(levels):
    return -(-levels // 8) * 8


def pack_kernel(geometry, owner_ref, cell_ref, values_ref, send_ref, slot_ref, slots, pay, sem):
    levels, high, columns, devices = geometry
    per_row = levels * columns
    chunks = owner_ref.shape[0]
    f32, bf16 = jnp.float32, jnp.bfloat16
    sub = lax.broadcasted_iota(jnp.int32, (LANES, LANES), 0)
    lane = lax.broadcasted_iota(jnp.int32, (LANES, LANES), 1)
    before = jnp.concatenate(
        [jnp.where(sub < lane, 1.0, 0.0), jnp.ones((LANES, LANES), f32)], axis=1
    ).astype(bf16)
    cells = cell_ref[...]
    tile_row = ((cells >> 4) * 5243) >> 17
    rest = cells - tile_row * per_row
    level = rest >> 2
    column = rest & 3
    place = (tile_row * columns + column) * high + level
    upper, lower = (place >> 6).astype(f32), (place & 63).astype(f32)
    carry = jnp.zeros((LANES, LANES), f32)
    total = jnp.zeros((LANES, LANES), f32)
    for i in range(chunks):
        own = owner_ref[i : i + 1, :]
        hot = jnp.where(sub == own, 1.0, 0.0)
        hot16 = hot.astype(bf16)
        counted = jnp.dot(hot16, before, preferred_element_type=f32)
        rank = jnp.sum(hot * (counted[:, :LANES] + carry), axis=0, keepdims=True)
        carry = carry + counted[:, LANES:]
        rank_i = rank.astype(jnp.int32)
        slots[i : i + 1, :] = own * SLOTS + rank_i
        parts = jnp.where(
            sub == rank_i,
            jnp.broadcast_to(upper[i : i + 1, :], (LANES, LANES)),
            jnp.where(sub == rank_i + 32, jnp.broadcast_to(lower[i : i + 1, :], (LANES, LANES)), 0.0),
        ).astype(bf16)
        total = total + lax.dot_general(
            hot16, parts, (((1,), (1,)), ((), ())), preferred_element_type=f32
        )
    copy = pltpu.make_async_copy(slots, slot_ref, sem)
    copy.start()
    places = total * 64.0 + pltpu.roll(total, LANES - 32, 1)
    dump = f32(2 * 8 * columns * high)
    pay[...] = jnp.where(
        lane < 32, jnp.where(lane.astype(f32) < carry, places, dump), carry
    )
    for o in range(devices):
        send_ref[o * SLOTS + 32] = pay[o : o + 1, :]
    copy.wait()
    unroll = 16
    for i in range(chunks):

        @pl.loop(0, LANES // unroll)
        def _(c):
            base = c * unroll
            for u in range(unroll):
                send_ref[slot_ref[i, base + u]] = values_ref[i * LANES + base + u]


def pack(owner, cell, values, levels, high, columns, devices):
    rows = values.shape[0]
    return pl.pallas_call(
        functools.partial(pack_kernel, (levels, high, columns, devices)),
        out_shape=jax.ShapeDtypeStruct((devices * SLOTS, 1, LANES), jnp.float32),
        in_specs=[pl.BlockSpec(memory_space=pltpu.VMEM)] * 3,
        out_specs=pl.BlockSpec(memory_space=pltpu.VMEM),
        scratch_shapes=[
            pltpu.SMEM((rows // LANES, LANES), jnp.int32),
            pltpu.VMEM((rows // LANES, LANES), jnp.int32),
            pltpu.VMEM((LANES, LANES), jnp.float32),
            pltpu.SemaphoreType.DMA,
        ],
        compiler_params=pltpu.CompilerParams(vmem_limit_bytes=12 * MIB),
    )(owner.reshape(rows // LANES, LANES), cell.reshape(rows // LANES, LANES), values.reshape(rows, 1, LANES))


def vertical(weight, cells):
    high = cells.shape[0]
    whole = cells.astype(jnp.bfloat16).astype(jnp.float32)
    both = jnp.concatenate([whole, cells - whole], axis=0).astype(jnp.bfloat16)
    product = jnp.dot(weight, both, preferred_element_type=jnp.float32)
    return product[:high] + product[high:]


def start_kernel(geometry, got_ref, base_ref, weight_ref, out_ref, west_ref, east_ref, *scratch):
    tracers, rows, high, columns, devices = geometry
    banks, addr_v, addr_s, sem = scratch[:BANKS], scratch[BANKS], scratch[BANKS + 1], scratch[BANKS + 2]
    for o in range(devices):
        addr_v[o : o + 1, :] = got_ref[o * SLOTS + 32].astype(jnp.int32)
    copy = pltpu.make_async_copy(addr_v, addr_s, sem)
    copy.start()
    clear = 64
    for bank in banks:

        @pl.loop(0, bank.shape[0] // clear)
        def _(i):
            bank[pl.ds(pl.multiple_of(i * clear, clear), clear), :] = jnp.zeros((clear, LANES), jnp.float32)

    copy.wait()

    @pl.loop(0, devices // BANKS)
    def _(group):
        first = group * BANKS
        most = addr_s[first, 32]
        for b in range(1, BANKS):
            most = jnp.maximum(most, addr_s[first + b, 32])

        @pl.loop(0, (most + 3) // 4)
        def _(c):
            for u in range(4):
                for b, bank in enumerate(banks):
                    place = addr_s[first + b, c * 4 + u]
                    bank[pl.ds(place, 1), :] += got_ref[(first + b) * SLOTS + c * 4 + u]

    west_ref[...] = jnp.zeros_like(west_ref)
    east_ref[...] = jnp.zeros_like(east_ref)
    for j in range(rows):
        weight = weight_ref[j]
        for t in range(tracers):
            row = t * rows + j
            done = []
            for half in range(columns // 2):
                pieces = []
                for c in (2 * half, 2 * half + 1):
                    at = (row * columns + c) * high
                    piece = base_ref[at : at + high, :]
                    for bank in banks:
                        piece = piece + bank[at : at + high, :]
                    pieces.append(piece)
                level = vertical(weight, jnp.concatenate(pieces, axis=1))
                out_ref[t, j, :, half * 2 * LANES : (half + 1) * 2 * LANES] = level
                done.append(level)
            lane = lax.broadcasted_iota(jnp.int32, (high, LANES), 1)
            west_ref[...] = jnp.where(lane == row, pltpu.roll(done[0][:, :LANES], row, 1), west_ref[...])
            east_ref[...] = jnp.where(lane == row, pltpu.roll(done[-1][:, LANES:], row + 1, 1), east_ref[...])


def start(got, base, weight, tracers, rows, high, columns, devices):
    f32 = jnp.float32
    places = tracers * rows * columns * high
    vmem = pl.BlockSpec(memory_space=pltpu.VMEM)
    return pl.pallas_call(
        functools.partial(start_kernel, (tracers, rows, high, columns, devices)),
        out_shape=(
            jax.ShapeDtypeStruct((tracers, rows, high, columns * LANES), f32),
            jax.ShapeDtypeStruct((high, LANES), f32),
            jax.ShapeDtypeStruct((high, LANES), f32),
        ),
        in_specs=[vmem] * 3,
        out_specs=(vmem,) * 3,
        scratch_shapes=[pltpu.VMEM((places + 64, LANES), f32) for _ in range(BANKS)]
        + [
            pltpu.VMEM((devices, LANES), jnp.int32),
            pltpu.SMEM((devices, LANES), jnp.int32),
            pltpu.SemaphoreType.DMA,
        ],
        compiler_params=pltpu.CompilerParams(vmem_limit_bytes=32 * MIB),
    )(got, base, weight)


def transported(t, j, j_last, levels, field_ref, courant_ref, mask, north_ref, south_ref, hw_ref, he_ref, rows):
    wide = field_ref.shape[-1]
    row = t * rows + j
    for at in range(0, levels, 8):
        count = min(8, levels - at)
        strip = pl.ds(at, count)
        here = field_ref[t, j, strip, :]
        lane = lax.broadcasted_iota(jnp.int32, (count, wide), 1)
        east_end = jnp.tile(pltpu.roll(he_ref[strip, :], LANES - 1 - row, 1), (1, wide // LANES))
        west_end = jnp.tile(pltpu.roll(hw_ref[strip, :], (LANES - row) % LANES, 1), (1, wide // LANES))
        east = jnp.where(lane == wide - 1, east_end, pltpu.roll(here, wide - 1, 1))
        west = jnp.where(lane == 0, west_end, pltpu.roll(here, 1, 1))
        north = north_ref[t, strip, :] if j == rows - 1 else field_ref[t, j + 1, strip, :]
        south = south_ref[t, strip, :] if j == 0 else field_ref[t, j - 1, strip, :]
        moved = (
            here
            + courant_ref[0, 0, strip, :] * (east - here)
            + courant_ref[1, 0, strip, :] * (west - here)
            + courant_ref[2, 0, strip, :] * (north - here)
            + courant_ref[3, 0, strip, :] * (south - here)
        )
        yield at, count, mask * moved


def step_kernel(levels, field_ref, courant_ref, mask_ref, north_ref, south_ref, hw_ref, he_ref, weight_ref,
                out_ref, west_ref, east_ref, state):
    tracers, rows, high, wide = field_ref.shape
    step = pl.program_id(0)

    @pl.when(step == 0)
    def _():
        west_ref[...] = jnp.zeros_like(west_ref)
        east_ref[...] = jnp.zeros_like(east_ref)
        state[...] = jnp.zeros_like(state)

    for j in range(rows):

        @pl.when(step == j)
        def _():
            mask = mask_ref[j : j + 1, :].astype(jnp.float32)
            weight = weight_ref[0]
            lane = lax.broadcasted_iota(jnp.int32, (high, LANES), 1)
            for t in range(tracers):
                for at, count, value in transported(
                    t, j, rows - 1, levels, field_ref, courant_ref, mask, north_ref, south_ref, hw_ref, he_ref, rows
                ):
                    state[t, at : at + count, :] = value
                row = t * rows + j
                for half in range(wide // (2 * LANES)):
                    span = slice(half * 2 * LANES, (half + 1) * 2 * LANES)
                    level = vertical(weight, state[t, :, span])
                    out_ref[t, 0, :, span] = level
                    if half == 0:
                        west_ref[...] = jnp.where(
                            lane == row, pltpu.roll(level[:, :LANES], row, 1), west_ref[...]
                        )
                last = out_ref[t, 0, :, wide - LANES :]
                east_ref[...] = jnp.where(lane == row, pltpu.roll(last, row + 1, 1), east_ref[...])


def final_kernel(levels, field_ref, courant_ref, mask_ref, north_ref, south_ref, hw_ref, he_ref, out_ref, state, sems):
    tracers, rows, high, wide = field_ref.shape
    step = pl.program_id(0)
    for j in range(rows):

        @pl.when(step == j)
        def _():
            mask = mask_ref[j : j + 1, :].astype(jnp.float32)
            for t in range(tracers):
                slot = (j % 2) * tracers + t
                copy = pltpu.make_async_copy(state.at[slot], out_ref.at[t, :, j, :], sems.at[slot])
                if j >= 2:
                    pltpu.make_async_copy(state.at[slot], out_ref.at[t, :, j - 2, :], sems.at[slot]).wait()
                for at, count, value in transported(
                    t, j, rows - 1, levels, field_ref, courant_ref, mask, north_ref, south_ref, hw_ref, he_ref, rows
                ):
                    state[slot, at : at + count, :] = value
                copy.start()
            if j == rows - 1:
                for k in (rows - 2, rows - 1):
                    for t in range(tracers):
                        slot = (k % 2) * tracers + t
                        pltpu.make_async_copy(state.at[slot], out_ref.at[t, :, k, :], sems.at[slot]).wait()


def step_specs(tracers, rows, levels, high, wide):
    whole = lambda *shape: pl.BlockSpec(shape, lambda j: (0,) * len(shape))
    return [
        whole(tracers, rows, high, wide),
        pl.BlockSpec((4, 1, levels, wide), lambda j: (0, j, 0, 0)),
        whole(rows, wide),
        whole(tracers, high, wide),
        whole(tracers, high, wide),
        whole(high, LANES),
        whole(high, LANES),
    ]


def one_step(levels, field, courant, mask, north, south, hw, he, weight):
    f32 = jnp.float32
    tracers, rows, high, wide = field.shape
    ends = pl.BlockSpec((high, LANES), lambda j: (0, 0))
    return pl.pallas_call(
        functools.partial(step_kernel, levels),
        grid=(rows,),
        out_shape=(
            jax.ShapeDtypeStruct(field.shape, f32),
            jax.ShapeDtypeStruct((high, LANES), f32),
            jax.ShapeDtypeStruct((high, LANES), f32),
        ),
        in_specs=step_specs(tracers, rows, levels, high, wide)
        + [pl.BlockSpec((1, 2 * high, 2 * high), lambda j: (j, 0, 0))],
        out_specs=(pl.BlockSpec((tracers, 1, high, wide), lambda j: (0, j, 0, 0)), ends, ends),
        scratch_shapes=[pltpu.VMEM((tracers, high, wide), f32)],
        compiler_params=pltpu.CompilerParams(vmem_limit_bytes=32 * MIB),
    )(field, courant, mask, north, south, hw, he, weight)


def last_step(levels, field, courant, mask, north, south, hw, he):
    f32 = jnp.float32
    tracers, rows, high, wide = field.shape
    return pl.pallas_call(
        functools.partial(final_kernel, levels),
        grid=(rows,),
        out_shape=jax.ShapeDtypeStruct((tracers, levels, rows, wide), f32),
        in_specs=step_specs(tracers, rows, levels, high, wide),
        out_specs=pl.BlockSpec(memory_space=pl.ANY),
        scratch_shapes=[pltpu.VMEM((2 * tracers, levels, wide), f32), pltpu.SemaphoreType.DMA((2 * tracers,))],
        compiler_params=pltpu.CompilerParams(vmem_limit_bytes=32 * MIB),
    )(field, courant, mask, north, south, hw, he)


def weights(inverse, high):
    rows, levels, _ = inverse.shape
    turned = jnp.swapaxes(inverse, 1, 2)
    pad = ((0, 0), (0, high - levels), (0, high - levels))
    whole = jnp.pad(lax.reduce_precision(turned, 8, 7), pad)
    rest = jnp.pad(turned, pad) - whole
    return jnp.concatenate(
        [jnp.concatenate([whole, whole], 2), jnp.concatenate([rest, rest], 2)], 1
    ).astype(jnp.bfloat16)


def exchange(field, west, east):
    lat = lax.axis_size("lat")
    lon = lax.axis_size("lon")
    up = [(i, i + 1) for i in range(lat - 1)]
    down = [(i + 1, i) for i in range(lat - 1)]
    south = lax.ppermute(field[:, -1], "lat", up)
    north = lax.ppermute(field[:, 0], "lat", down)
    he = lax.ppermute(west, "lon", [((i + 1) % lon, i) for i in range(lon)])
    hw = lax.ppermute(east, "lon", [(i, (i + 1) % lon) for i in range(lon)])
    return north, south, hw, he


def local(terminal, courant, inverse, land_mask, obs_values, obs_owner, obs_cell):
    devices = lax.axis_size("lat") * lax.axis_size("lon")
    tracers, rows, levels, wide = terminal.shape
    high = padded_levels(levels)
    columns = wide // LANES
    send = pack(obs_owner, obs_cell, obs_values, levels, high, columns, devices)
    got = lax.all_to_all(send, ("lat", "lon"), split_axis=0, concat_axis=0, tiled=True)
    base = terminal.reshape(tracers * rows, levels, columns, LANES)
    base = jnp.pad(jnp.swapaxes(base, 1, 2), ((0, 0), (0, 0), (0, high - levels), (0, 0)))
    base = base.reshape(tracers * rows * columns * high, LANES)
    weight = weights(inverse, high)
    field, west, east = start(got, base, weight, tracers, rows, high, columns, devices)
    for _ in range(STEPS - 1):
        field, west, east = one_step(levels, field, courant, land_mask, *exchange(field, west, east), weight)
    out = last_step(levels, field, courant, land_mask, *exchange(field, west, east))
    return jnp.swapaxes(out, 1, 2)


def solution(mesh):
    placed = (
        P(None, "lat", None, "lon"),
        P(None, "lat", None, "lon"),
        P("lat", None, None),
        P("lat", "lon"),
        P(("lat", "lon"), None),
        P(("lat", "lon"), None),
        P(("lat", "lon")),
    )
    return jax.shard_map(
        local, mesh=mesh, in_specs=placed, out_specs=P(None, "lat", None, "lon"), check_vma=False
    )
```

```python
import functools

import jax
import jax.numpy as jnp
from jax import lax
from jax.experimental import pallas as pl
from jax.experimental.pallas import tpu as pltpu
from jax.sharding import PartitionSpec as P

STEPS = 2
LANES = 128
SLOTS = 33
BANKS = 4
MIB = 1 << 20


def padded_levels(levels):
    return -(-levels // 8) * 8


VMEM = pl.BlockSpec(memory_space=pltpu.VMEM)
SMEM = pl.BlockSpec(memory_space=pltpu.SMEM)
HBM = pl.BlockSpec(memory_space=pltpu.HBM)


def pack_kernel(geometry, owner_hbm, cell_hbm, values_hbm, send_ref, slot_ref, owner_ref, cell_ref, values_ref, slots, pay, sems):
    levels, high, columns, devices = geometry
    per_row = levels * columns
    chunks = owner_ref.shape[0]
    f32, bf16 = jnp.float32, jnp.bfloat16
    get_owner = pltpu.make_async_copy(owner_hbm, owner_ref, sems.at[0])
    get_cell = pltpu.make_async_copy(cell_hbm, cell_ref, sems.at[1])
    get_values = pltpu.make_async_copy(values_hbm, values_ref, sems.at[2])
    get_owner.start()
    get_cell.start()
    get_values.start()
    sub = lax.broadcasted_iota(jnp.int32, (LANES, LANES), 0)
    lane = lax.broadcasted_iota(jnp.int32, (LANES, LANES), 1)
    before = jnp.concatenate(
        [jnp.where(sub < lane, 1.0, 0.0), jnp.ones((LANES, LANES), f32)], axis=1
    ).astype(bf16)
    get_owner.wait()
    get_cell.wait()
    cells = cell_ref[...]
    tile_row = ((cells >> 4) * 5243) >> 17
    rest = cells - tile_row * per_row
    level = rest >> 2
    column = rest & 3
    place = (tile_row * columns + column) * high + level
    upper, lower = (place >> 6).astype(f32), (place & 63).astype(f32)
    carry = jnp.zeros((LANES, LANES), f32)
    total = jnp.zeros((LANES, LANES), f32)
    for i in range(chunks):
        own = owner_ref[i : i + 1, :]
        hot = jnp.where(sub == own, 1.0, 0.0)
        hot16 = hot.astype(bf16)
        counted = jnp.dot(hot16, before, preferred_element_type=f32)
        rank = jnp.sum(hot * (counted[:, :LANES] + carry), axis=0, keepdims=True)
        carry = carry + counted[:, LANES:]
        rank_i = rank.astype(jnp.int32)
        slots[i : i + 1, :] = own * SLOTS + rank_i
        near_sub = sub[:64]
        parts = jnp.where(
            near_sub == rank_i,
            jnp.broadcast_to(upper[i : i + 1, :], (64, LANES)),
            jnp.where(near_sub == rank_i + 32, jnp.broadcast_to(lower[i : i + 1, :], (64, LANES)), 0.0),
        )
        parts = jnp.concatenate([parts, jnp.zeros_like(parts)], axis=0).astype(bf16)
        total = total + lax.dot_general(
            hot16, parts, (((1,), (1,)), ((), ())), preferred_element_type=f32
        )
    copy = pltpu.make_async_copy(slots, slot_ref, sems.at[3])
    copy.start()
    places = total * 64.0 + pltpu.roll(total, LANES - 32, 1)
    dump = f32(2 * 8 * columns * high)
    pay[...] = jnp.where(
        lane < 32, jnp.where(lane.astype(f32) < carry, places, dump), carry
    )
    for o in range(devices):
        send_ref[o * SLOTS + 32] = pay[o : o + 1, :]
    get_values.wait()
    copy.wait()
    unroll = 32
    for i in range(chunks):

        @pl.loop(0, LANES // unroll)
        def _(c):
            base = c * unroll
            for u in range(unroll):
                send_ref[slot_ref[i, base + u]] = values_ref[i * LANES + base + u]


def pack(owner, cell, values, levels, high, columns, devices):
    rows = values.shape[0]
    chunks = rows // LANES
    return pl.pallas_call(
        functools.partial(pack_kernel, (levels, high, columns, devices)),
        out_shape=jax.ShapeDtypeStruct((devices * SLOTS, 1, LANES), jnp.float32),
        in_specs=[HBM] * 3,
        out_specs=VMEM,
        scratch_shapes=[
            pltpu.SMEM((chunks, LANES), jnp.int32),
            pltpu.VMEM((chunks, LANES), jnp.int32),
            pltpu.VMEM((chunks, LANES), jnp.int32),
            pltpu.VMEM((rows, 1, LANES), jnp.float32),
            pltpu.VMEM((chunks, LANES), jnp.int32),
            pltpu.VMEM((LANES, LANES), jnp.float32),
            pltpu.SemaphoreType.DMA((4,)),
        ],
        compiler_params=pltpu.CompilerParams(vmem_limit_bytes=12 * MIB),
    )(owner.reshape(chunks, LANES), cell.reshape(chunks, LANES), values.reshape(rows, 1, LANES))


def vertical(weight, cells):
    high = cells.shape[0]
    whole = cells.astype(jnp.bfloat16).astype(jnp.float32)
    both = jnp.concatenate([whole, cells - whole], axis=0).astype(jnp.bfloat16)
    product = jnp.dot(weight, both, preferred_element_type=jnp.float32)
    return product[:high] + product[high:]


def keep_ends(row, first, last, west, east):
    lane = lax.broadcasted_iota(jnp.int32, first.shape, 1)
    west[...] = jnp.where(lane == row, pltpu.roll(first, row, 1), west[...])
    east[...] = jnp.where(lane == row, pltpu.roll(last, (row + 1) % LANES, 1), east[...])


def hand_out(odd_ref, field, west, east, near_ref, far_ref, pair_ref, other_ref):
    last = field.shape[1] - 1
    for axis, (low, top, mine, others) in enumerate((
        (field.at[:, 0], field.at[:, last], near_ref, far_ref),
        (west, east, pair_ref, other_ref),
    )):
        odd = odd_ref[axis]

        @pl.when(odd == 0)
        def _():
            mine[...] = top[...]
            others[...] = low[...]

        @pl.when(odd != 0)
        def _():
            mine[...] = low[...]
            others[...] = top[...]


def start_kernel(geometry, odd_ref, got_ref, base_hbm, weight_hbm, courant_ref,
                 out_ref, near_ref, far_ref, pair_ref, other_ref, *scratch):
    tracers, rows, high, columns, devices = geometry
    banks, addr_v, addr_s, base_ref, weight_ref, west, east, sems = scratch[:BANKS], *scratch[BANKS:]
    get_base = pltpu.make_async_copy(base_hbm, base_ref, sems.at[1])
    get_weight = pltpu.make_async_copy(weight_hbm, weight_ref, sems.at[2])
    get_base.start()
    get_weight.start()
    for o in range(devices):
        addr_v[o : o + 1, :] = got_ref[o * SLOTS + 32].astype(jnp.int32)
    copy = pltpu.make_async_copy(addr_v, addr_s, sems.at[0])
    copy.start()
    clear = 64
    for bank in banks:

        @pl.loop(0, bank.shape[0] // clear)
        def _(i):
            bank[pl.ds(pl.multiple_of(i * clear, clear), clear), :] = jnp.zeros((clear, LANES), jnp.float32)

    west[...] = jnp.zeros_like(west)
    east[...] = jnp.zeros_like(east)
    copy.wait()

    @pl.loop(0, devices // BANKS)
    def _(group):
        first = group * BANKS
        most = addr_s[first, 32]
        for b in range(1, BANKS):
            most = jnp.maximum(most, addr_s[first + b, 32])

        @pl.loop(0, (most + 3) // 4)
        def _(c):
            for u in range(4):
                for b, bank in enumerate(banks):
                    place = addr_s[first + b, c * 4 + u]
                    bank[pl.ds(place, 1), :] += got_ref[(first + b) * SLOTS + c * 4 + u]

    get_base.wait()
    get_weight.wait()
    for j in range(rows):
        weight = weight_ref[j]
        for t in range(tracers):
            row = t * rows + j
            done = []
            for half in range(columns // 2):
                pieces = []
                for c in (2 * half, 2 * half + 1):
                    at = (row * columns + c) * high
                    piece = base_ref[at : at + high, :]
                    for bank in banks:
                        piece = piece + bank[at : at + high, :]
                    pieces.append(piece)
                level = vertical(weight, jnp.concatenate(pieces, axis=1))
                out_ref[t, j, :, half * 2 * LANES : (half + 1) * 2 * LANES] = level
                done.append(level)
            keep_ends(row, done[0][:, :LANES], done[-1][:, LANES:], west, east)
    hand_out(odd_ref, out_ref, west, east, near_ref, far_ref, pair_ref, other_ref)


def shapes_of(tracers, rows, high, wide):
    f32 = jnp.float32
    edge = jax.ShapeDtypeStruct((tracers, high, wide), f32)
    end = jax.ShapeDtypeStruct((high, LANES), f32)
    return jax.ShapeDtypeStruct((tracers, rows, high, wide), f32), edge, edge, end, end


def start(odd, got, base, weight, courant, tracers, rows, high, columns, devices):
    f32 = jnp.float32
    places = tracers * rows * columns * high
    return pl.pallas_call(
        functools.partial(start_kernel, (tracers, rows, high, columns, devices)),
        out_shape=shapes_of(tracers, rows, high, columns * LANES),
        in_specs=[SMEM, VMEM, HBM, HBM, VMEM],
        out_specs=(VMEM,) * 5,
        scratch_shapes=[pltpu.VMEM((places + 64, LANES), f32) for _ in range(BANKS)]
        + [
            pltpu.VMEM((devices, LANES), jnp.int32),
            pltpu.SMEM((devices, LANES), jnp.int32),
            pltpu.VMEM(base.shape, f32),
            pltpu.VMEM(weight.shape, weight.dtype),
            pltpu.VMEM((high, LANES), f32),
            pltpu.VMEM((high, LANES), f32),
            pltpu.SemaphoreType.DMA((3,)),
        ],
        compiler_params=pltpu.CompilerParams(vmem_limit_bytes=40 * MIB),
    )(odd, got, base, weight, courant)


def ends_in_place(odd_ref, pair_ref, other_ref, west, east):
    odd = odd_ref[1] != 0
    pair, other = pair_ref[...], other_ref[...]
    west[...] = jnp.where(odd, pair, other)
    east[...] = jnp.where(odd, other, pair)


def transported(t, j, levels, field, courant_ref, mask, lat, west, east, store):
    rows, wide = field.shape[1], field.shape[3]
    row = t * rows + j
    tiles = [slice(c * LANES, (c + 1) * LANES) for c in range(wide // LANES)]
    for at in range(0, levels, 8):
        count = min(8, levels - at)
        strip = slice(at, at + count)
        lane = lax.broadcasted_iota(jnp.int32, (count, LANES), 1)
        here = [field[t, j, strip, tile] for tile in tiles]
        left = [pltpu.roll(x, LANES - 1, 1) for x in here]
        left.append(pltpu.roll(east[strip, :], LANES - 1 - row, 1))
        right = [pltpu.roll(west[strip, :], (LANES - row) % LANES, 1)]
        right += [pltpu.roll(x, 1, 1) for x in here]
        for c, tile in enumerate(tiles):
            v = here[c]
            e = jnp.where(lane == LANES - 1, left[c + 1], left[c])
            w = jnp.where(lane == 0, right[c], right[c + 1])
            n = lat[0](t, strip, tile) if j == rows - 1 else field[t, j + 1, strip, tile]
            s = lat[1](t, strip, tile) if j == 0 else field[t, j - 1, strip, tile]
            moved = (
                v
                + courant_ref[0, j, strip, tile] * (e - v)
                + courant_ref[1, j, strip, tile] * (w - v)
                + courant_ref[2, j, strip, tile] * (n - v)
                + courant_ref[3, j, strip, tile] * (s - v)
            )
            store(strip, tile, mask[c] * moved)


def mask_row(mask_ref, j):
    wide = mask_ref.shape[1]
    return [mask_ref[j : j + 1, c : c + LANES].astype(jnp.float32) for c in range(0, wide, LANES)]


def by_side(odd_ref, near_ref, far_ref):
    odd = odd_ref[0] != 0
    north = lambda t, strip, tile: jnp.where(odd, far_ref[t, strip, tile], near_ref[t, strip, tile])
    south = lambda t, strip, tile: jnp.where(odd, near_ref[t, strip, tile], far_ref[t, strip, tile])
    return north, south


def advance(rows_done, levels, lat, field, courant_ref, mask_ref, hw, he, weight_ref, out_ref, west, east, state):
    tracers, rows, high, wide = field.shape
    for slot in range(state.shape[0]):
        state[slot, levels:high, :] = jnp.zeros((high - levels, wide), jnp.float32)
    for j in rows_done:
        mask = mask_row(mask_ref, j)
        weight = weight_ref[j]
        for t in range(tracers):
            slot = (j * tracers + t) % state.shape[0]

            def store(strip, tile, value):
                state[slot, strip, tile] = value

            transported(t, j, levels, field, courant_ref, mask, lat, hw, he, store)
            done = []
            for at in range(0, wide, 2 * LANES):
                level = vertical(weight, state[slot, :, at : at + 2 * LANES])
                out_ref[t, j, :, at : at + 2 * LANES] = level
                done.append(level)
            keep_ends(t * rows + j, done[0][:, :LANES], done[-1][:, LANES:], west, east)


def inner_kernel(levels, odd_ref, pair_ref, other_ref, field, courant_ref, mask_ref, weight_ref,
                 out_ref, west, east, hw, he, state):
    ends_in_place(odd_ref, pair_ref, other_ref, hw, he)
    west[...] = jnp.zeros_like(west)
    east[...] = jnp.zeros_like(east)
    rows = field.shape[1]
    advance(range(1, rows - 1), levels, None, field, courant_ref, mask_ref, hw, he, weight_ref, out_ref, west, east, state)


def edge_kernel(levels, odd_ref, pair_ref, other_ref, field, courant_ref, mask_ref, weight_ref, near_in, far_in,
                part_ref, west_in, east_in, out_ref, near_ref, far_ref, pair_out, other_out, hw, he, west, east, state):
    ends_in_place(odd_ref, pair_ref, other_ref, hw, he)
    west[...] = west_in[...]
    east[...] = east_in[...]
    rows = field.shape[1]
    lat = by_side(odd_ref, near_in, far_in)
    advance((0, rows - 1), levels, lat, field, courant_ref, mask_ref, hw, he, weight_ref, out_ref, west, east, state)
    hand_out(odd_ref, out_ref, west, east, near_ref, far_ref, pair_out, other_out)


def step(levels, odd, field, courant, mask, weight, halos):
    f32 = jnp.float32
    near, far, pair, other = halos
    tracers, rows, high, wide = field.shape
    field_shape, edge, _, end, _ = shapes_of(tracers, rows, high, wide)
    ends = [pltpu.VMEM((high, LANES), f32)] * 2
    state = [pltpu.VMEM((2, high, wide), f32)]
    params = pltpu.CompilerParams(vmem_limit_bytes=20 * MIB)
    cost = lambda n: pl.CostEstimate(flops=n * 500_000_000, bytes_accessed=n * 1_000_000, transcendentals=0)
    part, west, east = pl.pallas_call(
        functools.partial(inner_kernel, levels),
        out_shape=(field_shape, end, end),
        in_specs=[SMEM] + [VMEM] * 6,
        out_specs=(VMEM,) * 3,
        scratch_shapes=ends + state,
        compiler_params=params,
        cost_estimate=cost(rows - 2),
    )(odd, pair, other, field, courant, mask, weight)
    return pl.pallas_call(
        functools.partial(edge_kernel, levels),
        out_shape=(field_shape, edge, edge, end, end),
        in_specs=[SMEM] + [VMEM] * 11,
        out_specs=(VMEM,) * 5,
        scratch_shapes=ends + ends + state,
        input_output_aliases={9: 0},
        compiler_params=params,
        cost_estimate=cost(2),
    )(odd, pair, other, field, courant, mask, weight, near, far, part, west, east)


def finish(rows_done, levels, lat, field, courant_ref, mask_ref, hw, he, out_ref, state, sems):
    tracers = field.shape[0]
    slots = state.shape[0]
    flying = {}
    for k, (j, t) in enumerate((j, t) for j in rows_done for t in range(tracers)):
        slot = k % slots
        if slot in flying:
            flying.pop(slot).wait()

        def store(strip, tile, value):
            state[slot, strip, tile] = value

        transported(t, j, levels, field, courant_ref, mask_row(mask_ref, j), lat, hw, he, store)
        copy = pltpu.make_async_copy(state.at[slot], out_ref.at[t, :, j, :], sems.at[slot])
        copy.start()
        flying[slot] = copy
    for copy in flying.values():
        copy.wait()


def final_inner_kernel(levels, odd_ref, pair_ref, other_ref, field, courant_ref, mask_ref, out_ref, hw, he, state, sems):
    ends_in_place(odd_ref, pair_ref, other_ref, hw, he)
    rows = field.shape[1]
    finish(range(1, rows - 1), levels, None, field, courant_ref, mask_ref, hw, he, out_ref, state, sems)


def final_edge_kernel(levels, odd_ref, pair_ref, other_ref, field, courant_ref, mask_ref, near_in, far_in, part_ref,
                      out_ref, hw, he, state, sems):
    ends_in_place(odd_ref, pair_ref, other_ref, hw, he)
    rows = field.shape[1]
    lat = by_side(odd_ref, near_in, far_in)
    finish((0, rows - 1), levels, lat, field, courant_ref, mask_ref, hw, he, out_ref, state, sems)


def last_step(levels, odd, field, courant, mask, halos):
    f32 = jnp.float32
    near, far, pair, other = halos
    tracers, rows, high, wide = field.shape
    slots = 4
    scratch = [pltpu.VMEM((high, LANES), f32)] * 2 + [
        pltpu.VMEM((slots, levels, wide), f32),
        pltpu.SemaphoreType.DMA((slots,)),
    ]
    shape = jax.ShapeDtypeStruct((tracers, levels, rows, wide), f32)
    params = pltpu.CompilerParams(vmem_limit_bytes=20 * MIB)
    cost = lambda n: pl.CostEstimate(flops=n * 500_000_000, bytes_accessed=n * 1_000_000, transcendentals=0)
    part = pl.pallas_call(
        functools.partial(final_inner_kernel, levels),
        out_shape=shape,
        in_specs=[SMEM] + [VMEM] * 5,
        out_specs=HBM,
        scratch_shapes=scratch,
        compiler_params=params,
        cost_estimate=cost(rows - 2),
    )(odd, pair, other, field, courant, mask)
    return pl.pallas_call(
        functools.partial(final_edge_kernel, levels),
        out_shape=shape,
        in_specs=[SMEM] + [VMEM] * 7 + [HBM],
        out_specs=HBM,
        scratch_shapes=scratch,
        input_output_aliases={8: 0},
        compiler_params=params,
        cost_estimate=cost(2),
    )(odd, pair, other, field, courant, mask, near, far, part)


def weights(inverse, high):
    rows, levels, _ = inverse.shape
    turned = jnp.swapaxes(inverse, 1, 2)
    pad = ((0, 0), (0, high - levels), (0, high - levels))
    whole = jnp.pad(lax.reduce_precision(turned, 8, 7), pad)
    rest = jnp.pad(turned, pad) - whole
    return jnp.concatenate(
        [jnp.concatenate([whole, whole], 2), jnp.concatenate([rest, rest], 2)], 1
    ).astype(jnp.bfloat16)


def exchange(near, far, pair, other):
    lat = lax.axis_size("lat")
    lon = lax.axis_size("lon")
    next_pair = [(i, i + 1 if i % 2 else i - 1) for i in range(1, lat - 1)]
    other = lax.ppermute(other, "lon", [(i, (i + 1 if i % 2 else i - 1) % lon) for i in range(lon)])
    pair = lax.ppermute(pair, "lon", [(i, i ^ 1) for i in range(lon)])
    far = lax.ppermute(far, "lat", next_pair)
    near = lax.ppermute(near, "lat", [(i, i ^ 1) for i in range(lat)])
    return near, far, pair, other


def local(terminal, courant, inverse, land_mask, obs_values, obs_owner, obs_cell):
    devices = lax.axis_size("lat") * lax.axis_size("lon")
    tracers, rows, levels, wide = terminal.shape
    high = padded_levels(levels)
    columns = wide // LANES
    odd = jnp.stack([lax.axis_index("lat") % 2, lax.axis_index("lon") % 2]).astype(jnp.int32)
    send = pack(obs_owner, obs_cell, obs_values, levels, high, columns, devices)
    got = lax.all_to_all(send, ("lat", "lon"), split_axis=0, concat_axis=0, tiled=True)
    base = terminal.reshape(tracers * rows, levels, columns, LANES)
    base = jnp.pad(jnp.swapaxes(base, 1, 2), ((0, 0), (0, 0), (0, high - levels), (0, 0)))
    base = base.reshape(tracers * rows * columns * high, LANES)
    weight = weights(inverse, high)
    field, *edges = start(odd, got, base, weight, courant, tracers, rows, high, columns, devices)
    for _ in range(STEPS - 1):
        field, *edges = step(levels, odd, field, courant, land_mask, weight, exchange(*edges))
    out = last_step(levels, odd, field, courant, land_mask, exchange(*edges))
    return jnp.swapaxes(out, 1, 2)


def solution(mesh):
    placed = (
        P(None, "lat", None, "lon"),
        P(None, "lat", None, "lon"),
        P("lat", None, None),
        P("lat", "lon"),
        P(("lat", "lon"), None),
        P(("lat", "lon"), None),
        P(("lat", "lon")),
    )
    return jax.shard_map(
        local, mesh=mesh, in_specs=placed, out_specs=P(None, "lat", None, "lon"), check_vma=False
    )
```

```python
import functools

import jax
import jax.numpy as jnp
from jax import lax
from jax.experimental import pallas as pl
from jax.experimental.pallas import tpu as pltpu
from jax.sharding import PartitionSpec as P

STEPS = 2
LANES = 128
SLOTS = 33
BANKS = 4
MIB = 1 << 20


def padded_levels(levels):
    return -(-levels // 8) * 8


VMEM = pl.BlockSpec(memory_space=pltpu.VMEM)
SMEM = pl.BlockSpec(memory_space=pltpu.SMEM)
HBM = pl.BlockSpec(memory_space=pltpu.HBM)


def pack_kernel(geometry, owner_hbm, cell_hbm, values_hbm, send_ref, slot_ref, owner_ref, cell_ref, values_ref, slots, pay, sems):
    levels, high, columns, devices = geometry
    per_row = levels * columns
    chunks = owner_ref.shape[0]
    f32, bf16 = jnp.float32, jnp.bfloat16
    get_owner = pltpu.make_async_copy(owner_hbm, owner_ref, sems.at[0])
    get_cell = pltpu.make_async_copy(cell_hbm, cell_ref, sems.at[1])
    get_values = pltpu.make_async_copy(values_hbm, values_ref, sems.at[2])
    get_owner.start()
    get_cell.start()
    get_values.start()
    sub = lax.broadcasted_iota(jnp.int32, (LANES, LANES), 0)
    lane = lax.broadcasted_iota(jnp.int32, (LANES, LANES), 1)
    before = jnp.concatenate(
        [jnp.where(sub < lane, 1.0, 0.0), jnp.ones((LANES, LANES), f32)], axis=1
    ).astype(bf16)
    get_owner.wait()
    get_cell.wait()
    cells = cell_ref[...]
    tile_row = ((cells >> 4) * 5243) >> 17
    rest = cells - tile_row * per_row
    level = rest >> 2
    column = rest & 3
    place = (tile_row * columns + column) * high + level
    upper, lower = (place >> 6).astype(f32), (place & 63).astype(f32)
    carry = jnp.zeros((LANES, LANES), f32)
    total = jnp.zeros((LANES, LANES), f32)
    for i in range(chunks):
        own = owner_ref[i : i + 1, :]
        hot = jnp.where(sub == own, 1.0, 0.0)
        hot16 = hot.astype(bf16)
        counted = jnp.dot(hot16, before, preferred_element_type=f32)
        rank = jnp.sum(hot * (counted[:, :LANES] + carry), axis=0, keepdims=True)
        carry = carry + counted[:, LANES:]
        rank_i = rank.astype(jnp.int32)
        slots[i : i + 1, :] = own * SLOTS + rank_i
        near_sub = sub[:64]
        parts = jnp.where(
            near_sub == rank_i,
            jnp.broadcast_to(upper[i : i + 1, :], (64, LANES)),
            jnp.where(near_sub == rank_i + 32, jnp.broadcast_to(lower[i : i + 1, :], (64, LANES)), 0.0),
        )
        parts = jnp.concatenate([parts, jnp.zeros_like(parts)], axis=0).astype(bf16)
        total = total + lax.dot_general(
            hot16, parts, (((1,), (1,)), ((), ())), preferred_element_type=f32
        )
    copy = pltpu.make_async_copy(slots, slot_ref, sems.at[3])
    copy.start()
    places = total * 64.0 + pltpu.roll(total, LANES - 32, 1)
    dump = f32(2 * 8 * columns * high)
    pay[...] = jnp.where(
        lane < 32, jnp.where(lane.astype(f32) < carry, places, dump), carry
    )
    for o in range(devices):
        send_ref[o * SLOTS + 32] = pay[o : o + 1, :]
    get_values.wait()
    copy.wait()
    unroll = 64
    for i in range(chunks):

        @pl.loop(0, LANES // unroll)
        def _(c):
            base = c * unroll
            for u in range(unroll):
                send_ref[slot_ref[i, base + u]] = values_ref[i * LANES + base + u]


def pack(owner, cell, values, levels, high, columns, devices):
    rows = values.shape[0]
    chunks = rows // LANES
    return pl.pallas_call(
        functools.partial(pack_kernel, (levels, high, columns, devices)),
        out_shape=jax.ShapeDtypeStruct((devices * SLOTS, 1, LANES), jnp.float32),
        in_specs=[HBM] * 3,
        out_specs=VMEM,
        scratch_shapes=[
            pltpu.SMEM((chunks, LANES), jnp.int32),
            pltpu.VMEM((chunks, LANES), jnp.int32),
            pltpu.VMEM((chunks, LANES), jnp.int32),
            pltpu.VMEM((rows, 1, LANES), jnp.float32),
            pltpu.VMEM((chunks, LANES), jnp.int32),
            pltpu.VMEM((LANES, LANES), jnp.float32),
            pltpu.SemaphoreType.DMA((4,)),
        ],
        compiler_params=pltpu.CompilerParams(vmem_limit_bytes=60 * MIB),
    )(owner.reshape(chunks, LANES), cell.reshape(chunks, LANES), values.reshape(rows, 1, LANES))


def vertical(weight, cells):
    high = cells.shape[0]
    whole = cells.astype(jnp.bfloat16).astype(jnp.float32)
    both = jnp.concatenate([whole, cells - whole], axis=0).astype(jnp.bfloat16)
    product = jnp.dot(weight, both, preferred_element_type=jnp.float32)
    return product[:high] + product[high:]


def collect_ends(rows_done, field, before):
    tracers, rows, high, wide = field.shape
    lane = lax.broadcasted_iota(jnp.int32, (8, LANES), 1)
    for at in range(0, high, 8):
        strip = slice(at, at + 8)
        west, east = before(strip)
        for t in range(tracers):
            for j in rows_done:
                row = t * rows + j
                first = pltpu.roll(field[t, j, strip, :LANES], row, 1)
                last = pltpu.roll(field[t, j, strip, wide - LANES :], (row + 1) % LANES, 1)
                west = jnp.where(lane == row, first, west)
                east = jnp.where(lane == row, last, east)
        yield strip, west, east


def no_ends(strip):
    return jnp.zeros((8, LANES), jnp.float32), jnp.zeros((8, LANES), jnp.float32)


def hand_out(odd_ref, field, rows_done, before, near_ref, far_ref, pair_ref, other_ref):
    odd_lon = odd_ref[1] != 0
    for strip, west, east in collect_ends(rows_done, field, before):
        pair_ref[strip, :] = jnp.where(odd_lon, west, east)
        other_ref[strip, :] = jnp.where(odd_lon, east, west)
    last = field.shape[1] - 1
    odd = odd_ref[0]

    @pl.when(odd == 0)
    def _():
        near_ref[...] = field[:, last]
        far_ref[...] = field[:, 0]

    @pl.when(odd != 0)
    def _():
        near_ref[...] = field[:, 0]
        far_ref[...] = field[:, last]


def prepare_kernel(terminal_in, courant_in, terminal_out, courant_out, sems):
    copies = []
    for source, target in ((terminal_in, terminal_out), (courant_in, courant_out)):
        parts, rows = target.shape[:2]
        for part in range(parts):
            for j in range(rows):
                copies.append(
                    pltpu.make_async_copy(source.at[part, :, j, :], target.at[part, j], sems.at[len(copies)])
                )
                copies[-1].start()
    for copy in copies:
        copy.wait()


def prepare(terminal, courant):
    rows = terminal.shape[1]
    return pl.pallas_call(
        prepare_kernel,
        out_shape=tuple(jax.ShapeDtypeStruct(x.shape, x.dtype) for x in (terminal, courant)),
        in_specs=[HBM] * 2,
        out_specs=(HBM,) * 2,
        scratch_shapes=[pltpu.SemaphoreType.DMA(((terminal.shape[0] + courant.shape[0]) * rows,))],
        compiler_params=pltpu.CompilerParams(vmem_limit_bytes=60 * MIB),
    )(jnp.swapaxes(terminal, 1, 2), jnp.swapaxes(courant, 1, 2))


def start_kernel(devices, odd_ref, got_ref, weight_hbm, terminal_hbm, out_ref, near_ref, far_ref, pair_ref, other_ref,
                 terminal_ref, weight_ref, addr_v, addr_s, state, sems, *banks):
    tracers, rows, levels, wide = terminal_ref.shape
    columns = wide // LANES
    get_terminal = pltpu.make_async_copy(terminal_hbm, terminal_ref, sems.at[1])
    get_weight = pltpu.make_async_copy(weight_hbm, weight_ref, sems.at[2])
    get_terminal.start()
    get_weight.start()
    high = state.shape[1]
    whole = levels // 8 * 8
    for o in range(devices):
        addr_v[o : o + 1, :] = got_ref[o * SLOTS + 32].astype(jnp.int32)
    copy = pltpu.make_async_copy(addr_v, addr_s, sems.at[0])
    copy.start()
    clear = 64
    for bank in banks:

        @pl.loop(0, bank.shape[0] // clear)
        def _(i):
            bank[pl.ds(pl.multiple_of(i * clear, clear), clear), :] = jnp.zeros((clear, LANES), jnp.float32)

    copy.wait()

    @pl.loop(0, devices // BANKS)
    def _(group):
        first = group * BANKS
        most = addr_s[first, 32]
        for b in range(1, BANKS):
            most = jnp.maximum(most, addr_s[first + b, 32])

        @pl.loop(0, (most + 3) // 4)
        def _(c):
            for u in range(4):
                for b, bank in enumerate(banks):
                    place = addr_s[first + b, c * 4 + u]
                    bank[pl.ds(place, 1), :] += got_ref[(first + b) * SLOTS + c * 4 + u]

    for slot in range(state.shape[0]):
        state[slot, levels:high, :] = jnp.zeros((high - levels, wide), jnp.float32)
    get_terminal.wait()
    get_weight.wait()
    for j in range(rows):
        weight = weight_ref[j]
        for t in range(tracers):
            slot = (j * tracers + t) % state.shape[0]
            for c in range(columns):
                tile = slice(c * LANES, (c + 1) * LANES)
                base = ((t * rows + j) * columns + c) * high
                for low, top in ((0, whole), (whole, levels)):
                    total = terminal_ref[t, j, low:top, tile]
                    for bank in banks:
                        total = total + bank[base + low : base + top, :]
                    state[slot, low:top, tile] = total
            for at in range(0, wide, 2 * LANES):
                out_ref[t, j, :, at : at + 2 * LANES] = vertical(weight, state[slot, :, at : at + 2 * LANES])
    hand_out(odd_ref, out_ref, range(rows), no_ends, near_ref, far_ref, pair_ref, other_ref)


def shapes_of(tracers, rows, high, wide):
    f32 = jnp.float32
    edge = jax.ShapeDtypeStruct((tracers, high, wide), f32)
    end = jax.ShapeDtypeStruct((high, LANES), f32)
    return jax.ShapeDtypeStruct((tracers, rows, high, wide), f32), edge, edge, end, end


def start(odd, got, weight, terminal, high, devices):
    f32 = jnp.float32
    tracers, rows, levels, wide = terminal.shape
    places = tracers * rows * (wide // LANES) * high
    return pl.pallas_call(
        functools.partial(start_kernel, devices),
        out_shape=shapes_of(tracers, rows, high, wide),
        in_specs=[SMEM, VMEM, HBM, HBM],
        out_specs=(VMEM,) * 5,
        scratch_shapes=[
            pltpu.VMEM(terminal.shape, f32),
            pltpu.VMEM(weight.shape, weight.dtype),
            pltpu.VMEM((devices, LANES), jnp.int32),
            pltpu.SMEM((devices, LANES), jnp.int32),
            pltpu.VMEM((2, high, wide), f32),
            pltpu.SemaphoreType.DMA((3,)),
        ]
        + [pltpu.VMEM((places + 64, LANES), f32) for _ in range(BANKS)],
        compiler_params=pltpu.CompilerParams(vmem_limit_bytes=32 * MIB),
    )(odd, got, weight, terminal)


def ends_in_place(odd_ref, pair_ref, other_ref, west, east):
    odd = odd_ref[1] != 0
    pair, other = pair_ref[...], other_ref[...]
    west[...] = jnp.where(odd, pair, other)
    east[...] = jnp.where(odd, other, pair)


def transported(t, j, levels, field, courant_ref, mask, lat, west, east, store):
    rows, wide = field.shape[1], field.shape[3]
    row = t * rows + j
    tiles = [slice(c * LANES, (c + 1) * LANES) for c in range(wide // LANES)]
    for at in range(0, levels, 8):
        count = min(8, levels - at)
        strip = slice(at, at + count)
        lane = lax.broadcasted_iota(jnp.int32, (count, LANES), 1)
        here = [field[t, j, strip, tile] for tile in tiles]
        left = [pltpu.roll(x, LANES - 1, 1) for x in here]
        left.append(pltpu.roll(east[strip, :], LANES - 1 - row, 1))
        right = [pltpu.roll(west[strip, :], (LANES - row) % LANES, 1)]
        right += [pltpu.roll(x, 1, 1) for x in here]
        for c, tile in enumerate(tiles):
            v = here[c]
            e = jnp.where(lane == LANES - 1, left[c + 1], left[c])
            w = jnp.where(lane == 0, right[c], right[c + 1])
            n = lat[0](t, strip, tile) if j == rows - 1 else field[t, j + 1, strip, tile]
            s = lat[1](t, strip, tile) if j == 0 else field[t, j - 1, strip, tile]
            moved = (
                v
                + courant_ref[0, j, strip, tile] * (e - v)
                + courant_ref[1, j, strip, tile] * (w - v)
                + courant_ref[2, j, strip, tile] * (n - v)
                + courant_ref[3, j, strip, tile] * (s - v)
            )
            store(strip, tile, mask[c] * moved)


def mask_row(mask_ref, j):
    wide = mask_ref.shape[1]
    return [mask_ref[j : j + 1, c : c + LANES].astype(jnp.float32) for c in range(0, wide, LANES)]


def by_side(odd_ref, near_ref, far_ref):
    odd = odd_ref[0] != 0
    north = lambda t, strip, tile: jnp.where(odd, far_ref[t, strip, tile], near_ref[t, strip, tile])
    south = lambda t, strip, tile: jnp.where(odd, near_ref[t, strip, tile], far_ref[t, strip, tile])
    return north, south


def advance(rows_done, levels, lat, field, courant_ref, mask_ref, hw, he, weight_ref, out_ref, state):
    tracers, rows, high, wide = field.shape
    for slot in range(state.shape[0]):
        state[slot, levels:high, :] = jnp.zeros((high - levels, wide), jnp.float32)
    for j in rows_done:
        mask = mask_row(mask_ref, j)
        weight = weight_ref[j]
        for t in range(tracers):
            slot = (j * tracers + t) % state.shape[0]

            def store(strip, tile, value):
                state[slot, strip, tile] = value

            transported(t, j, levels, field, courant_ref, mask, lat, hw, he, store)
            for at in range(0, wide, 2 * LANES):
                level = vertical(weight, state[slot, :, at : at + 2 * LANES])
                out_ref[t, j, :, at : at + 2 * LANES] = level


def inner_kernel(levels, odd_ref, pair_ref, other_ref, field, courant_ref, mask_ref, weight_ref,
                 out_ref, west, east, hw, he, state):
    ends_in_place(odd_ref, pair_ref, other_ref, hw, he)
    rows_done = range(1, field.shape[1] - 1)
    advance(rows_done, levels, None, field, courant_ref, mask_ref, hw, he, weight_ref, out_ref, state)
    for strip, first, last in collect_ends(rows_done, out_ref, no_ends):
        west[strip, :] = first
        east[strip, :] = last


def edge_kernel(levels, odd_ref, pair_ref, other_ref, field, courant_ref, mask_ref, weight_ref, near_in, far_in,
                part_ref, west, east, out_ref, near_ref, far_ref, pair_out, other_out, hw, he, state):
    ends_in_place(odd_ref, pair_ref, other_ref, hw, he)
    rows_done = (0, field.shape[1] - 1)
    lat = by_side(odd_ref, near_in, far_in)
    advance(rows_done, levels, lat, field, courant_ref, mask_ref, hw, he, weight_ref, out_ref, state)
    before = lambda strip: (west[strip, :], east[strip, :])
    hand_out(odd_ref, out_ref, rows_done, before, near_ref, far_ref, pair_out, other_out)


def step(levels, odd, field, courant, mask, weight, halos):
    f32 = jnp.float32
    near, far, pair, other = halos
    tracers, rows, high, wide = field.shape
    field_shape, edge, _, end, _ = shapes_of(tracers, rows, high, wide)
    ends = [pltpu.VMEM((high, LANES), f32)] * 2
    state = [pltpu.VMEM((2, high, wide), f32)]
    params = pltpu.CompilerParams(vmem_limit_bytes=24 * MIB)
    cost = lambda n: pl.CostEstimate(flops=n * 5_000_000_000, bytes_accessed=n * 1_000_000, transcendentals=0)
    part, west, east = pl.pallas_call(
        functools.partial(inner_kernel, levels),
        out_shape=(field_shape, end, end),
        in_specs=[SMEM] + [VMEM] * 6,
        out_specs=(VMEM,) * 3,
        scratch_shapes=ends + state,
        compiler_params=params,
        cost_estimate=cost(rows - 2),
    )(odd, pair, other, field, courant, mask, weight)
    return pl.pallas_call(
        functools.partial(edge_kernel, levels),
        out_shape=(field_shape, edge, edge, end, end),
        in_specs=[SMEM] + [VMEM] * 11,
        out_specs=(VMEM,) * 5,
        scratch_shapes=ends + state,
        input_output_aliases={9: 0},
        compiler_params=params,
        cost_estimate=cost(2),
    )(odd, pair, other, field, courant, mask, weight, near, far, part, west, east)


def finish(rows_done, levels, lat, field, courant_ref, mask_ref, hw, he, out_ref, state, sems):
    tracers = field.shape[0]
    slots = state.shape[0]
    flying = {}
    for k, (j, t) in enumerate((j, t) for j in rows_done for t in range(tracers)):
        slot = k % slots
        if slot in flying:
            flying.pop(slot).wait()

        def store(strip, tile, value):
            state[slot, strip, tile] = value

        transported(t, j, levels, field, courant_ref, mask_row(mask_ref, j), lat, hw, he, store)
        copy = pltpu.make_async_copy(state.at[slot], out_ref.at[t, :, j, :], sems.at[slot])
        copy.start()
        flying[slot] = copy
    for copy in flying.values():
        copy.wait()


def final_inner_kernel(levels, odd_ref, pair_ref, other_ref, field, courant_ref, mask_ref, out_ref, hw, he, state, sems):
    ends_in_place(odd_ref, pair_ref, other_ref, hw, he)
    rows = field.shape[1]
    finish(range(1, rows - 1), levels, None, field, courant_ref, mask_ref, hw, he, out_ref, state, sems)


def final_edge_kernel(levels, odd_ref, pair_ref, other_ref, field, courant_ref, mask_ref, near_in, far_in, part_ref,
                      out_ref, hw, he, state, sems):
    ends_in_place(odd_ref, pair_ref, other_ref, hw, he)
    rows = field.shape[1]
    lat = by_side(odd_ref, near_in, far_in)
    finish((0, rows - 1), levels, lat, field, courant_ref, mask_ref, hw, he, out_ref, state, sems)


def last_step(levels, odd, field, courant, mask, halos):
    f32 = jnp.float32
    near, far, pair, other = halos
    tracers, rows, high, wide = field.shape
    slots = 4
    scratch = [pltpu.VMEM((high, LANES), f32)] * 2 + [
        pltpu.VMEM((slots, levels, wide), f32),
        pltpu.SemaphoreType.DMA((slots,)),
    ]
    shape = jax.ShapeDtypeStruct((tracers, levels, rows, wide), f32)
    params = pltpu.CompilerParams(vmem_limit_bytes=24 * MIB)
    cost = lambda n: pl.CostEstimate(flops=n * 5_000_000_000, bytes_accessed=n * 1_000_000, transcendentals=0)
    part = pl.pallas_call(
        functools.partial(final_inner_kernel, levels),
        out_shape=shape,
        in_specs=[SMEM] + [VMEM] * 5,
        out_specs=HBM,
        scratch_shapes=scratch,
        compiler_params=params,
        cost_estimate=cost(rows - 2),
    )(odd, pair, other, field, courant, mask)
    return pl.pallas_call(
        functools.partial(final_edge_kernel, levels),
        out_shape=shape,
        in_specs=[SMEM] + [VMEM] * 7 + [HBM],
        out_specs=HBM,
        scratch_shapes=scratch,
        input_output_aliases={8: 0},
        compiler_params=params,
        cost_estimate=cost(2),
    )(odd, pair, other, field, courant, mask, near, far, part)


def weights(inverse, high):
    rows, levels, _ = inverse.shape
    turned = jnp.swapaxes(inverse, 1, 2)
    pad = ((0, 0), (0, high - levels), (0, high - levels))
    whole = jnp.pad(lax.reduce_precision(turned, 8, 7), pad)
    rest = jnp.pad(turned, pad) - whole
    return jnp.concatenate(
        [jnp.concatenate([whole, whole], 2), jnp.concatenate([rest, rest], 2)], 1
    ).astype(jnp.bfloat16)


def exchange(near, far, pair, other):
    lat = lax.axis_size("lat")
    lon = lax.axis_size("lon")
    next_pair = [(i, i + 1 if i % 2 else i - 1) for i in range(1, lat - 1)]
    other = lax.ppermute(other, "lon", [(i, (i + 1 if i % 2 else i - 1) % lon) for i in range(lon)])
    pair = lax.ppermute(pair, "lon", [(i, i ^ 1) for i in range(lon)])
    far = lax.ppermute(far, "lat", next_pair)
    near = lax.ppermute(near, "lat", [(i, i ^ 1) for i in range(lat)])
    return near, far, pair, other


def local(terminal, courant, inverse, land_mask, obs_values, obs_owner, obs_cell):
    devices = lax.axis_size("lat") * lax.axis_size("lon")
    tracers, rows, levels, wide = terminal.shape
    high = padded_levels(levels)
    odd = jnp.stack([lax.axis_index("lat") % 2, lax.axis_index("lon") % 2]).astype(jnp.int32)
    send = pack(obs_owner, obs_cell, obs_values, levels, high, wide // LANES, devices)
    got = lax.all_to_all(send, ("lat", "lon"), split_axis=0, concat_axis=0, tiled=True)
    terminal, courant = prepare(terminal, courant)
    weight = weights(inverse, high)
    field, *edges = start(odd, got, weight, terminal, high, devices)
    for _ in range(STEPS - 1):
        field, *edges = step(levels, odd, field, courant, land_mask, weight, exchange(*edges))
    out = last_step(levels, odd, field, courant, land_mask, exchange(*edges))
    return jnp.swapaxes(out, 1, 2)


def solution(mesh):
    placed = (
        P(None, "lat", None, "lon"),
        P(None, "lat", None, "lon"),
        P("lat", None, None),
        P("lat", "lon"),
        P(("lat", "lon"), None),
        P(("lat", "lon"), None),
        P(("lat", "lon")),
    )
    return jax.shard_map(
        local, mesh=mesh, in_specs=placed, out_specs=P(None, "lat", None, "lon"), check_vma=False
    )
```

```python
import functools

import jax
import jax.numpy as jnp
from jax import lax
from jax.experimental import pallas as pl
from jax.experimental.pallas import tpu as pltpu
from jax.sharding import PartitionSpec as P

STEPS = 2
LANES = 128
SLOTS = 33
BANKS = 4
MIB = 1 << 20


def padded_levels(levels):
    return -(-levels // 8) * 8


SPARE = 10
LIMIT = 36
VMEM = pl.BlockSpec(memory_space=pltpu.VMEM)
SMEM = pl.BlockSpec(memory_space=pltpu.SMEM)
HBM = pl.BlockSpec(memory_space=pltpu.HBM)


def pack_kernel(geometry, owner_hbm, cell_hbm, values_hbm, send_ref, slot_ref, owner_ref, cell_ref, values_ref, slots, pay, sems):
    levels, high, columns, devices = geometry
    per_row = levels * columns
    chunks = owner_ref.shape[0]
    f32, bf16 = jnp.float32, jnp.bfloat16
    get_owner = pltpu.make_async_copy(owner_hbm, owner_ref, sems.at[0])
    get_cell = pltpu.make_async_copy(cell_hbm, cell_ref, sems.at[1])
    get_values = pltpu.make_async_copy(values_hbm, values_ref, sems.at[2])
    get_owner.start()
    get_cell.start()
    get_values.start()
    sub = lax.broadcasted_iota(jnp.int32, (LANES, LANES), 0)
    lane = lax.broadcasted_iota(jnp.int32, (LANES, LANES), 1)
    before = jnp.concatenate(
        [jnp.where(sub < lane, 1.0, 0.0), jnp.ones((LANES, LANES), f32)], axis=1
    ).astype(bf16)
    get_owner.wait()
    get_cell.wait()
    cells = cell_ref[...]
    tile_row = ((cells >> 4) * 5243) >> 17
    rest = cells - tile_row * per_row
    level = rest >> 2
    column = rest & 3
    place = (tile_row * columns + column) * high + level
    upper, lower = (place >> 6).astype(f32), (place & 63).astype(f32)
    carry = jnp.zeros((LANES, LANES), f32)
    total = jnp.zeros((LANES, LANES), f32)
    for i in range(chunks):
        own = owner_ref[i : i + 1, :]
        hot = jnp.where(sub == own, 1.0, 0.0)
        hot16 = hot.astype(bf16)
        counted = jnp.dot(hot16, before, preferred_element_type=f32)
        rank = jnp.sum(hot * (counted[:, :LANES] + carry), axis=0, keepdims=True)
        carry = carry + counted[:, LANES:]
        rank_i = rank.astype(jnp.int32)
        slots[i : i + 1, :] = own * SLOTS + rank_i
        near_sub = sub[:64]
        parts = jnp.where(
            near_sub == rank_i,
            jnp.broadcast_to(upper[i : i + 1, :], (64, LANES)),
            jnp.where(near_sub == rank_i + 32, jnp.broadcast_to(lower[i : i + 1, :], (64, LANES)), 0.0),
        )
        parts = jnp.concatenate([parts, jnp.zeros_like(parts)], axis=0).astype(bf16)
        total = total + lax.dot_general(
            hot16, parts, (((1,), (1,)), ((), ())), preferred_element_type=f32
        )
    copy = pltpu.make_async_copy(slots, slot_ref, sems.at[3])
    copy.start()
    places = total * 64.0 + pltpu.roll(total, LANES - 32, 1)
    dump = f32(2 * 8 * columns * high)
    pay[...] = jnp.where(
        lane < 32, jnp.where(lane.astype(f32) < carry, places, dump), carry
    )
    for o in range(devices):
        send_ref[o * SLOTS + 32] = pay[o : o + 1, :]
    get_values.wait()
    copy.wait()
    unroll = 64
    for i in range(chunks):

        @pl.loop(0, LANES // unroll)
        def _(c):
            base = c * unroll
            for u in range(unroll):
                send_ref[slot_ref[i, base + u]] = values_ref[i * LANES + base + u]


def pack(owner, cell, values, levels, high, columns, devices):
    rows = values.shape[0]
    chunks = rows // LANES
    return pl.pallas_call(
        functools.partial(pack_kernel, (levels, high, columns, devices)),
        out_shape=jax.ShapeDtypeStruct((devices * SLOTS, 1, LANES), jnp.float32),
        in_specs=[HBM] * 3,
        out_specs=VMEM,
        scratch_shapes=[
            pltpu.SMEM((chunks, LANES), jnp.int32),
            pltpu.VMEM((chunks, LANES), jnp.int32),
            pltpu.VMEM((chunks, LANES), jnp.int32),
            pltpu.VMEM((rows, 1, LANES), jnp.float32),
            pltpu.VMEM((chunks, LANES), jnp.int32),
            pltpu.VMEM((LANES, LANES), jnp.float32),
            pltpu.SemaphoreType.DMA((4,)),
        ],
        compiler_params=pltpu.CompilerParams(vmem_limit_bytes=60 * MIB),
    )(owner.reshape(chunks, LANES), cell.reshape(chunks, LANES), values.reshape(rows, 1, LANES))


def vertical(weight, cells):
    high = cells.shape[0]
    whole = cells.astype(jnp.bfloat16).astype(jnp.float32)
    both = jnp.concatenate([whole, cells - whole], axis=0).astype(jnp.bfloat16)
    product = jnp.dot(weight, both, preferred_element_type=jnp.float32)
    return product[:high] + product[high:]


def collect_ends(rows_done, field, before):
    tracers, rows, high, wide = field.shape
    lane = lax.broadcasted_iota(jnp.int32, (8, LANES), 1)
    for at in range(0, high, 8):
        strip = slice(at, at + 8)
        west, east = before(strip)
        for t in range(tracers):
            for j in rows_done:
                row = t * rows + j
                first = pltpu.roll(field[t, j, strip, :LANES], row, 1)
                last = pltpu.roll(field[t, j, strip, wide - LANES :], (row + 1) % LANES, 1)
                west = jnp.where(lane == row, first, west)
                east = jnp.where(lane == row, last, east)
        yield strip, west, east


def no_ends(strip):
    return jnp.zeros((8, LANES), jnp.float32), jnp.zeros((8, LANES), jnp.float32)


def hand_out(odd_ref, field, rows_done, before, near_ref, far_ref, pair_ref, other_ref):
    odd_lon = odd_ref[1] != 0
    for strip, west, east in collect_ends(rows_done, field, before):
        pair_ref[strip, :] = jnp.where(odd_lon, west, east)
        other_ref[strip, :] = jnp.where(odd_lon, east, west)
    last = field.shape[1] - 1
    odd = odd_ref[0]

    @pl.when(odd == 0)
    def _():
        near_ref[...] = field[:, last]
        far_ref[...] = field[:, 0]

    @pl.when(odd != 0)
    def _():
        near_ref[...] = field[:, 0]
        far_ref[...] = field[:, last]


def prepare_kernel(terminal_in, courant_in, out, stage, sems):
    moves = []
    for source in (terminal_in, courant_in):
        for part in range(source.shape[0]):
            at = len(moves) // out.shape[1]
            for j in range(out.shape[1]):
                sem = sems.at[len(moves)]
                load = pltpu.make_async_copy(source.at[part, :, j, :], stage.at[at, j], sem)
                moves.append((load, pltpu.make_async_copy(stage.at[at, j], out.at[at, j], sem)))
                load.start()
    for load, save in moves:
        load.wait()
        save.start()
    for load, save in moves:
        save.wait()


def prepare(terminal, courant):
    _, rows, levels, wide = terminal.shape
    parts = terminal.shape[0] + courant.shape[0]
    return pl.pallas_call(
        prepare_kernel,
        out_shape=jax.ShapeDtypeStruct((parts + SPARE, rows, levels, wide), terminal.dtype),
        in_specs=[HBM] * 2,
        out_specs=HBM,
        scratch_shapes=[
            pltpu.VMEM((parts, rows, levels, wide), terminal.dtype),
            pltpu.SemaphoreType.DMA((parts * rows,)),
        ],
        compiler_params=pltpu.CompilerParams(vmem_limit_bytes=60 * MIB),
    )(jnp.swapaxes(terminal, 1, 2), jnp.swapaxes(courant, 1, 2))


def courant_copies(tracers, inputs_hbm, target, sems, rows_done, first=0, spots=None):
    spots = spots or rows_done
    return {
        j: [
            pltpu.make_async_copy(
                inputs_hbm.at[tracers + part, j], target.at[part, spot], sems.at[first + n * target.shape[0] + part]
            )
            for part in range(target.shape[0])
        ]
        for n, (j, spot) in enumerate(zip(rows_done, spots))
    }


def start_kernel(devices, odd_ref, got_ref, weight_hbm, inputs_hbm, out_ref, near_ref, far_ref, pair_ref, other_ref,
                 terminal_ref, weight_ref, addr_v, addr_s, state, sems, *banks):
    tracers, rows, levels, wide = terminal_ref.shape
    columns = wide // LANES
    get_terminal = pltpu.make_async_copy(inputs_hbm.at[pl.ds(0, terminal_ref.shape[0])], terminal_ref, sems.at[1])
    get_weight = pltpu.make_async_copy(weight_hbm, weight_ref, sems.at[2])
    get_terminal.start()
    get_weight.start()
    high = state.shape[1]
    whole = levels // 8 * 8
    for o in range(devices):
        addr_v[o : o + 1, :] = got_ref[o * SLOTS + 32].astype(jnp.int32)
    copy = pltpu.make_async_copy(addr_v, addr_s, sems.at[0])
    copy.start()
    clear = 64
    for bank in banks:

        @pl.loop(0, bank.shape[0] // clear)
        def _(i):
            bank[pl.ds(pl.multiple_of(i * clear, clear), clear), :] = jnp.zeros((clear, LANES), jnp.float32)

    copy.wait()

    @pl.loop(0, devices // BANKS)
    def _(group):
        first = group * BANKS
        most = addr_s[first, 32]
        for b in range(1, BANKS):
            most = jnp.maximum(most, addr_s[first + b, 32])

        @pl.loop(0, (most + 3) // 4)
        def _(c):
            for u in range(4):
                for b, bank in enumerate(banks):
                    place = addr_s[first + b, c * 4 + u]
                    bank[pl.ds(place, 1), :] += got_ref[(first + b) * SLOTS + c * 4 + u]

    for slot in range(state.shape[0]):
        state[slot, levels:high, :] = jnp.zeros((high - levels, wide), jnp.float32)
    get_terminal.wait()
    get_weight.wait()
    for j in range(rows):
        weight = weight_ref[j]
        for t in range(tracers):
            slot = (j * tracers + t) % state.shape[0]
            for c in range(columns):
                tile = slice(c * LANES, (c + 1) * LANES)
                base = ((t * rows + j) * columns + c) * high
                for low, top in ((0, whole), (whole, levels)):
                    total = terminal_ref[t, j, low:top, tile]
                    for bank in banks:
                        total = total + bank[base + low : base + top, :]
                    state[slot, low:top, tile] = total
            for at in range(0, wide, 2 * LANES):
                out_ref[t, j, :, at : at + 2 * LANES] = vertical(weight, state[slot, :, at : at + 2 * LANES])
    hand_out(odd_ref, out_ref, range(rows), no_ends, near_ref, far_ref, pair_ref, other_ref)


def shapes_of(tracers, rows, high, wide):
    f32 = jnp.float32
    edge = jax.ShapeDtypeStruct((tracers, high, wide), f32)
    end = jax.ShapeDtypeStruct((high, LANES), f32)
    return jax.ShapeDtypeStruct((tracers, rows, high, wide), f32), edge, edge, end, end


def start(odd, got, weight, inputs, tracers, high, devices):
    f32 = jnp.float32
    _, rows, levels, wide = inputs.shape
    places = tracers * rows * (wide // LANES) * high
    return pl.pallas_call(
        functools.partial(start_kernel, devices),
        out_shape=shapes_of(tracers, rows, high, wide),
        in_specs=[SMEM, VMEM, HBM, HBM],
        out_specs=(VMEM,) * 5,
        scratch_shapes=[
            pltpu.VMEM((tracers, rows, levels, wide), f32),
            pltpu.VMEM(weight.shape, weight.dtype),
            pltpu.VMEM((devices, LANES), jnp.int32),
            pltpu.SMEM((devices, LANES), jnp.int32),
            pltpu.VMEM((2, high, wide), f32),
            pltpu.SemaphoreType.DMA((3,)),
        ]
        + [pltpu.VMEM((places + 64, LANES), f32) for _ in range(BANKS)],
        compiler_params=pltpu.CompilerParams(vmem_limit_bytes=36 * MIB),
    )(odd, got, weight, inputs)


def ends_in_place(odd_ref, pair_ref, other_ref, west, east):
    odd = odd_ref[1] != 0
    pair, other = pair_ref[...], other_ref[...]
    west[...] = jnp.where(odd, pair, other)
    east[...] = jnp.where(odd, other, pair)


def transported(t, j, levels, field, courant, mask, lat, west, east, store):
    rows, wide = field.shape[1], field.shape[3]
    row = t * rows + j
    tiles = [slice(c * LANES, (c + 1) * LANES) for c in range(wide // LANES)]
    for at in range(0, levels, 8):
        count = min(8, levels - at)
        strip = slice(at, at + count)
        lane = lax.broadcasted_iota(jnp.int32, (count, LANES), 1)
        here = [field[t, j, strip, tile] for tile in tiles]
        left = [pltpu.roll(x, LANES - 1, 1) for x in here]
        left.append(pltpu.roll(east[strip, :], LANES - 1 - row, 1))
        right = [pltpu.roll(west[strip, :], (LANES - row) % LANES, 1)]
        right += [pltpu.roll(x, 1, 1) for x in here]
        for c, tile in enumerate(tiles):
            v = here[c]
            e = jnp.where(lane == LANES - 1, left[c + 1], left[c])
            w = jnp.where(lane == 0, right[c], right[c + 1])
            n = lat[0](t, strip, tile) if j == rows - 1 else field[t, j + 1, strip, tile]
            s = lat[1](t, strip, tile) if j == 0 else field[t, j - 1, strip, tile]
            moved = (
                v
                + courant(0, j, strip, tile) * (e - v)
                + courant(1, j, strip, tile) * (w - v)
                + courant(2, j, strip, tile) * (n - v)
                + courant(3, j, strip, tile) * (s - v)
            )
            store(strip, tile, mask[c] * moved)


def mask_row(mask_ref, j):
    wide = mask_ref.shape[1]
    return [mask_ref[j : j + 1, c : c + LANES].astype(jnp.float32) for c in range(0, wide, LANES)]


def by_side(odd_ref, near_ref, far_ref):
    odd = odd_ref[0] != 0
    north = lambda t, strip, tile: jnp.where(odd, far_ref[t, strip, tile], near_ref[t, strip, tile])
    south = lambda t, strip, tile: jnp.where(odd, near_ref[t, strip, tile], far_ref[t, strip, tile])
    return north, south


def advance(rows_done, levels, lat, field, courant, ready, mask_ref, hw, he, weight_ref, out_ref, state):
    tracers, rows, high, wide = field.shape
    for slot in range(state.shape[0]):
        state[slot, levels:high, :] = jnp.zeros((high - levels, wide), jnp.float32)
    for j in rows_done:
        ready(j)
        mask = mask_row(mask_ref, j)
        weight = weight_ref[j]
        for t in range(tracers):
            slot = (j * tracers + t) % state.shape[0]

            def store(strip, tile, value):
                state[slot, strip, tile] = value

            transported(t, j, levels, field, courant, mask, lat, hw, he, store)
            for at in range(0, wide, 2 * LANES):
                level = vertical(weight, state[slot, :, at : at + 2 * LANES])
                out_ref[t, j, :, at : at + 2 * LANES] = level


def arriving(copies):
    def ready(j):
        for copy in copies[j]:
            copy.wait()

    return ready


def inner_courant(courant_ref):
    return lambda k, j, strip, tile: courant_ref[k, j - 1, strip, tile]


def edge_courant(courant_ref):
    return lambda k, j, strip, tile: courant_ref[k, min(j, 1), strip, tile]


def inner_kernel(levels, odd_ref, pair_ref, other_ref, field, inputs_hbm, mask_ref, weight_ref,
                 out_ref, west, east, edge_ref, hw, he, state, courant_ref, sems):
    tracers, rows = field.shape[:2]
    rows_done = range(1, rows - 1)
    copies = courant_copies(tracers, inputs_hbm, courant_ref, sems, rows_done, 0, range(rows - 2))
    edges = courant_copies(
        tracers, inputs_hbm, edge_ref, sems, (0, rows - 1), (rows - 2) * courant_ref.shape[0], (0, 1)
    )
    for group in (*copies.values(), *edges.values()):
        for copy in group:
            copy.start()
    ends_in_place(odd_ref, pair_ref, other_ref, hw, he)
    courant = inner_courant(courant_ref)
    advance(rows_done, levels, None, field, courant, arriving(copies), mask_ref, hw, he, weight_ref, out_ref, state)
    for strip, first, last in collect_ends(rows_done, out_ref, no_ends):
        west[strip, :] = first
        east[strip, :] = last
    for j in edges:
        arriving(edges)(j)


def edge_kernel(levels, odd_ref, pair_ref, other_ref, field, courant_ref, mask_ref, weight_ref, near_in, far_in,
                part_ref, west, east, out_ref, near_ref, far_ref, pair_out, other_out, hw, he, state):
    ends_in_place(odd_ref, pair_ref, other_ref, hw, he)
    rows_done = (0, field.shape[1] - 1)
    lat = by_side(odd_ref, near_in, far_in)
    courant = edge_courant(courant_ref)
    advance(rows_done, levels, lat, field, courant, lambda j: None, mask_ref, hw, he, weight_ref, out_ref, state)
    before = lambda strip: (west[strip, :], east[strip, :])
    hand_out(odd_ref, out_ref, rows_done, before, near_ref, far_ref, pair_out, other_out)


COST = pl.CostEstimate(flops=30_000_000_000, bytes_accessed=8_000_000, transcendentals=0)


def step(levels, odd, field, inputs, mask, weight, halos):
    f32 = jnp.float32
    near, far, pair, other = halos
    tracers, rows, high, wide = field.shape
    field_shape, edge, _, end, _ = shapes_of(tracers, rows, high, wide)
    parts = inputs.shape[0] - tracers - SPARE
    ends = [pltpu.VMEM((high, LANES), f32)] * 2
    state = [pltpu.VMEM((2, high, wide), f32)]
    params = pltpu.CompilerParams(vmem_limit_bytes=LIMIT * MIB)
    part, west, east, edge_flow = pl.pallas_call(
        functools.partial(inner_kernel, levels),
        out_shape=(field_shape, end, end, jax.ShapeDtypeStruct((parts, 2, levels, wide), f32)),
        in_specs=[SMEM] + [VMEM] * 3 + [HBM] + [VMEM] * 2,
        out_specs=(VMEM,) * 4,
        scratch_shapes=ends
        + state
        + [pltpu.VMEM((parts, rows - 2, levels, wide), f32), pltpu.SemaphoreType.DMA((parts * rows,))],
        compiler_params=params,
        cost_estimate=COST,
    )(odd, pair, other, field, inputs, mask, weight)
    return *pl.pallas_call(
        functools.partial(edge_kernel, levels),
        out_shape=(field_shape, edge, edge, end, end),
        in_specs=[SMEM] + [VMEM] * 11,
        out_specs=(VMEM,) * 5,
        scratch_shapes=ends + state,
        input_output_aliases={9: 0},
        compiler_params=params,
    )(odd, pair, other, field, edge_flow, mask, weight, near, far, part, west, east), edge_flow


def finish(rows_done, levels, lat, field, courant, ready, mask_ref, hw, he, out_ref, state, sems):
    tracers = field.shape[0]
    slots = state.shape[0]
    flying = {}
    for k, (j, t) in enumerate((j, t) for j in rows_done for t in range(tracers)):
        slot = k % slots
        if t == 0:
            ready(j)
        if slot in flying:
            flying.pop(slot).wait()

        def store(strip, tile, value):
            state[slot, strip, tile] = value

        transported(t, j, levels, field, courant, mask_row(mask_ref, j), lat, hw, he, store)
        copy = pltpu.make_async_copy(state.at[slot], out_ref.at[t, :, j, :], sems.at[slot])
        copy.start()
        flying[slot] = copy
    for copy in flying.values():
        copy.wait()


def final_inner_kernel(levels, odd_ref, pair_ref, other_ref, field, inputs_hbm, mask_ref, out_ref, hw, he, state, sems,
                       courant_ref, courant_sems):
    tracers, rows = field.shape[:2]
    rows_done = range(1, rows - 1)
    copies = courant_copies(tracers, inputs_hbm, courant_ref, courant_sems, rows_done, 0, range(rows - 2))
    for group in copies.values():
        for copy in group:
            copy.start()
    ends_in_place(odd_ref, pair_ref, other_ref, hw, he)
    courant = inner_courant(courant_ref)
    finish(rows_done, levels, None, field, courant, arriving(copies), mask_ref, hw, he, out_ref, state, sems)


def final_edge_kernel(levels, odd_ref, pair_ref, other_ref, field, courant_ref, mask_ref, near_in, far_in, part_ref,
                      out_ref, hw, he, state, sems):
    ends_in_place(odd_ref, pair_ref, other_ref, hw, he)
    rows = field.shape[1]
    lat = by_side(odd_ref, near_in, far_in)
    courant = edge_courant(courant_ref)
    finish((0, rows - 1), levels, lat, field, courant, lambda j: None, mask_ref, hw, he, out_ref, state, sems)


def last_step(levels, odd, field, inputs, edge_flow, mask, halos):
    f32 = jnp.float32
    near, far, pair, other = halos
    tracers, rows, high, wide = field.shape
    parts = edge_flow.shape[0]
    slots = 4
    scratch = [pltpu.VMEM((high, LANES), f32)] * 2 + [
        pltpu.VMEM((slots, levels, wide), f32),
        pltpu.SemaphoreType.DMA((slots,)),
    ]
    shape = jax.ShapeDtypeStruct((tracers, levels, rows, wide), f32)
    params = pltpu.CompilerParams(vmem_limit_bytes=LIMIT * MIB)
    part = pl.pallas_call(
        functools.partial(final_inner_kernel, levels),
        out_shape=shape,
        in_specs=[SMEM] + [VMEM] * 3 + [HBM, VMEM],
        out_specs=HBM,
        scratch_shapes=scratch
        + [
            pltpu.VMEM((parts, rows - 2, levels, wide), f32),
            pltpu.SemaphoreType.DMA((parts * (rows - 2),)),
        ],
        compiler_params=params,
        cost_estimate=COST,
    )(odd, pair, other, field, inputs, mask)
    return pl.pallas_call(
        functools.partial(final_edge_kernel, levels),
        out_shape=shape,
        in_specs=[SMEM] + [VMEM] * 7 + [HBM],
        out_specs=HBM,
        scratch_shapes=scratch,
        input_output_aliases={8: 0},
        compiler_params=params,
    )(odd, pair, other, field, edge_flow, mask, near, far, part)


def weights(inverse, high):
    rows, levels, _ = inverse.shape
    turned = jnp.swapaxes(inverse, 1, 2)
    pad = ((0, 0), (0, high - levels), (0, high - levels))
    whole = jnp.pad(lax.reduce_precision(turned, 8, 7), pad)
    rest = jnp.pad(turned, pad) - whole
    return jnp.concatenate(
        [jnp.concatenate([whole, whole], 2), jnp.concatenate([rest, rest], 2)], 1
    ).astype(jnp.bfloat16)


def exchange(near, far, pair, other):
    lat = lax.axis_size("lat")
    lon = lax.axis_size("lon")
    next_pair = [(i, i + 1 if i % 2 else i - 1) for i in range(1, lat - 1)]
    other = lax.ppermute(other, "lon", [(i, (i + 1 if i % 2 else i - 1) % lon) for i in range(lon)])
    pair = lax.ppermute(pair, "lon", [(i, i ^ 1) for i in range(lon)])
    far = lax.ppermute(far, "lat", next_pair)
    near = lax.ppermute(near, "lat", [(i, i ^ 1) for i in range(lat)])
    return near, far, pair, other


def local(terminal, courant, inverse, land_mask, obs_values, obs_owner, obs_cell):
    devices = lax.axis_size("lat") * lax.axis_size("lon")
    tracers, rows, levels, wide = terminal.shape
    high = padded_levels(levels)
    odd = jnp.stack([lax.axis_index("lat") % 2, lax.axis_index("lon") % 2]).astype(jnp.int32)
    send = pack(obs_owner, obs_cell, obs_values, levels, high, wide // LANES, devices)
    got = lax.all_to_all(send, ("lat", "lon"), split_axis=0, concat_axis=0, tiled=True)
    inputs = prepare(terminal, courant)
    weight = weights(inverse, high)
    field, *edges = start(odd, got, weight, inputs, tracers, high, devices)
    for _ in range(STEPS - 1):
        field, *edges, edge_flow = step(levels, odd, field, inputs, land_mask, weight, exchange(*edges))
    out = last_step(levels, odd, field, inputs, edge_flow, land_mask, exchange(*edges))
    return jnp.swapaxes(out, 1, 2)


def solution(mesh):
    placed = (
        P(None, "lat", None, "lon"),
        P(None, "lat", None, "lon"),
        P("lat", None, None),
        P("lat", "lon"),
        P(("lat", "lon"), None),
        P(("lat", "lon"), None),
        P(("lat", "lon")),
    )
    return jax.shard_map(
        local, mesh=mesh, in_specs=placed, out_specs=P(None, "lat", None, "lon"), check_vma=False
    )
```

```python
import functools

import jax
import jax.numpy as jnp
from jax import lax
from jax.experimental import pallas as pl
from jax.experimental.pallas import tpu as pltpu
from jax.sharding import PartitionSpec as P

STEPS = 2
LANES = 128
SLOTS = 33
BANKS = 4
MIB = 1 << 20


def padded_levels(levels):
    return -(-levels // 8) * 8


SPARE = 10
LIMIT = 24
VMEM = pl.BlockSpec(memory_space=pltpu.VMEM)
SMEM = pl.BlockSpec(memory_space=pltpu.SMEM)
HBM = pl.BlockSpec(memory_space=pltpu.HBM)


def pack_kernel(geometry, owner_hbm, cell_hbm, values_hbm, send_ref, slot_ref, owner_ref, cell_ref, values_ref, slots, pay, sems):
    levels, high, columns, devices = geometry
    per_row = levels * columns
    chunks = owner_ref.shape[0]
    f32, bf16 = jnp.float32, jnp.bfloat16
    get_owner = pltpu.make_async_copy(owner_hbm, owner_ref, sems.at[0])
    get_cell = pltpu.make_async_copy(cell_hbm, cell_ref, sems.at[1])
    get_values = pltpu.make_async_copy(values_hbm, values_ref, sems.at[2])
    get_owner.start()
    get_cell.start()
    get_values.start()
    sub = lax.broadcasted_iota(jnp.int32, (LANES, LANES), 0)
    lane = lax.broadcasted_iota(jnp.int32, (LANES, LANES), 1)
    before = jnp.concatenate(
        [jnp.where(sub < lane, 1.0, 0.0), jnp.ones((LANES, LANES), f32)], axis=1
    ).astype(bf16)
    get_owner.wait()
    get_cell.wait()
    cells = cell_ref[...]
    tile_row = ((cells >> 4) * 5243) >> 17
    rest = cells - tile_row * per_row
    level = rest >> 2
    column = rest & 3
    place = (tile_row * columns + column) * high + level
    upper, lower = (place >> 6).astype(f32), (place & 63).astype(f32)
    carry = jnp.zeros((LANES, LANES), f32)
    total = jnp.zeros((LANES, LANES), f32)
    for i in range(chunks):
        own = owner_ref[i : i + 1, :]
        hot = jnp.where(sub == own, 1.0, 0.0)
        hot16 = hot.astype(bf16)
        counted = jnp.dot(hot16, before, preferred_element_type=f32)
        rank = jnp.sum(hot * (counted[:, :LANES] + carry), axis=0, keepdims=True)
        carry = carry + counted[:, LANES:]
        rank_i = rank.astype(jnp.int32)
        slots[i : i + 1, :] = own * SLOTS + rank_i
        near_sub = sub[:64]
        parts = jnp.where(
            near_sub == rank_i,
            jnp.broadcast_to(upper[i : i + 1, :], (64, LANES)),
            jnp.where(near_sub == rank_i + 32, jnp.broadcast_to(lower[i : i + 1, :], (64, LANES)), 0.0),
        )
        parts = jnp.concatenate([parts, jnp.zeros_like(parts)], axis=0).astype(bf16)
        total = total + lax.dot_general(
            hot16, parts, (((1,), (1,)), ((), ())), preferred_element_type=f32
        )
    copy = pltpu.make_async_copy(slots, slot_ref, sems.at[3])
    copy.start()
    places = total * 64.0 + pltpu.roll(total, LANES - 32, 1)
    dump = f32(2 * 8 * columns * high)
    pay[...] = jnp.where(
        lane < 32, jnp.where(lane.astype(f32) < carry, places, dump), carry
    )
    for o in range(devices):
        send_ref[o * SLOTS + 32] = pay[o : o + 1, :]
    get_values.wait()
    copy.wait()
    unroll = 64
    for i in range(chunks):

        @pl.loop(0, LANES // unroll)
        def _(c):
            base = c * unroll
            for u in range(unroll):
                send_ref[slot_ref[i, base + u]] = values_ref[i * LANES + base + u]


def pack(owner, cell, values, levels, high, columns, devices):
    rows = values.shape[0]
    chunks = rows // LANES
    return pl.pallas_call(
        functools.partial(pack_kernel, (levels, high, columns, devices)),
        out_shape=jax.ShapeDtypeStruct((devices * SLOTS, 1, LANES), jnp.float32),
        in_specs=[HBM] * 3,
        out_specs=VMEM,
        scratch_shapes=[
            pltpu.SMEM((chunks, LANES), jnp.int32),
            pltpu.VMEM((chunks, LANES), jnp.int32),
            pltpu.VMEM((chunks, LANES), jnp.int32),
            pltpu.VMEM((rows, 1, LANES), jnp.float32),
            pltpu.VMEM((chunks, LANES), jnp.int32),
            pltpu.VMEM((LANES, LANES), jnp.float32),
            pltpu.SemaphoreType.DMA((4,)),
        ],
        compiler_params=pltpu.CompilerParams(vmem_limit_bytes=60 * MIB),
    )(owner.reshape(chunks, LANES), cell.reshape(chunks, LANES), values.reshape(rows, 1, LANES))


def vertical(weight, cells):
    high = cells.shape[0]
    whole = cells.astype(jnp.bfloat16).astype(jnp.float32)
    both = jnp.concatenate([whole, cells - whole], axis=0).astype(jnp.bfloat16)
    product = jnp.dot(weight, both, preferred_element_type=jnp.float32)
    return product[:high] + product[high:]


def collect_ends(rows_done, field, before):
    tracers, rows, high, wide = field.shape
    lane = lax.broadcasted_iota(jnp.int32, (8, LANES), 1)
    for at in range(0, high, 8):
        strip = slice(at, at + 8)
        west, east = before(strip)
        for t in range(tracers):
            for j in rows_done:
                row = t * rows + j
                first = pltpu.roll(field[t, j, strip, :LANES], row, 1)
                last = pltpu.roll(field[t, j, strip, wide - LANES :], (row + 1) % LANES, 1)
                west = jnp.where(lane == row, first, west)
                east = jnp.where(lane == row, last, east)
        yield strip, west, east


def no_ends(strip):
    return jnp.zeros((8, LANES), jnp.float32), jnp.zeros((8, LANES), jnp.float32)


def hand_out(odd_ref, field, rows_done, before, near_ref, far_ref, pair_ref, other_ref):
    odd_lon = odd_ref[1] != 0
    for strip, west, east in collect_ends(rows_done, field, before):
        pair_ref[strip, :] = jnp.where(odd_lon, west, east)
        other_ref[strip, :] = jnp.where(odd_lon, east, west)
    last = field.shape[1] - 1
    odd = odd_ref[0]

    @pl.when(odd == 0)
    def _():
        near_ref[...] = field[:, last]
        far_ref[...] = field[:, 0]

    @pl.when(odd != 0)
    def _():
        near_ref[...] = field[:, 0]
        far_ref[...] = field[:, last]


def prepare_kernel(terminal_in, courant_in, out, stage, sems):
    moves = []
    for source in (terminal_in, courant_in):
        for part in range(source.shape[0]):
            at = len(moves) // out.shape[1]
            for j in range(out.shape[1]):
                sem = sems.at[len(moves)]
                load = pltpu.make_async_copy(source.at[part, :, j, :], stage.at[at, j], sem)
                moves.append((load, pltpu.make_async_copy(stage.at[at, j], out.at[at, j], sem)))
                load.start()
    for load, save in moves:
        load.wait()
        save.start()
    for load, save in moves:
        save.wait()


def prepare(terminal, courant):
    _, rows, levels, wide = terminal.shape
    parts = terminal.shape[0] + courant.shape[0]
    return pl.pallas_call(
        prepare_kernel,
        out_shape=jax.ShapeDtypeStruct((parts + SPARE, rows, levels, wide), terminal.dtype),
        in_specs=[HBM] * 2,
        out_specs=HBM,
        scratch_shapes=[
            pltpu.VMEM((parts, rows, levels, wide), terminal.dtype),
            pltpu.SemaphoreType.DMA((parts * rows,)),
        ],
        compiler_params=pltpu.CompilerParams(vmem_limit_bytes=60 * MIB),
    )(jnp.swapaxes(terminal, 1, 2), jnp.swapaxes(courant, 1, 2))


def start_kernel(devices, odd_ref, got_ref, weight_hbm, inputs_hbm, out_ref, near_ref, far_ref, pair_ref, other_ref, courant_ref,
                 terminal_ref, weight_ref, addr_v, addr_s, state, sems, *banks):
    tracers, rows, levels, wide = terminal_ref.shape
    columns = wide // LANES
    get_terminal = pltpu.make_async_copy(inputs_hbm.at[pl.ds(0, terminal_ref.shape[0])], terminal_ref, sems.at[1])
    get_weight = pltpu.make_async_copy(weight_hbm, weight_ref, sems.at[2])
    tracers, parts = terminal_ref.shape[0], courant_ref.shape[0]
    get_courant = pltpu.make_async_copy(inputs_hbm.at[pl.ds(tracers, parts)], courant_ref, sems.at[3])
    get_terminal.start()
    get_weight.start()
    get_courant.start()
    high = state.shape[1]
    whole = levels // 8 * 8
    for o in range(devices):
        addr_v[o : o + 1, :] = got_ref[o * SLOTS + 32].astype(jnp.int32)
    copy = pltpu.make_async_copy(addr_v, addr_s, sems.at[0])
    copy.start()
    clear = 64
    for bank in banks:

        @pl.loop(0, bank.shape[0] // clear)
        def _(i):
            bank[pl.ds(pl.multiple_of(i * clear, clear), clear), :] = jnp.zeros((clear, LANES), jnp.float32)

    copy.wait()

    @pl.loop(0, devices // BANKS)
    def _(group):
        first = group * BANKS
        most = addr_s[first, 32]
        for b in range(1, BANKS):
            most = jnp.maximum(most, addr_s[first + b, 32])

        @pl.loop(0, (most + 7) // 8)
        def _(c):
            for u in range(8):
                for b, bank in enumerate(banks):
                    place = addr_s[first + b, c * 8 + u]
                    bank[pl.ds(place, 1), :] += got_ref[(first + b) * SLOTS + c * 8 + u]

    for slot in range(state.shape[0]):
        state[slot, levels:high, :] = jnp.zeros((high - levels, wide), jnp.float32)
    get_terminal.wait()
    get_weight.wait()
    for j in range(rows):
        weight = weight_ref[j]
        for t in range(tracers):
            slot = (j * tracers + t) % state.shape[0]
            for c in range(columns):
                tile = slice(c * LANES, (c + 1) * LANES)
                base = ((t * rows + j) * columns + c) * high
                for low, top in ((0, whole), (whole, levels)):
                    total = terminal_ref[t, j, low:top, tile]
                    for bank in banks:
                        total = total + bank[base + low : base + top, :]
                    state[slot, low:top, tile] = total
            for at in range(0, wide, 2 * LANES):
                out_ref[t, j, :, at : at + 2 * LANES] = vertical(weight, state[slot, :, at : at + 2 * LANES])
    hand_out(odd_ref, out_ref, range(rows), no_ends, near_ref, far_ref, pair_ref, other_ref)
    get_courant.wait()


def shapes_of(tracers, rows, high, wide):
    f32 = jnp.float32
    edge = jax.ShapeDtypeStruct((tracers, high, wide), f32)
    end = jax.ShapeDtypeStruct((high, LANES), f32)
    return jax.ShapeDtypeStruct((tracers, rows, high, wide), f32), edge, edge, end, end


def start(odd, got, weight, inputs, tracers, high, devices):
    f32 = jnp.float32
    parts, rows, levels, wide = inputs.shape
    places = tracers * rows * (wide // LANES) * high
    return pl.pallas_call(
        functools.partial(start_kernel, devices),
        out_shape=shapes_of(tracers, rows, high, wide)
        + (jax.ShapeDtypeStruct((parts - SPARE - tracers, rows, levels, wide), f32),),
        in_specs=[SMEM, VMEM, HBM, HBM],
        out_specs=(VMEM,) * 6,
        scratch_shapes=[
            pltpu.VMEM((tracers, rows, levels, wide), f32),
            pltpu.VMEM(weight.shape, weight.dtype),
            pltpu.VMEM((devices, LANES), jnp.int32),
            pltpu.SMEM((devices, LANES), jnp.int32),
            pltpu.VMEM((2, high, wide), f32),
            pltpu.SemaphoreType.DMA((4,)),
        ]
        + [pltpu.VMEM((places + 64, LANES), f32) for _ in range(BANKS)],
        compiler_params=pltpu.CompilerParams(vmem_limit_bytes=36 * MIB),
    )(odd, got, weight, inputs)


def ends_in_place(odd_ref, pair_ref, other_ref, west, east):
    odd = odd_ref[1] != 0
    pair, other = pair_ref[...], other_ref[...]
    west[...] = jnp.where(odd, pair, other)
    east[...] = jnp.where(odd, other, pair)


def transported(t, j, levels, field, courant_ref, mask, lat, west, east, store):
    rows, wide = field.shape[1], field.shape[3]
    row = t * rows + j
    tiles = [slice(c * LANES, (c + 1) * LANES) for c in range(wide // LANES)]
    for at in range(0, levels, 8):
        count = min(8, levels - at)
        strip = slice(at, at + count)
        lane = lax.broadcasted_iota(jnp.int32, (count, LANES), 1)
        here = [field[t, j, strip, tile] for tile in tiles]
        left = [pltpu.roll(x, LANES - 1, 1) for x in here]
        left.append(pltpu.roll(east[strip, :], LANES - 1 - row, 1))
        right = [pltpu.roll(west[strip, :], (LANES - row) % LANES, 1)]
        right += [pltpu.roll(x, 1, 1) for x in here]
        for c, tile in enumerate(tiles):
            v = here[c]
            e = jnp.where(lane == LANES - 1, left[c + 1], left[c])
            w = jnp.where(lane == 0, right[c], right[c + 1])
            n = lat[0](t, strip, tile) if j == rows - 1 else field[t, j + 1, strip, tile]
            s = lat[1](t, strip, tile) if j == 0 else field[t, j - 1, strip, tile]
            moved = (
                v
                + courant_ref[0, j, strip, tile] * (e - v)
                + courant_ref[1, j, strip, tile] * (w - v)
                + courant_ref[2, j, strip, tile] * (n - v)
                + courant_ref[3, j, strip, tile] * (s - v)
            )
            store(strip, tile, mask[c] * moved)


def mask_row(mask_ref, j):
    wide = mask_ref.shape[1]
    return [mask_ref[j : j + 1, c : c + LANES].astype(jnp.float32) for c in range(0, wide, LANES)]


def by_side(odd_ref, near_ref, far_ref):
    odd = odd_ref[0] != 0
    north = lambda t, strip, tile: jnp.where(odd, far_ref[t, strip, tile], near_ref[t, strip, tile])
    south = lambda t, strip, tile: jnp.where(odd, near_ref[t, strip, tile], far_ref[t, strip, tile])
    return north, south


def advance(rows_done, levels, lat, field, courant_ref, mask_ref, hw, he, weight_ref, out_ref, state):
    tracers, rows, high, wide = field.shape
    for slot in range(state.shape[0]):
        state[slot, levels:high, :] = jnp.zeros((high - levels, wide), jnp.float32)
    for j in rows_done:
        mask = mask_row(mask_ref, j)
        weight = weight_ref[j]
        for t in range(tracers):
            slot = (j * tracers + t) % state.shape[0]

            def store(strip, tile, value):
                state[slot, strip, tile] = value

            transported(t, j, levels, field, courant_ref, mask, lat, hw, he, store)
            for at in range(0, wide, 2 * LANES):
                level = vertical(weight, state[slot, :, at : at + 2 * LANES])
                out_ref[t, j, :, at : at + 2 * LANES] = level


def inner_kernel(levels, odd_ref, pair_ref, other_ref, field, courant_ref, mask_ref, weight_ref,
                 out_ref, west, east, hw, he, state):
    ends_in_place(odd_ref, pair_ref, other_ref, hw, he)
    rows_done = range(1, field.shape[1] - 1)
    advance(rows_done, levels, None, field, courant_ref, mask_ref, hw, he, weight_ref, out_ref, state)
    for strip, first, last in collect_ends(rows_done, out_ref, no_ends):
        west[strip, :] = first
        east[strip, :] = last


def edge_kernel(levels, odd_ref, pair_ref, other_ref, field, courant_ref, mask_ref, weight_ref, near_in, far_in,
                part_ref, west, east, out_ref, near_ref, far_ref, pair_out, other_out, hw, he, state):
    ends_in_place(odd_ref, pair_ref, other_ref, hw, he)
    rows_done = (0, field.shape[1] - 1)
    lat = by_side(odd_ref, near_in, far_in)
    advance(rows_done, levels, lat, field, courant_ref, mask_ref, hw, he, weight_ref, out_ref, state)
    before = lambda strip: (west[strip, :], east[strip, :])
    hand_out(odd_ref, out_ref, rows_done, before, near_ref, far_ref, pair_out, other_out)


COST = pl.CostEstimate(flops=30_000_000_000, bytes_accessed=8_000_000, transcendentals=0)


def step(levels, odd, field, courant, mask, weight, halos):
    f32 = jnp.float32
    near, far, pair, other = halos
    tracers, rows, high, wide = field.shape
    field_shape, edge, _, end, _ = shapes_of(tracers, rows, high, wide)
    scratch = [pltpu.VMEM((high, LANES), f32)] * 2 + [pltpu.VMEM((2, high, wide), f32)]
    params = pltpu.CompilerParams(vmem_limit_bytes=LIMIT * MIB)
    part, west, east = pl.pallas_call(
        functools.partial(inner_kernel, levels),
        out_shape=(field_shape, end, end),
        in_specs=[SMEM] + [VMEM] * 6,
        out_specs=(VMEM,) * 3,
        scratch_shapes=scratch,
        compiler_params=params,
        cost_estimate=COST,
    )(odd, pair, other, field, courant, mask, weight)
    return pl.pallas_call(
        functools.partial(edge_kernel, levels),
        out_shape=(field_shape, edge, edge, end, end),
        in_specs=[SMEM] + [VMEM] * 11,
        out_specs=(VMEM,) * 5,
        scratch_shapes=scratch,
        input_output_aliases={9: 0},
        compiler_params=params,
    )(odd, pair, other, field, courant, mask, weight, near, far, part, west, east)


def finish(rows_done, levels, lat, field, courant_ref, mask_ref, hw, he, out_ref, state, sems):
    tracers = field.shape[0]
    slots = state.shape[0]
    flying = {}
    for k, (j, t) in enumerate((j, t) for j in rows_done for t in range(tracers)):
        slot = k % slots
        if slot in flying:
            flying.pop(slot).wait()

        def store(strip, tile, value):
            state[slot, strip, tile] = value

        transported(t, j, levels, field, courant_ref, mask_row(mask_ref, j), lat, hw, he, store)
        copy = pltpu.make_async_copy(state.at[slot], out_ref.at[t, :, j, :], sems.at[slot])
        copy.start()
        flying[slot] = copy
    for copy in flying.values():
        copy.wait()


def final_inner_kernel(levels, odd_ref, pair_ref, other_ref, field, courant_ref, mask_ref, out_ref, hw, he, state, sems):
    ends_in_place(odd_ref, pair_ref, other_ref, hw, he)
    rows_done = range(1, field.shape[1] - 1)
    finish(rows_done, levels, None, field, courant_ref, mask_ref, hw, he, out_ref, state, sems)


def final_edge_kernel(levels, odd_ref, pair_ref, other_ref, field, courant_ref, mask_ref, near_in, far_in, part_ref,
                      out_ref, hw, he, state, sems):
    ends_in_place(odd_ref, pair_ref, other_ref, hw, he)
    lat = by_side(odd_ref, near_in, far_in)
    finish((0, field.shape[1] - 1), levels, lat, field, courant_ref, mask_ref, hw, he, out_ref, state, sems)


def last_step(levels, odd, field, courant, mask, halos):
    f32 = jnp.float32
    near, far, pair, other = halos
    tracers, rows, high, wide = field.shape
    slots = 12
    scratch = [pltpu.VMEM((high, LANES), f32)] * 2 + [
        pltpu.VMEM((slots, levels, wide), f32),
        pltpu.SemaphoreType.DMA((slots,)),
    ]
    shape = jax.ShapeDtypeStruct((tracers, levels, rows, wide), f32)
    params = pltpu.CompilerParams(vmem_limit_bytes=LIMIT * MIB)
    part = pl.pallas_call(
        functools.partial(final_inner_kernel, levels),
        out_shape=shape,
        in_specs=[SMEM] + [VMEM] * 5,
        out_specs=HBM,
        scratch_shapes=scratch,
        compiler_params=params,
        cost_estimate=COST,
    )(odd, pair, other, field, courant, mask)
    return pl.pallas_call(
        functools.partial(final_edge_kernel, levels),
        out_shape=shape,
        in_specs=[SMEM] + [VMEM] * 7 + [HBM],
        out_specs=HBM,
        scratch_shapes=scratch,
        input_output_aliases={8: 0},
        compiler_params=params,
    )(odd, pair, other, field, courant, mask, near, far, part)


def weights(inverse, high):
    rows, levels, _ = inverse.shape
    turned = jnp.swapaxes(inverse, 1, 2)
    pad = ((0, 0), (0, high - levels), (0, high - levels))
    whole = jnp.pad(lax.reduce_precision(turned, 8, 7), pad)
    rest = jnp.pad(turned, pad) - whole
    return jnp.concatenate(
        [jnp.concatenate([whole, whole], 2), jnp.concatenate([rest, rest], 2)], 1
    ).astype(jnp.bfloat16)


def exchange(near, far, pair, other):
    lat = lax.axis_size("lat")
    lon = lax.axis_size("lon")
    next_pair = [(i, i + 1 if i % 2 else i - 1) for i in range(1, lat - 1)]
    other = lax.ppermute(other, "lon", [(i, (i + 1 if i % 2 else i - 1) % lon) for i in range(lon)])
    pair = lax.ppermute(pair, "lon", [(i, i ^ 1) for i in range(lon)])
    far = lax.ppermute(far, "lat", next_pair)
    near = lax.ppermute(near, "lat", [(i, i ^ 1) for i in range(lat)])
    return near, far, pair, other


def local(terminal, courant, inverse, land_mask, obs_values, obs_owner, obs_cell):
    devices = lax.axis_size("lat") * lax.axis_size("lon")
    tracers, rows, levels, wide = terminal.shape
    high = padded_levels(levels)
    odd = jnp.stack([lax.axis_index("lat") % 2, lax.axis_index("lon") % 2]).astype(jnp.int32)
    send = pack(obs_owner, obs_cell, obs_values, levels, high, wide // LANES, devices)
    got = lax.all_to_all(send, ("lat", "lon"), split_axis=0, concat_axis=0, tiled=True)
    inputs = prepare(terminal, courant)
    weight = weights(inverse, high)
    field, *edges, courant = start(odd, got, weight, inputs, tracers, high, devices)
    for _ in range(STEPS - 1):
        field, *edges = step(levels, odd, field, courant, land_mask, weight, exchange(*edges))
    out = last_step(levels, odd, field, courant, land_mask, exchange(*edges))
    return jnp.swapaxes(out, 1, 2)


def solution(mesh):
    placed = (
        P(None, "lat", None, "lon"),
        P(None, "lat", None, "lon"),
        P("lat", None, None),
        P("lat", "lon"),
        P(("lat", "lon"), None),
        P(("lat", "lon"), None),
        P(("lat", "lon")),
    )
    return jax.shard_map(
        local, mesh=mesh, in_specs=placed, out_specs=P(None, "lat", None, "lon"), check_vma=False
    )
```

```python
import functools

import jax
import jax.numpy as jnp
from jax import lax
from jax.experimental import pallas as pl
from jax.experimental.pallas import tpu as pltpu
from jax.sharding import PartitionSpec as P

STEPS = 2
LANES = 128
SLOTS = 33
BANKS = 4
MIB = 1 << 20


def padded_levels(levels):
    return -(-levels // 8) * 8


SPARE = 10
LIMIT = 24
VMEM = pl.BlockSpec(memory_space=pltpu.VMEM)
SMEM = pl.BlockSpec(memory_space=pltpu.SMEM)
HBM = pl.BlockSpec(memory_space=pltpu.HBM)


def pack_kernel(geometry, owner_hbm, cell_hbm, values_hbm, send_ref, slot_ref, owner_ref, cell_ref, values_ref, slots, pay, sems):
    levels, high, columns, devices = geometry
    per_row = levels * columns
    chunks = owner_ref.shape[0]
    f32, bf16 = jnp.float32, jnp.bfloat16
    get_owner = pltpu.make_async_copy(owner_hbm, owner_ref, sems.at[0])
    get_cell = pltpu.make_async_copy(cell_hbm, cell_ref, sems.at[1])
    get_values = pltpu.make_async_copy(values_hbm, values_ref, sems.at[2])
    get_owner.start()
    get_cell.start()
    get_values.start()
    sub = lax.broadcasted_iota(jnp.int32, (LANES, LANES), 0)
    lane = lax.broadcasted_iota(jnp.int32, (LANES, LANES), 1)
    before = jnp.concatenate(
        [jnp.where(sub < lane, 1.0, 0.0), jnp.ones((LANES, LANES), f32)], axis=1
    ).astype(bf16)
    get_owner.wait()
    get_cell.wait()
    cells = cell_ref[...]
    tile_row = ((cells >> 4) * 5243) >> 17
    rest = cells - tile_row * per_row
    level = rest >> 2
    column = rest & 3
    place = (tile_row * columns + column) * high + level
    upper, lower = (place >> 6).astype(f32), (place & 63).astype(f32)
    carry = jnp.zeros((LANES, LANES), f32)
    total = jnp.zeros((LANES, LANES), f32)
    for i in range(chunks):
        own = owner_ref[i : i + 1, :]
        hot = jnp.where(sub == own, 1.0, 0.0)
        hot16 = hot.astype(bf16)
        counted = jnp.dot(hot16, before, preferred_element_type=f32)
        rank = jnp.sum(hot * (counted[:, :LANES] + carry), axis=0, keepdims=True)
        carry = carry + counted[:, LANES:]
        rank_i = rank.astype(jnp.int32)
        slots[i : i + 1, :] = own * SLOTS + rank_i
        near_sub = sub[:64]
        parts = jnp.where(
            near_sub == rank_i,
            jnp.broadcast_to(upper[i : i + 1, :], (64, LANES)),
            jnp.where(near_sub == rank_i + 32, jnp.broadcast_to(lower[i : i + 1, :], (64, LANES)), 0.0),
        )
        parts = jnp.concatenate([parts, jnp.zeros_like(parts)], axis=0).astype(bf16)
        total = total + lax.dot_general(
            hot16, parts, (((1,), (1,)), ((), ())), preferred_element_type=f32
        )
    copy = pltpu.make_async_copy(slots, slot_ref, sems.at[3])
    copy.start()
    places = total * 64.0 + pltpu.roll(total, LANES - 32, 1)
    dump = f32(2 * 8 * columns * high)
    pay[...] = jnp.where(
        lane < 32, jnp.where(lane.astype(f32) < carry, places, dump), carry
    )
    for o in range(devices):
        send_ref[o * SLOTS + 32] = pay[o : o + 1, :]
    get_values.wait()
    copy.wait()
    unroll = 64
    for i in range(chunks):

        @pl.loop(0, LANES // unroll)
        def _(c):
            base = c * unroll
            for u in range(unroll):
                send_ref[slot_ref[i, base + u]] = values_ref[i * LANES + base + u]


def pack(owner, cell, values, levels, high, columns, devices):
    rows = values.shape[0]
    chunks = rows // LANES
    return pl.pallas_call(
        functools.partial(pack_kernel, (levels, high, columns, devices)),
        out_shape=jax.ShapeDtypeStruct((devices * SLOTS, 1, LANES), jnp.float32),
        in_specs=[HBM] * 3,
        out_specs=VMEM,
        scratch_shapes=[
            pltpu.SMEM((chunks, LANES), jnp.int32),
            pltpu.VMEM((chunks, LANES), jnp.int32),
            pltpu.VMEM((chunks, LANES), jnp.int32),
            pltpu.VMEM((rows, 1, LANES), jnp.float32),
            pltpu.VMEM((chunks, LANES), jnp.int32),
            pltpu.VMEM((LANES, LANES), jnp.float32),
            pltpu.SemaphoreType.DMA((4,)),
        ],
        compiler_params=pltpu.CompilerParams(vmem_limit_bytes=60 * MIB),
    )(owner.reshape(chunks, LANES), cell.reshape(chunks, LANES), values.reshape(rows, 1, LANES))


def vertical(weight, cells):
    high = cells.shape[0]
    whole = cells.astype(jnp.bfloat16).astype(jnp.float32)
    both = jnp.concatenate([whole, cells - whole], axis=0).astype(jnp.bfloat16)
    product = jnp.dot(weight, both, preferred_element_type=jnp.float32)
    return product[:high] + product[high:]


def collect_ends(rows_done, field, before):
    tracers, rows, high, wide = field.shape
    lane = lax.broadcasted_iota(jnp.int32, (8, LANES), 1)
    for at in range(0, high, 8):
        strip = slice(at, at + 8)
        west, east = before(strip)
        for t in range(tracers):
            for j in rows_done:
                row = t * rows + j
                first = pltpu.roll(field[t, j, strip, :LANES], row, 1)
                last = pltpu.roll(field[t, j, strip, wide - LANES :], (row + 1) % LANES, 1)
                west = jnp.where(lane == row, first, west)
                east = jnp.where(lane == row, last, east)
        yield strip, west, east


def no_ends(strip):
    return jnp.zeros((8, LANES), jnp.float32), jnp.zeros((8, LANES), jnp.float32)


def hand_out(odd_ref, field, rows_done, before, near_ref, far_ref, pair_ref, other_ref):
    odd_lon = odd_ref[1] != 0
    for strip, west, east in collect_ends(rows_done, field, before):
        pair_ref[strip, :] = jnp.where(odd_lon, west, east)
        other_ref[strip, :] = jnp.where(odd_lon, east, west)
    last = field.shape[1] - 1
    odd = odd_ref[0]

    @pl.when(odd == 0)
    def _():
        near_ref[...] = field[:, last]
        far_ref[...] = field[:, 0]

    @pl.when(odd != 0)
    def _():
        near_ref[...] = field[:, 0]
        far_ref[...] = field[:, last]


def prepare_kernel(terminal_in, courant_in, out, stage, sems):
    moves = []
    for source in (terminal_in, courant_in):
        for part in range(source.shape[0]):
            at = len(moves) // out.shape[1]
            for j in range(out.shape[1]):
                sem = sems.at[len(moves)]
                load = pltpu.make_async_copy(source.at[part, :, j, :], stage.at[at, j], sem)
                moves.append((load, pltpu.make_async_copy(stage.at[at, j], out.at[at, j], sem)))
                load.start()
    for load, save in moves:
        load.wait()
        save.start()
    for load, save in moves:
        save.wait()


def prepare(terminal, courant):
    _, rows, levels, wide = terminal.shape
    parts = terminal.shape[0] + courant.shape[0]
    return pl.pallas_call(
        prepare_kernel,
        out_shape=jax.ShapeDtypeStruct((parts + SPARE, rows, levels, wide), terminal.dtype),
        in_specs=[HBM] * 2,
        out_specs=HBM,
        scratch_shapes=[
            pltpu.VMEM((parts, rows, levels, wide), terminal.dtype),
            pltpu.SemaphoreType.DMA((parts * rows,)),
        ],
        compiler_params=pltpu.CompilerParams(vmem_limit_bytes=60 * MIB),
    )(jnp.swapaxes(terminal, 1, 2), jnp.swapaxes(courant, 1, 2))


def start_kernel(devices, odd_ref, got_ref, weight_hbm, inputs_hbm, out_ref, near_ref, far_ref, pair_ref, other_ref, courant_ref,
                 terminal_ref, weight_ref, addr_v, addr_s, state, sems, *banks):
    tracers, rows, levels, wide = terminal_ref.shape
    columns = wide // LANES
    get_terminal = pltpu.make_async_copy(inputs_hbm.at[pl.ds(0, terminal_ref.shape[0])], terminal_ref, sems.at[1])
    get_weight = pltpu.make_async_copy(weight_hbm, weight_ref, sems.at[2])
    tracers, parts = terminal_ref.shape[0], courant_ref.shape[0]
    get_courant = pltpu.make_async_copy(inputs_hbm.at[pl.ds(tracers, parts)], courant_ref, sems.at[3])
    get_terminal.start()
    get_weight.start()
    get_courant.start()
    high = state.shape[1]
    whole = levels // 8 * 8
    for o in range(devices):
        addr_v[o : o + 1, :] = got_ref[o * SLOTS + 32].astype(jnp.int32)
    copy = pltpu.make_async_copy(addr_v, addr_s, sems.at[0])
    copy.start()
    clear = 64
    for bank in banks:

        @pl.loop(0, bank.shape[0] // clear)
        def _(i):
            bank[pl.ds(pl.multiple_of(i * clear, clear), clear), :] = jnp.zeros((clear, LANES), jnp.float32)

    copy.wait()

    @pl.loop(0, devices // BANKS)
    def _(group):
        first = group * BANKS
        most = addr_s[first, 32]
        for b in range(1, BANKS):
            most = jnp.maximum(most, addr_s[first + b, 32])

        @pl.loop(0, (most + 7) // 8)
        def _(c):
            for u in range(8):
                for b, bank in enumerate(banks):
                    place = addr_s[first + b, c * 8 + u]
                    bank[pl.ds(place, 1), :] += got_ref[(first + b) * SLOTS + c * 8 + u]

    for slot in range(state.shape[0]):
        state[slot, levels:high, :] = jnp.zeros((high - levels, wide), jnp.float32)
    get_terminal.wait()
    get_weight.wait()
    for j in range(rows):
        weight = weight_ref[j]
        for t in range(tracers):
            slot = (j * tracers + t) % state.shape[0]
            for c in range(columns):
                tile = slice(c * LANES, (c + 1) * LANES)
                base = ((t * rows + j) * columns + c) * high
                for low, top in ((0, whole), (whole, levels)):
                    total = terminal_ref[t, j, low:top, tile]
                    for bank in banks:
                        total = total + bank[base + low : base + top, :]
                    state[slot, low:top, tile] = total
            for at in range(0, wide, 2 * LANES):
                out_ref[t, j, :, at : at + 2 * LANES] = vertical(weight, state[slot, :, at : at + 2 * LANES])
    hand_out(odd_ref, out_ref, range(rows), no_ends, near_ref, far_ref, pair_ref, other_ref)
    get_courant.wait()


def shapes_of(tracers, rows, high, wide):
    f32 = jnp.float32
    edge = jax.ShapeDtypeStruct((tracers, high, wide), f32)
    end = jax.ShapeDtypeStruct((high, LANES), f32)
    return jax.ShapeDtypeStruct((tracers, rows, high, wide), f32), edge, edge, end, end


def start(odd, got, weight, inputs, tracers, high, devices):
    f32 = jnp.float32
    parts, rows, levels, wide = inputs.shape
    places = tracers * rows * (wide // LANES) * high
    return pl.pallas_call(
        functools.partial(start_kernel, devices),
        out_shape=shapes_of(tracers, rows, high, wide)
        + (jax.ShapeDtypeStruct((parts - SPARE - tracers, rows, levels, wide), f32),),
        in_specs=[SMEM, VMEM, HBM, HBM],
        out_specs=(VMEM,) * 6,
        scratch_shapes=[
            pltpu.VMEM((tracers, rows, levels, wide), f32),
            pltpu.VMEM(weight.shape, weight.dtype),
            pltpu.VMEM((devices, LANES), jnp.int32),
            pltpu.SMEM((devices, LANES), jnp.int32),
            pltpu.VMEM((2, high, wide), f32),
            pltpu.SemaphoreType.DMA((4,)),
        ]
        + [pltpu.VMEM((places + 64, LANES), f32) for _ in range(BANKS)],
        compiler_params=pltpu.CompilerParams(vmem_limit_bytes=36 * MIB),
    )(odd, got, weight, inputs)


def ends_in_place(odd_ref, pair_ref, other_ref, west, east):
    odd = odd_ref[1] != 0
    pair, other = pair_ref[...], other_ref[...]
    west[...] = jnp.where(odd, pair, other)
    east[...] = jnp.where(odd, other, pair)


def transported(t, j, levels, field, courant_ref, mask, lat, west, east, store):
    rows, wide = field.shape[1], field.shape[3]
    row = t * rows + j
    tiles = [slice(c * LANES, (c + 1) * LANES) for c in range(wide // LANES)]
    for at in range(0, levels, 8):
        count = min(8, levels - at)
        strip = slice(at, at + count)
        lane = lax.broadcasted_iota(jnp.int32, (count, LANES), 1)
        here = [field[t, j, strip, tile] for tile in tiles]
        left = [pltpu.roll(x, LANES - 1, 1) for x in here]
        left.append(pltpu.roll(east[strip, :], LANES - 1 - row, 1))
        right = [pltpu.roll(west[strip, :], (LANES - row) % LANES, 1)]
        right += [pltpu.roll(x, 1, 1) for x in here]
        for c, tile in enumerate(tiles):
            v = here[c]
            e = jnp.where(lane == LANES - 1, left[c + 1], left[c])
            w = jnp.where(lane == 0, right[c], right[c + 1])
            n = lat[0](t, strip, tile) if j == rows - 1 else field[t, j + 1, strip, tile]
            s = lat[1](t, strip, tile) if j == 0 else field[t, j - 1, strip, tile]
            moved = (
                v
                + courant_ref[0, j, strip, tile] * (e - v)
                + courant_ref[1, j, strip, tile] * (w - v)
                + courant_ref[2, j, strip, tile] * (n - v)
                + courant_ref[3, j, strip, tile] * (s - v)
            )
            store(strip, tile, mask[c] * moved)


def mask_row(mask_ref, j):
    wide = mask_ref.shape[1]
    return [mask_ref[j : j + 1, c : c + LANES].astype(jnp.float32) for c in range(0, wide, LANES)]


def by_side(odd_ref, near_ref, far_ref):
    odd = odd_ref[0] != 0
    north = lambda t, strip, tile: jnp.where(odd, far_ref[t, strip, tile], near_ref[t, strip, tile])
    south = lambda t, strip, tile: jnp.where(odd, near_ref[t, strip, tile], far_ref[t, strip, tile])
    return north, south


def advance(rows_done, levels, lat, field, courant_ref, mask_ref, hw, he, weight_ref, out_ref, state):
    tracers, rows, high, wide = field.shape
    for slot in range(state.shape[0]):
        state[slot, levels:high, :] = jnp.zeros((high - levels, wide), jnp.float32)
    for j in rows_done:
        mask = mask_row(mask_ref, j)
        weight = weight_ref[j]
        for t in range(tracers):
            slot = (j * tracers + t) % state.shape[0]

            def store(strip, tile, value):
                state[slot, strip, tile] = value

            transported(t, j, levels, field, courant_ref, mask, lat, hw, he, store)
            for at in range(0, wide, 2 * LANES):
                level = vertical(weight, state[slot, :, at : at + 2 * LANES])
                out_ref[t, j, :, at : at + 2 * LANES] = level


def inner_kernel(levels, odd_ref, pair_ref, other_ref, field, courant_ref, mask_ref, weight_ref,
                 out_ref, west, east, hw, he, state):
    ends_in_place(odd_ref, pair_ref, other_ref, hw, he)
    rows_done = range(1, field.shape[1] - 1)
    advance(rows_done, levels, None, field, courant_ref, mask_ref, hw, he, weight_ref, out_ref, state)
    for strip, first, last in collect_ends(rows_done, out_ref, no_ends):
        west[strip, :] = first
        east[strip, :] = last


def edge_kernel(levels, odd_ref, pair_ref, other_ref, field, courant_ref, mask_ref, weight_ref, far_in, near_in,
                part_ref, west, east, out_ref, near_ref, far_ref, pair_out, other_out, hw, he, state):
    ends_in_place(odd_ref, pair_ref, other_ref, hw, he)
    rows_done = (0, field.shape[1] - 1)
    lat = by_side(odd_ref, near_in, far_in)
    advance(rows_done, levels, lat, field, courant_ref, mask_ref, hw, he, weight_ref, out_ref, state)
    before = lambda strip: (west[strip, :], east[strip, :])
    hand_out(odd_ref, out_ref, rows_done, before, near_ref, far_ref, pair_out, other_out)


COST = pl.CostEstimate(flops=30_000_000_000, bytes_accessed=8_000_000, transcendentals=0)


def step(levels, odd, field, courant, mask, weight, halos):
    f32 = jnp.float32
    near, far, pair, other = halos
    tracers, rows, high, wide = field.shape
    field_shape, edge, _, end, _ = shapes_of(tracers, rows, high, wide)
    scratch = [pltpu.VMEM((high, LANES), f32)] * 2 + [pltpu.VMEM((2, high, wide), f32)]
    params = pltpu.CompilerParams(vmem_limit_bytes=LIMIT * MIB)
    part, west, east = pl.pallas_call(
        functools.partial(inner_kernel, levels),
        out_shape=(field_shape, end, end),
        in_specs=[SMEM] + [VMEM] * 6,
        out_specs=(VMEM,) * 3,
        scratch_shapes=scratch,
        compiler_params=params,
        cost_estimate=COST,
    )(odd, pair, other, field, courant, mask, weight)
    return pl.pallas_call(
        functools.partial(edge_kernel, levels),
        out_shape=(field_shape, edge, edge, end, end),
        in_specs=[SMEM] + [VMEM] * 11,
        out_specs=(VMEM,) * 5,
        scratch_shapes=scratch,
        input_output_aliases={9: 0},
        compiler_params=params,
    )(odd, pair, other, field, courant, mask, weight, far, near, part, west, east)


def finish(rows_done, levels, lat, field, courant_ref, mask_ref, hw, he, out_ref, state, sems):
    tracers = field.shape[0]
    slots = state.shape[0]
    flying = {}
    for k, (j, t) in enumerate((j, t) for j in rows_done for t in range(tracers)):
        slot = k % slots
        if slot in flying:
            flying.pop(slot).wait()

        def store(strip, tile, value):
            state[slot, strip, tile] = value

        transported(t, j, levels, field, courant_ref, mask_row(mask_ref, j), lat, hw, he, store)
        copy = pltpu.make_async_copy(state.at[slot], out_ref.at[t, :, j, :], sems.at[slot])
        copy.start()
        flying[slot] = copy
    for copy in flying.values():
        copy.wait()


def final_inner_kernel(levels, odd_ref, pair_ref, other_ref, field, courant_ref, mask_ref, out_ref, hw, he, state, sems):
    ends_in_place(odd_ref, pair_ref, other_ref, hw, he)
    rows_done = range(1, field.shape[1] - 1)
    finish(rows_done, levels, None, field, courant_ref, mask_ref, hw, he, out_ref, state, sems)


def final_edge_kernel(levels, odd_ref, pair_ref, other_ref, field, courant_ref, mask_ref, far_in, near_in, part_ref,
                      out_ref, hw, he, state, sems):
    ends_in_place(odd_ref, pair_ref, other_ref, hw, he)
    lat = by_side(odd_ref, near_in, far_in)
    finish((0, field.shape[1] - 1), levels, lat, field, courant_ref, mask_ref, hw, he, out_ref, state, sems)


def last_step(levels, odd, field, courant, mask, halos):
    f32 = jnp.float32
    near, far, pair, other = halos
    tracers, rows, high, wide = field.shape
    slots = 12
    scratch = [pltpu.VMEM((high, LANES), f32)] * 2 + [
        pltpu.VMEM((slots, levels, wide), f32),
        pltpu.SemaphoreType.DMA((slots,)),
    ]
    shape = jax.ShapeDtypeStruct((tracers, levels, rows, wide), f32)
    params = pltpu.CompilerParams(vmem_limit_bytes=LIMIT * MIB)
    part = pl.pallas_call(
        functools.partial(final_inner_kernel, levels),
        out_shape=shape,
        in_specs=[SMEM] + [VMEM] * 5,
        out_specs=HBM,
        scratch_shapes=scratch,
        compiler_params=params,
        cost_estimate=COST,
    )(odd, pair, other, field, courant, mask)
    return pl.pallas_call(
        functools.partial(final_edge_kernel, levels),
        out_shape=shape,
        in_specs=[SMEM] + [VMEM] * 7 + [HBM],
        out_specs=HBM,
        scratch_shapes=scratch,
        input_output_aliases={8: 0},
        compiler_params=params,
    )(odd, pair, other, field, courant, mask, far, near, part)


def weights(inverse, high):
    rows, levels, _ = inverse.shape
    turned = jnp.swapaxes(inverse, 1, 2)
    pad = ((0, 0), (0, high - levels), (0, high - levels))
    whole = jnp.pad(lax.reduce_precision(turned, 8, 7), pad)
    rest = jnp.pad(turned, pad) - whole
    return jnp.concatenate(
        [jnp.concatenate([whole, whole], 2), jnp.concatenate([rest, rest], 2)], 1
    ).astype(jnp.bfloat16)


def exchange(near, far, pair, other):
    lat = lax.axis_size("lat")
    lon = lax.axis_size("lon")
    next_pair = [(i, i + 1 if i % 2 else i - 1) for i in range(1, lat - 1)]
    other = lax.ppermute(other, "lon", [(i, (i + 1 if i % 2 else i - 1) % lon) for i in range(lon)])
    pair = lax.ppermute(pair, "lon", [(i, i ^ 1) for i in range(lon)])
    far = lax.ppermute(far, "lat", next_pair)
    near = lax.ppermute(near, "lat", [(i, i ^ 1) for i in range(lat)])
    return near, far, pair, other


def local(terminal, courant, inverse, land_mask, obs_values, obs_owner, obs_cell):
    devices = lax.axis_size("lat") * lax.axis_size("lon")
    tracers, rows, levels, wide = terminal.shape
    high = padded_levels(levels)
    odd = jnp.stack([lax.axis_index("lat") % 2, lax.axis_index("lon") % 2]).astype(jnp.int32)
    send = pack(obs_owner, obs_cell, obs_values, levels, high, wide // LANES, devices)
    got = lax.all_to_all(send, ("lat", "lon"), split_axis=0, concat_axis=0, tiled=True)
    inputs = prepare(terminal, courant)
    weight = weights(inverse, high)
    field, *edges, courant = start(odd, got, weight, inputs, tracers, high, devices)
    for _ in range(STEPS - 1):
        field, *edges = step(levels, odd, field, courant, land_mask, weight, exchange(*edges))
    out = last_step(levels, odd, field, courant, land_mask, exchange(*edges))
    return jnp.swapaxes(out, 1, 2)


def solution(mesh):
    placed = (
        P(None, "lat", None, "lon"),
        P(None, "lat", None, "lon"),
        P("lat", None, None),
        P("lat", "lon"),
        P(("lat", "lon"), None),
        P(("lat", "lon"), None),
        P(("lat", "lon")),
    )
    return jax.shard_map(
        local, mesh=mesh, in_specs=placed, out_specs=P(None, "lat", None, "lon"), check_vma=False
    )
```

```python
import functools

import jax
import jax.numpy as jnp
from jax import lax
from jax.experimental import pallas as pl
from jax.experimental.pallas import tpu as pltpu
from jax.sharding import PartitionSpec as P

STEPS = 2
LANES = 128
SLOTS = 33
BANKS = 4
MIB = 1 << 20


def padded_levels(levels):
    return -(-levels // 8) * 8


SPARE = 10
LIMIT = 24
VMEM = pl.BlockSpec(memory_space=pltpu.VMEM)
SMEM = pl.BlockSpec(memory_space=pltpu.SMEM)
HBM = pl.BlockSpec(memory_space=pltpu.HBM)


def pack_kernel(geometry, owner_hbm, cell_hbm, values_hbm, send_ref, slot_ref, owner_ref, cell_ref, values_ref, slots, pay, sems):
    levels, high, columns, devices = geometry
    per_row = levels * columns
    chunks = owner_ref.shape[0]
    f32, bf16 = jnp.float32, jnp.bfloat16
    get_owner = pltpu.make_async_copy(owner_hbm, owner_ref, sems.at[0])
    get_cell = pltpu.make_async_copy(cell_hbm, cell_ref, sems.at[1])
    get_values = pltpu.make_async_copy(values_hbm, values_ref, sems.at[2])
    get_owner.start()
    get_cell.start()
    get_values.start()
    sub = lax.broadcasted_iota(jnp.int32, (LANES, LANES), 0)
    lane = lax.broadcasted_iota(jnp.int32, (LANES, LANES), 1)
    before = jnp.concatenate(
        [jnp.where(sub < lane, 1.0, 0.0), jnp.ones((LANES, LANES), f32)], axis=1
    ).astype(bf16)
    get_owner.wait()
    get_cell.wait()
    cells = cell_ref[...]
    tile_row = ((cells >> 4) * 5243) >> 17
    rest = cells - tile_row * per_row
    level = rest >> 2
    column = rest & 3
    place = (tile_row * columns + column) * high + level
    upper, lower = (place >> 6).astype(f32), (place & 63).astype(f32)
    carry = jnp.zeros((LANES, LANES), f32)
    total = jnp.zeros((LANES, LANES), f32)
    for i in range(chunks):
        own = owner_ref[i : i + 1, :]
        hot = jnp.where(sub == own, 1.0, 0.0)
        hot16 = hot.astype(bf16)
        counted = jnp.dot(hot16, before, preferred_element_type=f32)
        rank = jnp.sum(hot * (counted[:, :LANES] + carry), axis=0, keepdims=True)
        carry = carry + counted[:, LANES:]
        rank_i = rank.astype(jnp.int32)
        slots[i : i + 1, :] = own * SLOTS + rank_i
        near_sub = sub[:64]
        parts = jnp.where(
            near_sub == rank_i,
            jnp.broadcast_to(upper[i : i + 1, :], (64, LANES)),
            jnp.where(near_sub == rank_i + 32, jnp.broadcast_to(lower[i : i + 1, :], (64, LANES)), 0.0),
        )
        parts = jnp.concatenate([parts, jnp.zeros_like(parts)], axis=0).astype(bf16)
        total = total + lax.dot_general(
            hot16, parts, (((1,), (1,)), ((), ())), preferred_element_type=f32
        )
    copy = pltpu.make_async_copy(slots, slot_ref, sems.at[3])
    copy.start()
    places = total * 64.0 + pltpu.roll(total, LANES - 32, 1)
    dump = f32(2 * 8 * columns * high)
    pay[...] = jnp.where(
        lane < 32, jnp.where(lane.astype(f32) < carry, places, dump), carry
    )
    for o in range(devices):
        send_ref[o * SLOTS + 32] = pay[o : o + 1, :]
    get_values.wait()
    copy.wait()
    unroll = 64
    for i in range(chunks):

        @pl.loop(0, LANES // unroll)
        def _(c):
            base = c * unroll
            for u in range(unroll):
                send_ref[slot_ref[i, base + u]] = values_ref[i * LANES + base + u]


def pack(owner, cell, values, levels, high, columns, devices):
    rows = values.shape[0]
    chunks = rows // LANES
    return pl.pallas_call(
        functools.partial(pack_kernel, (levels, high, columns, devices)),
        out_shape=jax.ShapeDtypeStruct((devices * SLOTS, 1, LANES), jnp.float32),
        in_specs=[HBM] * 3,
        out_specs=VMEM,
        scratch_shapes=[
            pltpu.SMEM((chunks, LANES), jnp.int32),
            pltpu.VMEM((chunks, LANES), jnp.int32),
            pltpu.VMEM((chunks, LANES), jnp.int32),
            pltpu.VMEM((rows, 1, LANES), jnp.float32),
            pltpu.VMEM((chunks, LANES), jnp.int32),
            pltpu.VMEM((LANES, LANES), jnp.float32),
            pltpu.SemaphoreType.DMA((4,)),
        ],
        compiler_params=pltpu.CompilerParams(vmem_limit_bytes=60 * MIB),
    )(owner.reshape(chunks, LANES), cell.reshape(chunks, LANES), values.reshape(rows, 1, LANES))


def vertical(weight, cells):
    high = cells.shape[0]
    whole = cells.astype(jnp.bfloat16).astype(jnp.float32)
    both = jnp.concatenate([whole, cells - whole], axis=0).astype(jnp.bfloat16)
    product = jnp.dot(weight, both, preferred_element_type=jnp.float32)
    return product[:high] + product[high:]


def collect_ends(rows_done, field, before):
    tracers, rows, high, wide = field.shape
    lane = lax.broadcasted_iota(jnp.int32, (8, LANES), 1)
    for at in range(0, high, 8):
        strip = slice(at, at + 8)
        west, east = before(strip)
        for t in range(tracers):
            for j in rows_done:
                row = t * rows + j
                first = pltpu.roll(field[t, j, strip, :LANES], row, 1)
                last = pltpu.roll(field[t, j, strip, wide - LANES :], (row + 1) % LANES, 1)
                west = jnp.where(lane == row, first, west)
                east = jnp.where(lane == row, last, east)
        yield strip, west, east


def no_ends(strip):
    return jnp.zeros((8, LANES), jnp.float32), jnp.zeros((8, LANES), jnp.float32)


def hand_out(odd_ref, field, rows_done, before, near_ref, far_ref, pair_ref, other_ref):
    odd_lon = odd_ref[1] != 0
    for strip, west, east in collect_ends(rows_done, field, before):
        pair_ref[strip, :] = jnp.where(odd_lon, west, east)
        other_ref[strip, :] = jnp.where(odd_lon, east, west)
    last = field.shape[1] - 1
    odd = odd_ref[0]

    @pl.when(odd == 0)
    def _():
        near_ref[...] = field[:, last]
        far_ref[...] = field[:, 0]

    @pl.when(odd != 0)
    def _():
        near_ref[...] = field[:, 0]
        far_ref[...] = field[:, last]


def prepare_kernel(terminal_in, courant_in, out, stage, sems):
    moves = []
    for source in (terminal_in, courant_in):
        for part in range(source.shape[0]):
            at = len(moves) // out.shape[1]
            for j in range(out.shape[1]):
                sem = sems.at[len(moves)]
                load = pltpu.make_async_copy(source.at[part, :, j, :], stage.at[at, j], sem)
                moves.append((load, pltpu.make_async_copy(stage.at[at, j], out.at[at, j], sem)))
                load.start()
    for load, save in moves:
        load.wait()
        save.start()
    for load, save in moves:
        save.wait()


def prepare(terminal, courant):
    _, rows, levels, wide = terminal.shape
    parts = terminal.shape[0] + courant.shape[0]
    return pl.pallas_call(
        prepare_kernel,
        out_shape=jax.ShapeDtypeStruct((parts + SPARE, rows, levels, wide), terminal.dtype),
        in_specs=[HBM] * 2,
        out_specs=HBM,
        scratch_shapes=[
            pltpu.VMEM((parts, rows, levels, wide), terminal.dtype),
            pltpu.SemaphoreType.DMA((parts * rows,)),
        ],
        compiler_params=pltpu.CompilerParams(vmem_limit_bytes=60 * MIB),
    )(jnp.swapaxes(terminal, 1, 2), jnp.swapaxes(courant, 1, 2))


def start_kernel(devices, odd_ref, got_ref, weight_hbm, inputs_hbm, out_ref, near_ref, far_ref, pair_ref, other_ref, courant_ref,
                 terminal_ref, weight_ref, addr_v, addr_s, state, sems, *banks):
    tracers, rows, levels, wide = terminal_ref.shape
    columns = wide // LANES
    get_terminal = pltpu.make_async_copy(inputs_hbm.at[pl.ds(0, terminal_ref.shape[0])], terminal_ref, sems.at[1])
    get_weight = pltpu.make_async_copy(weight_hbm, weight_ref, sems.at[2])
    tracers, parts = terminal_ref.shape[0], courant_ref.shape[0]
    get_courant = pltpu.make_async_copy(inputs_hbm.at[pl.ds(tracers, parts)], courant_ref, sems.at[3])
    get_terminal.start()
    get_weight.start()
    get_courant.start()
    high = state.shape[1]
    whole = levels // 8 * 8
    for o in range(devices):
        addr_v[o : o + 1, :] = got_ref[o * SLOTS + 32].astype(jnp.int32)
    copy = pltpu.make_async_copy(addr_v, addr_s, sems.at[0])
    copy.start()
    clear = 64
    for bank in banks:

        @pl.loop(0, bank.shape[0] // clear)
        def _(i):
            bank[pl.ds(pl.multiple_of(i * clear, clear), clear), :] = jnp.zeros((clear, LANES), jnp.float32)

    copy.wait()

    @pl.loop(0, devices // BANKS)
    def _(group):
        first = group * BANKS
        most = addr_s[first, 32]
        for b in range(1, BANKS):
            most = jnp.maximum(most, addr_s[first + b, 32])

        @pl.loop(0, (most + 7) // 8)
        def _(c):
            for u in range(8):
                for b, bank in enumerate(banks):
                    place = addr_s[first + b, c * 8 + u]
                    bank[pl.ds(place, 1), :] += got_ref[(first + b) * SLOTS + c * 8 + u]

    for slot in range(state.shape[0]):
        state[slot, levels:high, :] = jnp.zeros((high - levels, wide), jnp.float32)
    get_terminal.wait()
    get_weight.wait()
    for j in range(rows):
        weight = weight_ref[j]
        for t in range(tracers):
            slot = (j * tracers + t) % state.shape[0]
            for c in range(columns):
                tile = slice(c * LANES, (c + 1) * LANES)
                base = ((t * rows + j) * columns + c) * high
                for low, top in ((0, whole), (whole, levels)):
                    total = terminal_ref[t, j, low:top, tile]
                    for bank in banks:
                        total = total + bank[base + low : base + top, :]
                    state[slot, low:top, tile] = total
            for at in range(0, wide, 2 * LANES):
                out_ref[t, j, :, at : at + 2 * LANES] = vertical(weight, state[slot, :, at : at + 2 * LANES])
    hand_out(odd_ref, out_ref, range(rows), no_ends, near_ref, far_ref, pair_ref, other_ref)
    get_courant.wait()


def shapes_of(tracers, rows, high, wide):
    f32 = jnp.float32
    edge = jax.ShapeDtypeStruct((tracers, high, wide), f32)
    end = jax.ShapeDtypeStruct((high, LANES), f32)
    return jax.ShapeDtypeStruct((tracers, rows, high, wide), f32), edge, edge, end, end


def start(odd, got, weight, inputs, tracers, high, devices):
    f32 = jnp.float32
    parts, rows, levels, wide = inputs.shape
    places = tracers * rows * (wide // LANES) * high
    return pl.pallas_call(
        functools.partial(start_kernel, devices),
        out_shape=shapes_of(tracers, rows, high, wide)
        + (jax.ShapeDtypeStruct((parts - SPARE - tracers, rows, levels, wide), f32),),
        in_specs=[SMEM, VMEM, HBM, HBM],
        out_specs=(VMEM,) * 6,
        scratch_shapes=[
            pltpu.VMEM((tracers, rows, levels, wide), f32),
            pltpu.VMEM(weight.shape, weight.dtype),
            pltpu.VMEM((devices, LANES), jnp.int32),
            pltpu.SMEM((devices, LANES), jnp.int32),
            pltpu.VMEM((2, high, wide), f32),
            pltpu.SemaphoreType.DMA((4,)),
        ]
        + [pltpu.VMEM((places + 64, LANES), f32) for _ in range(BANKS)],
        compiler_params=pltpu.CompilerParams(vmem_limit_bytes=36 * MIB),
    )(odd, got, weight, inputs)


def ends_in_place(odd_ref, pair_ref, other_ref, west, east):
    odd = odd_ref[1] != 0
    pair, other = pair_ref[...], other_ref[...]
    west[...] = jnp.where(odd, pair, other)
    east[...] = jnp.where(odd, other, pair)


def transported(t, j, levels, field, courant_ref, mask, lat, west, east, store):
    rows, wide = field.shape[1], field.shape[3]
    row = t * rows + j
    tiles = [slice(c * LANES, (c + 1) * LANES) for c in range(wide // LANES)]
    for at in range(0, levels, 8):
        count = min(8, levels - at)
        strip = slice(at, at + count)
        lane = lax.broadcasted_iota(jnp.int32, (count, LANES), 1)
        here = [field[t, j, strip, tile] for tile in tiles]
        left = [pltpu.roll(x, LANES - 1, 1) for x in here]
        left.append(pltpu.roll(east[strip, :], LANES - 1 - row, 1))
        right = [pltpu.roll(west[strip, :], (LANES - row) % LANES, 1)]
        right += [pltpu.roll(x, 1, 1) for x in here]
        for c, tile in enumerate(tiles):
            v = here[c]
            e = jnp.where(lane == LANES - 1, left[c + 1], left[c])
            w = jnp.where(lane == 0, right[c], right[c + 1])
            n = lat[0](t, strip, tile) if j == rows - 1 else field[t, j + 1, strip, tile]
            s = lat[1](t, strip, tile) if j == 0 else field[t, j - 1, strip, tile]
            moved = (
                v
                + courant_ref[0, j, strip, tile] * (e - v)
                + courant_ref[1, j, strip, tile] * (w - v)
                + courant_ref[2, j, strip, tile] * (n - v)
                + courant_ref[3, j, strip, tile] * (s - v)
            )
            store(strip, tile, mask[c] * moved)


def mask_row(mask_ref, j):
    wide = mask_ref.shape[1]
    return [mask_ref[j : j + 1, c : c + LANES].astype(jnp.float32) for c in range(0, wide, LANES)]


def beyond(halo_ref):
    read = lambda t, strip, tile: halo_ref[t, strip, tile]
    return read, read


def each_row(odd_ref, rows, inner, near, do):
    if inner:
        for j in range(1, rows - 1):
            do(j)
    for j in (0, rows - 1):
        pl.when((odd_ref[0] != 0) == ((j == 0) == near))(functools.partial(do, j))


def advance(levels, lat, field, courant_ref, mask_ref, hw, he, weight_ref, out_ref, state):
    tracers, rows, high, wide = field.shape
    for slot in range(state.shape[0]):
        state[slot, levels:high, :] = jnp.zeros((high - levels, wide), jnp.float32)

    def do(j):
        mask = mask_row(mask_ref, j)
        weight = weight_ref[j]
        for t in range(tracers):
            slot = (j * tracers + t) % state.shape[0]

            def store(strip, tile, value):
                state[slot, strip, tile] = value

            transported(t, j, levels, field, courant_ref, mask, lat, hw, he, store)
            for at in range(0, wide, 2 * LANES):
                out_ref[t, j, :, at : at + 2 * LANES] = vertical(weight, state[slot, :, at : at + 2 * LANES])

    return do


def inner_kernel(levels, odd_ref, pair_ref, other_ref, field, courant_ref, mask_ref, weight_ref, near_in,
                 out_ref, west, east, hw, he, state):
    ends_in_place(odd_ref, pair_ref, other_ref, hw, he)
    rows = field.shape[1]
    do = advance(levels, beyond(near_in), field, courant_ref, mask_ref, hw, he, weight_ref, out_ref, state)
    each_row(odd_ref, rows, True, True, do)
    for strip, first, last in collect_ends(range(1, rows - 1), out_ref, no_ends):
        west[strip, :] = first
        east[strip, :] = last


def edge_kernel(levels, odd_ref, pair_ref, other_ref, field, courant_ref, mask_ref, weight_ref, far_in,
                part_ref, west, east, out_ref, near_ref, far_ref, pair_out, other_out, hw, he, state):
    ends_in_place(odd_ref, pair_ref, other_ref, hw, he)
    rows = field.shape[1]
    do = advance(levels, beyond(far_in), field, courant_ref, mask_ref, hw, he, weight_ref, out_ref, state)
    each_row(odd_ref, rows, False, False, do)
    before = lambda strip: (west[strip, :], east[strip, :])
    hand_out(odd_ref, out_ref, (0, rows - 1), before, near_ref, far_ref, pair_out, other_out)


COST = pl.CostEstimate(flops=3_000_000_000, bytes_accessed=8_000_000, transcendentals=0)


def step(levels, odd, field, courant, mask, weight, halos):
    f32 = jnp.float32
    near, far, pair, other = halos
    tracers, rows, high, wide = field.shape
    field_shape, edge, _, end, _ = shapes_of(tracers, rows, high, wide)
    scratch = [pltpu.VMEM((high, LANES), f32)] * 2 + [pltpu.VMEM((2, high, wide), f32)]
    params = pltpu.CompilerParams(vmem_limit_bytes=LIMIT * MIB)
    part, west, east = pl.pallas_call(
        functools.partial(inner_kernel, levels),
        out_shape=(field_shape, end, end),
        in_specs=[SMEM] + [VMEM] * 7,
        out_specs=(VMEM,) * 3,
        scratch_shapes=scratch,
        compiler_params=params,
        cost_estimate=COST,
    )(odd, pair, other, field, courant, mask, weight, near)
    return pl.pallas_call(
        functools.partial(edge_kernel, levels),
        out_shape=(field_shape, edge, edge, end, end),
        in_specs=[SMEM] + [VMEM] * 10,
        out_specs=(VMEM,) * 5,
        scratch_shapes=scratch,
        input_output_aliases={8: 0},
        compiler_params=params,
    )(odd, pair, other, field, courant, mask, weight, far, part, west, east)


def finish(levels, lat, field, courant_ref, mask_ref, hw, he, out_ref, state, sems, flying=None):
    tracers, rows = field.shape[:2]
    slots = state.shape[0]

    def do(j):
        started = []
        for t in range(tracers):
            slot = (j * tracers + t) % slots

            def store(strip, tile, value):
                state[slot, strip, tile] = value

            transported(t, j, levels, field, courant_ref, mask_row(mask_ref, j), lat, hw, he, store)
            copy = pltpu.make_async_copy(state.at[slot], out_ref.at[t, :, j, :], sems.at[slot])
            copy.start()
            started.append(copy)
        if flying is not None and 0 < j < rows - 1:
            flying.extend(started)
        else:
            for copy in started:
                copy.wait()

    return do


def final_inner_kernel(levels, odd_ref, pair_ref, other_ref, field, courant_ref, mask_ref, near_in, out_ref, hw, he, state,
                       sems):
    ends_in_place(odd_ref, pair_ref, other_ref, hw, he)
    flying = []
    do = finish(levels, beyond(near_in), field, courant_ref, mask_ref, hw, he, out_ref, state, sems, flying)
    each_row(odd_ref, field.shape[1], True, True, do)
    for copy in flying:
        copy.wait()


def final_edge_kernel(levels, odd_ref, pair_ref, other_ref, field, courant_ref, mask_ref, far_in, part_ref,
                      out_ref, hw, he, state, sems):
    ends_in_place(odd_ref, pair_ref, other_ref, hw, he)
    do = finish(levels, beyond(far_in), field, courant_ref, mask_ref, hw, he, out_ref, state, sems)
    each_row(odd_ref, field.shape[1], False, False, do)


def last_step(levels, odd, field, courant, mask, halos):
    f32 = jnp.float32
    near, far, pair, other = halos
    tracers, rows, high, wide = field.shape
    slots = tracers * rows
    scratch = [pltpu.VMEM((high, LANES), f32)] * 2 + [
        pltpu.VMEM((slots, levels, wide), f32),
        pltpu.SemaphoreType.DMA((slots,)),
    ]
    shape = jax.ShapeDtypeStruct((tracers, levels, rows, wide), f32)
    params = pltpu.CompilerParams(vmem_limit_bytes=LIMIT * MIB)
    part = pl.pallas_call(
        functools.partial(final_inner_kernel, levels),
        out_shape=shape,
        in_specs=[SMEM] + [VMEM] * 6,
        out_specs=HBM,
        scratch_shapes=scratch,
        compiler_params=params,
        cost_estimate=COST,
    )(odd, pair, other, field, courant, mask, near)
    return pl.pallas_call(
        functools.partial(final_edge_kernel, levels),
        out_shape=shape,
        in_specs=[SMEM] + [VMEM] * 6 + [HBM],
        out_specs=HBM,
        scratch_shapes=scratch,
        input_output_aliases={7: 0},
        compiler_params=params,
    )(odd, pair, other, field, courant, mask, far, part)


def weights(inverse, high):
    rows, levels, _ = inverse.shape
    turned = jnp.swapaxes(inverse, 1, 2)
    pad = ((0, 0), (0, high - levels), (0, high - levels))
    whole = jnp.pad(lax.reduce_precision(turned, 8, 7), pad)
    rest = jnp.pad(turned, pad) - whole
    return jnp.concatenate(
        [jnp.concatenate([whole, whole], 2), jnp.concatenate([rest, rest], 2)], 1
    ).astype(jnp.bfloat16)


def exchange(near, far, pair, other):
    lat = lax.axis_size("lat")
    lon = lax.axis_size("lon")
    next_pair = [(i, i + 1 if i % 2 else i - 1) for i in range(1, lat - 1)]
    other = lax.ppermute(other, "lon", [(i, (i + 1 if i % 2 else i - 1) % lon) for i in range(lon)])
    pair = lax.ppermute(pair, "lon", [(i, i ^ 1) for i in range(lon)])
    far = lax.ppermute(far, "lat", next_pair)
    near = lax.ppermute(near, "lat", [(i, i ^ 1) for i in range(lat)])
    return near, far, pair, other


def local(terminal, courant, inverse, land_mask, obs_values, obs_owner, obs_cell):
    devices = lax.axis_size("lat") * lax.axis_size("lon")
    tracers, rows, levels, wide = terminal.shape
    high = padded_levels(levels)
    odd = jnp.stack([lax.axis_index("lat") % 2, lax.axis_index("lon") % 2]).astype(jnp.int32)
    send = pack(obs_owner, obs_cell, obs_values, levels, high, wide // LANES, devices)
    got = lax.all_to_all(send, ("lat", "lon"), split_axis=0, concat_axis=0, tiled=True)
    inputs = prepare(terminal, courant)
    weight = weights(inverse, high)
    field, *edges, courant = start(odd, got, weight, inputs, tracers, high, devices)
    for _ in range(STEPS - 1):
        field, *edges = step(levels, odd, field, courant, land_mask, weight, exchange(*edges))
    out = last_step(levels, odd, field, courant, land_mask, exchange(*edges))
    return jnp.swapaxes(out, 1, 2)


def solution(mesh):
    placed = (
        P(None, "lat", None, "lon"),
        P(None, "lat", None, "lon"),
        P("lat", None, None),
        P("lat", "lon"),
        P(("lat", "lon"), None),
        P(("lat", "lon"), None),
        P(("lat", "lon")),
    )
    return jax.shard_map(
        local, mesh=mesh, in_specs=placed, out_specs=P(None, "lat", None, "lon"), check_vma=False
    )
```

```python
import functools

import jax
import jax.numpy as jnp
from jax import lax
from jax.experimental import pallas as pl
from jax.experimental.pallas import tpu as pltpu
from jax.sharding import PartitionSpec as P

STEPS = 2
LANES = 128
SLOTS = 33
BANKS = 4
MIB = 1 << 20


def padded_levels(levels):
    return -(-levels // 8) * 8


SPARE = 10
LIMIT = 26
VMEM = pl.BlockSpec(memory_space=pltpu.VMEM)
SMEM = pl.BlockSpec(memory_space=pltpu.SMEM)
HBM = pl.BlockSpec(memory_space=pltpu.HBM)


def pack_kernel(geometry, owner_hbm, cell_hbm, values_hbm, send_ref, slot_ref, owner_ref, cell_ref, values_ref, slots, pay, sems):
    levels, high, columns, devices = geometry
    per_row = levels * columns
    chunks = owner_ref.shape[0]
    f32, bf16 = jnp.float32, jnp.bfloat16
    get_owner = pltpu.make_async_copy(owner_hbm, owner_ref, sems.at[0])
    get_cell = pltpu.make_async_copy(cell_hbm, cell_ref, sems.at[1])
    get_values = pltpu.make_async_copy(values_hbm, values_ref, sems.at[2])
    get_owner.start()
    get_cell.start()
    get_values.start()
    sub = lax.broadcasted_iota(jnp.int32, (LANES, LANES), 0)
    lane = lax.broadcasted_iota(jnp.int32, (LANES, LANES), 1)
    before = jnp.concatenate(
        [jnp.where(sub < lane, 1.0, 0.0), jnp.ones((LANES, LANES), f32)], axis=1
    ).astype(bf16)
    get_owner.wait()
    get_cell.wait()
    cells = cell_ref[...]
    tile_row = ((cells >> 4) * 5243) >> 17
    rest = cells - tile_row * per_row
    level = rest >> 2
    column = rest & 3
    place = (tile_row * columns + column) * high + level
    upper, lower = (place >> 6).astype(f32), (place & 63).astype(f32)
    carry = jnp.zeros((LANES, LANES), f32)
    total = jnp.zeros((LANES, LANES), f32)
    for i in range(chunks):
        own = owner_ref[i : i + 1, :]
        hot = jnp.where(sub == own, 1.0, 0.0)
        hot16 = hot.astype(bf16)
        counted = jnp.dot(hot16, before, preferred_element_type=f32)
        rank = jnp.sum(hot * (counted[:, :LANES] + carry), axis=0, keepdims=True)
        carry = carry + counted[:, LANES:]
        rank_i = rank.astype(jnp.int32)
        slots[i : i + 1, :] = own * SLOTS + rank_i
        near_sub = sub[:64]
        parts = jnp.where(
            near_sub == rank_i,
            jnp.broadcast_to(upper[i : i + 1, :], (64, LANES)),
            jnp.where(near_sub == rank_i + 32, jnp.broadcast_to(lower[i : i + 1, :], (64, LANES)), 0.0),
        )
        parts = jnp.concatenate([parts, jnp.zeros_like(parts)], axis=0).astype(bf16)
        total = total + lax.dot_general(
            hot16, parts, (((1,), (1,)), ((), ())), preferred_element_type=f32
        )
    copy = pltpu.make_async_copy(slots, slot_ref, sems.at[3])
    copy.start()
    places = total * 64.0 + pltpu.roll(total, LANES - 32, 1)
    dump = f32(2 * 8 * columns * high)
    pay[...] = jnp.where(
        lane < 32, jnp.where(lane.astype(f32) < carry, places, dump), carry
    )
    for o in range(devices):
        send_ref[o * SLOTS + 32] = pay[o : o + 1, :]
    get_values.wait()
    copy.wait()
    unroll = 64
    for i in range(chunks):

        @pl.loop(0, LANES // unroll)
        def _(c):
            base = c * unroll
            for u in range(unroll):
                send_ref[slot_ref[i, base + u]] = values_ref[i * LANES + base + u]


def pack(owner, cell, values, levels, high, columns, devices):
    rows = values.shape[0]
    chunks = rows // LANES
    return pl.pallas_call(
        functools.partial(pack_kernel, (levels, high, columns, devices)),
        out_shape=jax.ShapeDtypeStruct((devices * SLOTS, 1, LANES), jnp.float32),
        in_specs=[HBM] * 3,
        out_specs=VMEM,
        scratch_shapes=[
            pltpu.SMEM((chunks, LANES), jnp.int32),
            pltpu.VMEM((chunks, LANES), jnp.int32),
            pltpu.VMEM((chunks, LANES), jnp.int32),
            pltpu.VMEM((rows, 1, LANES), jnp.float32),
            pltpu.VMEM((chunks, LANES), jnp.int32),
            pltpu.VMEM((LANES, LANES), jnp.float32),
            pltpu.SemaphoreType.DMA((4,)),
        ],
        compiler_params=pltpu.CompilerParams(vmem_limit_bytes=60 * MIB),
    )(owner.reshape(chunks, LANES), cell.reshape(chunks, LANES), values.reshape(rows, 1, LANES))


def vertical(weight, cells):
    high = cells.shape[0]
    whole = cells.astype(jnp.bfloat16).astype(jnp.float32)
    both = jnp.concatenate([whole, cells - whole], axis=0).astype(jnp.bfloat16)
    product = jnp.dot(weight, both, preferred_element_type=jnp.float32)
    return product[:high] + product[high:]


def collect_ends(rows_done, field, before):
    tracers, rows, high, wide = field.shape
    lane = lax.broadcasted_iota(jnp.int32, (8, LANES), 1)
    for at in range(0, high, 8):
        strip = slice(at, at + 8)
        west, east = before(strip)
        for t in range(tracers):
            for j in rows_done:
                row = t * rows + j
                first = pltpu.roll(field[t, j, strip, :LANES], row, 1)
                last = pltpu.roll(field[t, j, strip, wide - LANES :], (row + 1) % LANES, 1)
                west = jnp.where(lane == row, first, west)
                east = jnp.where(lane == row, last, east)
        yield strip, west, east


def no_ends(strip):
    return jnp.zeros((8, LANES), jnp.float32), jnp.zeros((8, LANES), jnp.float32)


def hand_out(odd_ref, field, rows_done, before, near_ref, far_ref, pair_ref, other_ref):
    odd_lon = odd_ref[1] != 0
    for strip, west, east in collect_ends(rows_done, field, before):
        pair_ref[strip, :] = jnp.where(odd_lon, west, east)
        other_ref[strip, :] = jnp.where(odd_lon, east, west)
    last = field.shape[1] - 1
    odd = odd_ref[0]

    @pl.when(odd == 0)
    def _():
        near_ref[...] = field[:, last]
        far_ref[...] = field[:, 0]

    @pl.when(odd != 0)
    def _():
        near_ref[...] = field[:, 0]
        far_ref[...] = field[:, last]


def prepare_kernel(terminal_in, courant_in, out, stage, sems):
    moves = []
    for source in (terminal_in, courant_in):
        for part in range(source.shape[0]):
            at = len(moves) // out.shape[1]
            for j in range(out.shape[1]):
                sem = sems.at[len(moves)]
                load = pltpu.make_async_copy(source.at[part, :, j, :], stage.at[at, j], sem)
                moves.append((load, pltpu.make_async_copy(stage.at[at, j], out.at[at, j], sem)))
                load.start()
    for load, save in moves:
        load.wait()
        save.start()
    for load, save in moves:
        save.wait()


def prepare(terminal, courant):
    _, rows, levels, wide = terminal.shape
    parts = terminal.shape[0] + courant.shape[0]
    return pl.pallas_call(
        prepare_kernel,
        out_shape=jax.ShapeDtypeStruct((parts + SPARE, rows, levels, wide), terminal.dtype),
        in_specs=[HBM] * 2,
        out_specs=HBM,
        scratch_shapes=[
            pltpu.VMEM((parts, rows, levels, wide), terminal.dtype),
            pltpu.SemaphoreType.DMA((parts * rows,)),
        ],
        compiler_params=pltpu.CompilerParams(vmem_limit_bytes=60 * MIB),
    )(jnp.swapaxes(terminal, 1, 2), jnp.swapaxes(courant, 1, 2))


def start_kernel(devices, odd_ref, got_ref, weight_hbm, inputs_hbm, out_ref, near_ref, far_ref, pair_ref, other_ref, courant_ref,
                 terminal_ref, weight_ref, addr_v, addr_s, state, sems, *banks):
    tracers, rows, levels, wide = terminal_ref.shape
    columns = wide // LANES
    get_terminal = pltpu.make_async_copy(inputs_hbm.at[pl.ds(0, terminal_ref.shape[0])], terminal_ref, sems.at[1])
    get_weight = pltpu.make_async_copy(weight_hbm, weight_ref, sems.at[2])
    tracers, parts = terminal_ref.shape[0], courant_ref.shape[0]
    get_courant = pltpu.make_async_copy(inputs_hbm.at[pl.ds(tracers, parts)], courant_ref, sems.at[3])
    get_terminal.start()
    get_weight.start()
    get_courant.start()
    high = state.shape[1]
    whole = levels // 8 * 8
    for o in range(devices):
        addr_v[o : o + 1, :] = got_ref[o * SLOTS + 32].astype(jnp.int32)
    copy = pltpu.make_async_copy(addr_v, addr_s, sems.at[0])
    copy.start()
    clear = 64
    for bank in banks:

        @pl.loop(0, bank.shape[0] // clear)
        def _(i):
            bank[pl.ds(pl.multiple_of(i * clear, clear), clear), :] = jnp.zeros((clear, LANES), jnp.float32)

    copy.wait()

    @pl.loop(0, devices // BANKS)
    def _(group):
        first = group * BANKS
        most = addr_s[first, 32]
        for b in range(1, BANKS):
            most = jnp.maximum(most, addr_s[first + b, 32])

        @pl.loop(0, (most + 7) // 8)
        def _(c):
            for u in range(8):
                for b, bank in enumerate(banks):
                    place = addr_s[first + b, c * 8 + u]
                    bank[pl.ds(place, 1), :] += got_ref[(first + b) * SLOTS + c * 8 + u]

    for slot in range(state.shape[0]):
        state[slot, levels:high, :] = jnp.zeros((high - levels, wide), jnp.float32)
    get_terminal.wait()
    get_weight.wait()
    for j in range(rows):
        weight = weight_ref[j]
        for t in range(tracers):
            slot = (j * tracers + t) % state.shape[0]
            for c in range(columns):
                tile = slice(c * LANES, (c + 1) * LANES)
                base = ((t * rows + j) * columns + c) * high
                for low, top in ((0, whole), (whole, levels)):
                    total = terminal_ref[t, j, low:top, tile]
                    for bank in banks:
                        total = total + bank[base + low : base + top, :]
                    state[slot, low:top, tile] = total
            for at in range(0, wide, 2 * LANES):
                out_ref[t, j, :, at : at + 2 * LANES] = vertical(weight, state[slot, :, at : at + 2 * LANES])
    hand_out(odd_ref, out_ref, range(rows), no_ends, near_ref, far_ref, pair_ref, other_ref)
    get_courant.wait()


def shapes_of(tracers, rows, high, wide):
    f32 = jnp.float32
    edge = jax.ShapeDtypeStruct((tracers, high, wide), f32)
    end = jax.ShapeDtypeStruct((high, LANES), f32)
    return jax.ShapeDtypeStruct((tracers, rows, high, wide), f32), edge, edge, end, end


def start(odd, got, weight, inputs, tracers, high, devices):
    f32 = jnp.float32
    parts, rows, levels, wide = inputs.shape
    places = tracers * rows * (wide // LANES) * high
    return pl.pallas_call(
        functools.partial(start_kernel, devices),
        out_shape=shapes_of(tracers, rows, high, wide)
        + (jax.ShapeDtypeStruct((parts - SPARE - tracers, rows, levels, wide), f32),),
        in_specs=[SMEM, VMEM, HBM, HBM],
        out_specs=(VMEM,) * 6,
        scratch_shapes=[
            pltpu.VMEM((tracers, rows, levels, wide), f32),
            pltpu.VMEM(weight.shape, weight.dtype),
            pltpu.VMEM((devices, LANES), jnp.int32),
            pltpu.SMEM((devices, LANES), jnp.int32),
            pltpu.VMEM((2, high, wide), f32),
            pltpu.SemaphoreType.DMA((4,)),
        ]
        + [pltpu.VMEM((places + 64, LANES), f32) for _ in range(BANKS)],
        compiler_params=pltpu.CompilerParams(vmem_limit_bytes=36 * MIB),
    )(odd, got, weight, inputs)


def ends_in_place(odd_ref, pair_ref, other_ref, west, east):
    odd = odd_ref[1] != 0
    pair, other = pair_ref[...], other_ref[...]
    west[...] = jnp.where(odd, pair, other)
    east[...] = jnp.where(odd, other, pair)


def transported(t, j, levels, field, courant_ref, mask, lat, west, east, store):
    rows, wide = field.shape[1], field.shape[3]
    row = t * rows + j
    tiles = [slice(c * LANES, (c + 1) * LANES) for c in range(wide // LANES)]
    for at in range(0, levels, 8):
        count = min(8, levels - at)
        strip = slice(at, at + count)
        lane = lax.broadcasted_iota(jnp.int32, (count, LANES), 1)
        here = [field[t, j, strip, tile] for tile in tiles]
        left = [pltpu.roll(x, LANES - 1, 1) for x in here]
        left.append(pltpu.roll(east[strip, :], LANES - 1 - row, 1))
        right = [pltpu.roll(west[strip, :], (LANES - row) % LANES, 1)]
        right += [pltpu.roll(x, 1, 1) for x in here]
        for c, tile in enumerate(tiles):
            v = here[c]
            e = jnp.where(lane == LANES - 1, left[c + 1], left[c])
            w = jnp.where(lane == 0, right[c], right[c + 1])
            n = lat[0](t, strip, tile) if j == rows - 1 else field[t, j + 1, strip, tile]
            s = lat[1](t, strip, tile) if j == 0 else field[t, j - 1, strip, tile]
            moved = (
                v
                + courant_ref[0, j, strip, tile] * (e - v)
                + courant_ref[1, j, strip, tile] * (w - v)
                + courant_ref[2, j, strip, tile] * (n - v)
                + courant_ref[3, j, strip, tile] * (s - v)
            )
            store(strip, tile, mask[c] * moved)


def mask_row(mask_ref, j):
    wide = mask_ref.shape[1]
    return [mask_ref[j : j + 1, c : c + LANES].astype(jnp.float32) for c in range(0, wide, LANES)]


def beyond(halo_ref):
    read = lambda t, strip, tile: halo_ref[t, strip, tile]
    return read, read


def each_row(odd_ref, rows, inner, near, do):
    if inner:
        for j in range(1, rows - 1):
            do(j)
    for j in (0, rows - 1):
        pl.when((odd_ref[0] != 0) == ((j == 0) == near))(functools.partial(do, j))


def advance(levels, lat, field, courant_ref, mask_ref, hw, he, weight_ref, out_ref, state):
    tracers, rows, high, wide = field.shape
    for slot in range(state.shape[0]):
        state[slot, levels:high, :] = jnp.zeros((high - levels, wide), jnp.float32)

    def do(j):
        mask = mask_row(mask_ref, j)
        weight = weight_ref[j]
        for t in range(tracers):
            slot = (j * tracers + t) % state.shape[0]

            def store(strip, tile, value):
                state[slot, strip, tile] = value

            transported(t, j, levels, field, courant_ref, mask, lat, hw, he, store)
            for at in range(0, wide, 2 * LANES):
                out_ref[t, j, :, at : at + 2 * LANES] = vertical(weight, state[slot, :, at : at + 2 * LANES])

    return do


def body_kernel(levels, field, courant_ref, mask_ref, out_ref, none):
    none[...] = jnp.zeros_like(none)
    tracers, rows = field.shape[:2]
    for j in range(1, rows - 1):
        mask = mask_row(mask_ref, j)
        for t in range(tracers):

            def store(strip, tile, value):
                out_ref[t, j, strip, tile] = value

            transported(t, j, levels, field, courant_ref, mask, None, none, none, store)


def body(levels, field, courant, mask):
    tracers, rows, high, wide = field.shape
    return pl.pallas_call(
        functools.partial(body_kernel, levels),
        out_shape=jax.ShapeDtypeStruct((tracers, rows, levels, wide), jnp.float32),
        in_specs=[VMEM] * 3,
        out_specs=VMEM,
        scratch_shapes=[pltpu.VMEM((high, LANES), jnp.float32)],
        compiler_params=pltpu.CompilerParams(vmem_limit_bytes=LIMIT * MIB),
        cost_estimate=COST,
    )(field, courant, mask)


def patched(t, j, levels, body_ref, courant_ref, mask, hw, he, rows, store):
    wide = body_ref.shape[3]
    row = t * rows + j
    first, last = slice(0, LANES), slice(wide - LANES, wide)
    for at in range(0, levels, 8):
        count = min(8, levels - at)
        strip = slice(at, at + count)
        lane = lax.broadcasted_iota(jnp.int32, (count, LANES), 1)
        w = jnp.where(lane == 0, pltpu.roll(hw[strip, :], (LANES - row) % LANES, 1), 0.0)
        e = jnp.where(lane == LANES - 1, pltpu.roll(he[strip, :], LANES - 1 - row, 1), 0.0)
        store(strip, 0, body_ref[t, j, strip, first] + mask[0] * (courant_ref[1, j, strip, first] * w))
        store(strip, 1, body_ref[t, j, strip, last] + mask[-1] * (courant_ref[0, j, strip, last] * e))


def inner_kernel(levels, odd_ref, pair_ref, other_ref, field, courant_ref, mask_ref, weight_ref, near_in, body_ref,
                 out_ref, west, east, hw, he, state):
    ends_in_place(odd_ref, pair_ref, other_ref, hw, he)
    tracers, rows, high, wide = field.shape
    do = advance(levels, beyond(near_in), field, courant_ref, mask_ref, hw, he, weight_ref, out_ref, state)
    for j in range(1, rows - 1):
        mask = mask_row(mask_ref, j)
        for t in range(tracers):
            slot = (j * tracers + t) % state.shape[0]

            def store(strip, side, value):
                state[slot, strip, side * (wide - LANES) : side * (wide - LANES) + LANES] = value

            patched(t, j, levels, body_ref, courant_ref, mask, hw, he, rows, store)
            state[slot, :levels, LANES : wide - LANES] = body_ref[t, j, :, LANES : wide - LANES]
            for at in range(0, wide, 2 * LANES):
                out_ref[t, j, :, at : at + 2 * LANES] = vertical(weight_ref[j], state[slot, :, at : at + 2 * LANES])
    each_row(odd_ref, rows, False, True, do)
    for strip, first, last in collect_ends(range(1, rows - 1), out_ref, no_ends):
        west[strip, :] = first
        east[strip, :] = last


def edge_kernel(levels, odd_ref, pair_ref, other_ref, field, courant_ref, mask_ref, weight_ref, far_in,
                part_ref, west, east, out_ref, near_ref, far_ref, pair_out, other_out, hw, he, state):
    ends_in_place(odd_ref, pair_ref, other_ref, hw, he)
    rows = field.shape[1]
    do = advance(levels, beyond(far_in), field, courant_ref, mask_ref, hw, he, weight_ref, out_ref, state)
    each_row(odd_ref, rows, False, False, do)
    before = lambda strip: (west[strip, :], east[strip, :])
    hand_out(odd_ref, out_ref, (0, rows - 1), before, near_ref, far_ref, pair_out, other_out)


COST = pl.CostEstimate(flops=1_000_000_000, bytes_accessed=8_000_000, transcendentals=0)


def step(levels, odd, field, courant, mask, weight, halos):
    f32 = jnp.float32
    near, far, pair, other = halos
    tracers, rows, high, wide = field.shape
    field_shape, edge, _, end, _ = shapes_of(tracers, rows, high, wide)
    scratch = [pltpu.VMEM((high, LANES), f32)] * 2 + [pltpu.VMEM((2, high, wide), f32)]
    params = pltpu.CompilerParams(vmem_limit_bytes=LIMIT * MIB)
    part, west, east = pl.pallas_call(
        functools.partial(inner_kernel, levels),
        out_shape=(field_shape, end, end),
        in_specs=[SMEM] + [VMEM] * 8,
        out_specs=(VMEM,) * 3,
        scratch_shapes=scratch,
        compiler_params=params,
        cost_estimate=COST,
    )(odd, pair, other, field, courant, mask, weight, near, body(levels, field, courant, mask))
    return pl.pallas_call(
        functools.partial(edge_kernel, levels),
        out_shape=(field_shape, edge, edge, end, end),
        in_specs=[SMEM] + [VMEM] * 10,
        out_specs=(VMEM,) * 5,
        scratch_shapes=scratch,
        input_output_aliases={8: 0},
        compiler_params=params,
    )(odd, pair, other, field, courant, mask, weight, far, part, west, east)


def finish(levels, lat, field, courant_ref, mask_ref, hw, he, out_ref, state, sems, flying=None):
    tracers, rows = field.shape[:2]
    slots = state.shape[0]

    def do(j):
        started = []
        for t in range(tracers):
            slot = (j * tracers + t) % slots

            def store(strip, tile, value):
                state[slot, strip, tile] = value

            transported(t, j, levels, field, courant_ref, mask_row(mask_ref, j), lat, hw, he, store)
            copy = pltpu.make_async_copy(state.at[slot], out_ref.at[t, :, j, :], sems.at[slot])
            copy.start()
            started.append(copy)
        if flying is not None and 0 < j < rows - 1:
            flying.extend(started)
        else:
            for copy in started:
                copy.wait()

    return do


def final_inner_kernel(levels, odd_ref, pair_ref, other_ref, field, courant_ref, mask_ref, near_in, body_ref, out_ref,
                       hw, he, state, sems, sides, side_sems):
    tracers, rows, _, wide = field.shape
    middle = pl.ds(LANES, wide - 2 * LANES)
    flying = []
    for j in range(1, rows - 1):
        for t in range(tracers):
            flying.append(pltpu.make_async_copy(
                body_ref.at[t, j, :, middle], out_ref.at[t, :, j, middle], sems.at[j * tracers + t]
            ))
            flying[-1].start()
    ends_in_place(odd_ref, pair_ref, other_ref, hw, he)
    for j in range(1, rows - 1):
        mask = mask_row(mask_ref, j)
        for t in range(tracers):
            slot = j * tracers + t

            def store(strip, side, value):
                sides[slot, side, strip, :] = value

            patched(t, j, levels, body_ref, courant_ref, mask, hw, he, rows, store)
            for side in (0, 1):
                flying.append(pltpu.make_async_copy(
                    sides.at[slot, side],
                    out_ref.at[t, :, j, pl.ds(side * (wide - LANES), LANES)],
                    side_sems.at[slot * 2 + side],
                ))
                flying[-1].start()
    do = finish(levels, beyond(near_in), field, courant_ref, mask_ref, hw, he, out_ref, state, sems)
    each_row(odd_ref, rows, False, True, do)
    for copy in flying:
        copy.wait()


def final_edge_kernel(levels, odd_ref, pair_ref, other_ref, field, courant_ref, mask_ref, far_in, part_ref,
                      out_ref, hw, he, state, sems):
    ends_in_place(odd_ref, pair_ref, other_ref, hw, he)
    do = finish(levels, beyond(far_in), field, courant_ref, mask_ref, hw, he, out_ref, state, sems)
    each_row(odd_ref, field.shape[1], False, False, do)


def last_step(levels, odd, field, courant, mask, halos):
    f32 = jnp.float32
    near, far, pair, other = halos
    tracers, rows, high, wide = field.shape
    slots = tracers * rows
    scratch = [pltpu.VMEM((high, LANES), f32)] * 2 + [
        pltpu.VMEM((slots, levels, wide), f32),
        pltpu.SemaphoreType.DMA((slots,)),
    ]
    shape = jax.ShapeDtypeStruct((tracers, levels, rows, wide), f32)
    params = pltpu.CompilerParams(vmem_limit_bytes=LIMIT * MIB)
    part = pl.pallas_call(
        functools.partial(final_inner_kernel, levels),
        out_shape=shape,
        in_specs=[SMEM] + [VMEM] * 7,
        out_specs=HBM,
        scratch_shapes=scratch
        + [pltpu.VMEM((slots, 2, levels, LANES), f32), pltpu.SemaphoreType.DMA((2 * slots,))],
        compiler_params=params,
        cost_estimate=COST,
    )(odd, pair, other, field, courant, mask, near, body(levels, field, courant, mask))
    return pl.pallas_call(
        functools.partial(final_edge_kernel, levels),
        out_shape=shape,
        in_specs=[SMEM] + [VMEM] * 6 + [HBM],
        out_specs=HBM,
        scratch_shapes=scratch,
        input_output_aliases={7: 0},
        compiler_params=params,
    )(odd, pair, other, field, courant, mask, far, part)


def weights(inverse, high):
    rows, levels, _ = inverse.shape
    turned = jnp.swapaxes(inverse, 1, 2)
    pad = ((0, 0), (0, high - levels), (0, high - levels))
    whole = jnp.pad(lax.reduce_precision(turned, 8, 7), pad)
    rest = jnp.pad(turned, pad) - whole
    return jnp.concatenate(
        [jnp.concatenate([whole, whole], 2), jnp.concatenate([rest, rest], 2)], 1
    ).astype(jnp.bfloat16)


def exchange(near, far, pair, other):
    lat = lax.axis_size("lat")
    lon = lax.axis_size("lon")
    next_pair = [(i, i + 1 if i % 2 else i - 1) for i in range(1, lat - 1)]
    other = lax.ppermute(other, "lon", [(i, (i + 1 if i % 2 else i - 1) % lon) for i in range(lon)])
    pair = lax.ppermute(pair, "lon", [(i, i ^ 1) for i in range(lon)])
    far = lax.ppermute(far, "lat", next_pair)
    near = lax.ppermute(near, "lat", [(i, i ^ 1) for i in range(lat)])
    return near, far, pair, other


def local(terminal, courant, inverse, land_mask, obs_values, obs_owner, obs_cell):
    devices = lax.axis_size("lat") * lax.axis_size("lon")
    tracers, rows, levels, wide = terminal.shape
    high = padded_levels(levels)
    odd = jnp.stack([lax.axis_index("lat") % 2, lax.axis_index("lon") % 2]).astype(jnp.int32)
    send = pack(obs_owner, obs_cell, obs_values, levels, high, wide // LANES, devices)
    got = lax.all_to_all(send, ("lat", "lon"), split_axis=0, concat_axis=0, tiled=True)
    inputs = prepare(terminal, courant)
    weight = weights(inverse, high)
    field, *edges, courant = start(odd, got, weight, inputs, tracers, high, devices)
    for _ in range(STEPS - 1):
        field, *edges = step(levels, odd, field, courant, land_mask, weight, exchange(*edges))
    out = last_step(levels, odd, field, courant, land_mask, exchange(*edges))
    return jnp.swapaxes(out, 1, 2)


def solution(mesh):
    placed = (
        P(None, "lat", None, "lon"),
        P(None, "lat", None, "lon"),
        P("lat", None, None),
        P("lat", "lon"),
        P(("lat", "lon"), None),
        P(("lat", "lon"), None),
        P(("lat", "lon")),
    )
    return jax.shard_map(
        local, mesh=mesh, in_specs=placed, out_specs=P(None, "lat", None, "lon"), check_vma=False
    )
```

```python
import functools

import jax
import jax.numpy as jnp
from jax import lax
from jax.experimental import pallas as pl
from jax.experimental.pallas import tpu as pltpu
from jax.sharding import PartitionSpec as P

STEPS = 2
LANES = 128
SLOTS = 33
BANKS = 4
MIB = 1 << 20


def padded_levels(levels):
    return -(-levels // 8) * 8


SPARE = 10
LIMIT = 26
VMEM = pl.BlockSpec(memory_space=pltpu.VMEM)
SMEM = pl.BlockSpec(memory_space=pltpu.SMEM)
HBM = pl.BlockSpec(memory_space=pltpu.HBM)


def pack_kernel(geometry, owner_hbm, cell_hbm, values_hbm, send_ref, slot_ref, owner_ref, cell_ref, values_ref, slots, pay, sems):
    levels, high, columns, devices = geometry
    per_row = levels * columns
    chunks = owner_ref.shape[0]
    f32, bf16 = jnp.float32, jnp.bfloat16
    get_owner = pltpu.make_async_copy(owner_hbm, owner_ref, sems.at[0])
    get_cell = pltpu.make_async_copy(cell_hbm, cell_ref, sems.at[1])
    get_values = pltpu.make_async_copy(values_hbm, values_ref, sems.at[2])
    get_owner.start()
    get_cell.start()
    get_values.start()
    sub = lax.broadcasted_iota(jnp.int32, (LANES, LANES), 0)
    lane = lax.broadcasted_iota(jnp.int32, (LANES, LANES), 1)
    before = jnp.concatenate(
        [jnp.where(sub < lane, 1.0, 0.0), jnp.ones((LANES, LANES), f32)], axis=1
    ).astype(bf16)
    get_owner.wait()
    get_cell.wait()
    cells = cell_ref[...]
    tile_row = ((cells >> 4) * 5243) >> 17
    rest = cells - tile_row * per_row
    level = rest >> 2
    column = rest & 3
    place = (tile_row * columns + column) * high + level
    upper, lower = (place >> 6).astype(f32), (place & 63).astype(f32)
    carry = jnp.zeros((LANES, LANES), f32)
    total = jnp.zeros((LANES, LANES), f32)
    for i in range(chunks):
        own = owner_ref[i : i + 1, :]
        hot = jnp.where(sub == own, 1.0, 0.0)
        hot16 = hot.astype(bf16)
        counted = jnp.dot(hot16, before, preferred_element_type=f32)
        rank = jnp.sum(hot * (counted[:, :LANES] + carry), axis=0, keepdims=True)
        carry = carry + counted[:, LANES:]
        rank_i = rank.astype(jnp.int32)
        slots[i : i + 1, :] = own * SLOTS + rank_i
        near_sub = sub[:64]
        parts = jnp.where(
            near_sub == rank_i,
            jnp.broadcast_to(upper[i : i + 1, :], (64, LANES)),
            jnp.where(near_sub == rank_i + 32, jnp.broadcast_to(lower[i : i + 1, :], (64, LANES)), 0.0),
        )
        parts = jnp.concatenate([parts, jnp.zeros_like(parts)], axis=0).astype(bf16)
        total = total + lax.dot_general(
            hot16, parts, (((1,), (1,)), ((), ())), preferred_element_type=f32
        )
    copy = pltpu.make_async_copy(slots, slot_ref, sems.at[3])
    copy.start()
    places = total * 64.0 + pltpu.roll(total, LANES - 32, 1)
    dump = f32(2 * 8 * columns * high)
    pay[...] = jnp.where(
        lane < 32, jnp.where(lane.astype(f32) < carry, places, dump), carry
    )
    for o in range(devices):
        send_ref[o * SLOTS + 32] = pay[o : o + 1, :]
    get_values.wait()
    copy.wait()
    unroll = 64
    for i in range(chunks):

        @pl.loop(0, LANES // unroll)
        def _(c):
            base = c * unroll
            for u in range(unroll):
                send_ref[slot_ref[i, base + u]] = values_ref[i * LANES + base + u]


def pack(owner, cell, values, levels, high, columns, devices):
    rows = values.shape[0]
    chunks = rows // LANES
    return pl.pallas_call(
        functools.partial(pack_kernel, (levels, high, columns, devices)),
        out_shape=jax.ShapeDtypeStruct((devices * SLOTS, 1, LANES), jnp.float32),
        in_specs=[HBM] * 3,
        out_specs=VMEM,
        scratch_shapes=[
            pltpu.SMEM((chunks, LANES), jnp.int32),
            pltpu.VMEM((chunks, LANES), jnp.int32),
            pltpu.VMEM((chunks, LANES), jnp.int32),
            pltpu.VMEM((rows, 1, LANES), jnp.float32),
            pltpu.VMEM((chunks, LANES), jnp.int32),
            pltpu.VMEM((LANES, LANES), jnp.float32),
            pltpu.SemaphoreType.DMA((4,)),
        ],
        compiler_params=pltpu.CompilerParams(vmem_limit_bytes=60 * MIB),
    )(owner.reshape(chunks, LANES), cell.reshape(chunks, LANES), values.reshape(rows, 1, LANES))


def vertical(weight, cells):
    high = cells.shape[0]
    whole = cells.astype(jnp.bfloat16).astype(jnp.float32)
    both = jnp.concatenate([whole, cells - whole], axis=0).astype(jnp.bfloat16)
    product = jnp.dot(weight, both, preferred_element_type=jnp.float32)
    return product[:high] + product[high:]


def collect_ends(rows_done, field, before):
    tracers, rows, high, wide = field.shape
    lane = lax.broadcasted_iota(jnp.int32, (8, LANES), 1)
    for at in range(0, high, 8):
        strip = slice(at, at + 8)
        west, east = before(strip)
        for t in range(tracers):
            for j in rows_done:
                row = t * rows + j
                first = pltpu.roll(field[t, j, strip, :LANES], row, 1)
                last = pltpu.roll(field[t, j, strip, wide - LANES :], (row + 1) % LANES, 1)
                west = jnp.where(lane == row, first, west)
                east = jnp.where(lane == row, last, east)
        yield strip, west, east


def no_ends(strip):
    return jnp.zeros((8, LANES), jnp.float32), jnp.zeros((8, LANES), jnp.float32)


def hand_out(odd_ref, field, rows_done, before, near_ref, far_ref, pair_ref, other_ref):
    odd_lon = odd_ref[1] != 0
    for strip, west, east in collect_ends(rows_done, field, before):
        pair_ref[strip, :] = jnp.where(odd_lon, west, east)
        other_ref[strip, :] = jnp.where(odd_lon, east, west)
    last = field.shape[1] - 1
    odd = odd_ref[0]

    @pl.when(odd == 0)
    def _():
        near_ref[...] = field[:, last]
        far_ref[...] = field[:, 0]

    @pl.when(odd != 0)
    def _():
        near_ref[...] = field[:, 0]
        far_ref[...] = field[:, last]


def prepare_kernel(terminal_in, courant_in, out, stage, sems):
    moves = []
    for source in (terminal_in, courant_in):
        for part in range(source.shape[0]):
            at = len(moves) // out.shape[1]
            for j in range(out.shape[1]):
                sem = sems.at[len(moves)]
                load = pltpu.make_async_copy(source.at[part, :, j, :], stage.at[at, j], sem)
                moves.append((load, pltpu.make_async_copy(stage.at[at, j], out.at[at, j], sem)))
                load.start()
    for load, save in moves:
        load.wait()
        save.start()
    for load, save in moves:
        save.wait()


def prepare(terminal, courant):
    _, rows, levels, wide = terminal.shape
    parts = terminal.shape[0] + courant.shape[0]
    return pl.pallas_call(
        prepare_kernel,
        out_shape=jax.ShapeDtypeStruct((parts + SPARE, rows, levels, wide), terminal.dtype),
        in_specs=[HBM] * 2,
        out_specs=HBM,
        scratch_shapes=[
            pltpu.VMEM((parts, rows, levels, wide), terminal.dtype),
            pltpu.SemaphoreType.DMA((parts * rows,)),
        ],
        compiler_params=pltpu.CompilerParams(vmem_limit_bytes=60 * MIB),
    )(jnp.swapaxes(terminal, 1, 2), jnp.swapaxes(courant, 1, 2))


def start_kernel(devices, odd_ref, got_ref, weight_hbm, inputs_hbm, out_ref, near_ref, far_ref, pair_ref, other_ref, courant_ref,
                 terminal_ref, weight_ref, addr_v, addr_s, state, sems, *banks):
    tracers, rows, levels, wide = terminal_ref.shape
    columns = wide // LANES
    get_terminal = pltpu.make_async_copy(inputs_hbm.at[pl.ds(0, terminal_ref.shape[0])], terminal_ref, sems.at[1])
    get_weight = pltpu.make_async_copy(weight_hbm, weight_ref, sems.at[2])
    tracers, parts = terminal_ref.shape[0], courant_ref.shape[0]
    get_courant = pltpu.make_async_copy(inputs_hbm.at[pl.ds(tracers, parts)], courant_ref, sems.at[3])
    get_terminal.start()
    get_weight.start()
    get_courant.start()
    high = state.shape[1]
    whole = levels // 8 * 8
    for o in range(devices):
        addr_v[o : o + 1, :] = got_ref[o * SLOTS + 32].astype(jnp.int32)
    copy = pltpu.make_async_copy(addr_v, addr_s, sems.at[0])
    copy.start()
    clear = 64
    for bank in banks:

        @pl.loop(0, bank.shape[0] // clear)
        def _(i):
            bank[pl.ds(pl.multiple_of(i * clear, clear), clear), :] = jnp.zeros((clear, LANES), jnp.float32)

    copy.wait()

    @pl.loop(0, devices // BANKS)
    def _(group):
        first = group * BANKS
        most = addr_s[first, 32]
        for b in range(1, BANKS):
            most = jnp.maximum(most, addr_s[first + b, 32])

        @pl.loop(0, (most + 7) // 8)
        def _(c):
            for u in range(8):
                for b, bank in enumerate(banks):
                    place = addr_s[first + b, c * 8 + u]
                    bank[pl.ds(place, 1), :] += got_ref[(first + b) * SLOTS + c * 8 + u]

    for slot in range(state.shape[0]):
        state[slot, levels:high, :] = jnp.zeros((high - levels, wide), jnp.float32)
    get_terminal.wait()
    get_weight.wait()
    for j in range(rows):
        weight = weight_ref[j]
        for t in range(tracers):
            slot = (j * tracers + t) % state.shape[0]
            for c in range(columns):
                tile = slice(c * LANES, (c + 1) * LANES)
                base = ((t * rows + j) * columns + c) * high
                for low, top in ((0, whole), (whole, levels)):
                    total = terminal_ref[t, j, low:top, tile]
                    for bank in banks:
                        total = total + bank[base + low : base + top, :]
                    state[slot, low:top, tile] = total
            for at in range(0, wide, 2 * LANES):
                out_ref[t, j, :, at : at + 2 * LANES] = vertical(weight, state[slot, :, at : at + 2 * LANES])
    hand_out(odd_ref, out_ref, range(rows), no_ends, near_ref, far_ref, pair_ref, other_ref)
    get_courant.wait()


def shapes_of(tracers, rows, high, wide):
    f32 = jnp.float32
    edge = jax.ShapeDtypeStruct((tracers, high, wide), f32)
    end = jax.ShapeDtypeStruct((high, LANES), f32)
    return jax.ShapeDtypeStruct((tracers, rows, high, wide), f32), edge, edge, end, end


def start(odd, got, weight, inputs, tracers, high, devices):
    f32 = jnp.float32
    parts, rows, levels, wide = inputs.shape
    places = tracers * rows * (wide // LANES) * high
    return pl.pallas_call(
        functools.partial(start_kernel, devices),
        out_shape=shapes_of(tracers, rows, high, wide)
        + (jax.ShapeDtypeStruct((parts - SPARE - tracers, rows, levels, wide), f32),),
        in_specs=[SMEM, VMEM, HBM, HBM],
        out_specs=(VMEM,) * 6,
        scratch_shapes=[
            pltpu.VMEM((tracers, rows, levels, wide), f32),
            pltpu.VMEM(weight.shape, weight.dtype),
            pltpu.VMEM((devices, LANES), jnp.int32),
            pltpu.SMEM((devices, LANES), jnp.int32),
            pltpu.VMEM((2, high, wide), f32),
            pltpu.SemaphoreType.DMA((4,)),
        ]
        + [pltpu.VMEM((places + 64, LANES), f32) for _ in range(BANKS)],
        compiler_params=pltpu.CompilerParams(vmem_limit_bytes=36 * MIB),
    )(odd, got, weight, inputs)


def ends_in_place(odd_ref, pair_ref, other_ref, west, east):
    odd = odd_ref[1] != 0
    pair, other = pair_ref[...], other_ref[...]
    west[...] = jnp.where(odd, pair, other)
    east[...] = jnp.where(odd, other, pair)


def transported(t, j, levels, field, courant_ref, mask, lat, west, east, store):
    rows, wide = field.shape[1], field.shape[3]
    row = t * rows + j
    tiles = [slice(c * LANES, (c + 1) * LANES) for c in range(wide // LANES)]
    for at in range(0, levels, 8):
        count = min(8, levels - at)
        strip = slice(at, at + count)
        lane = lax.broadcasted_iota(jnp.int32, (count, LANES), 1)
        here = [field[t, j, strip, tile] for tile in tiles]
        left = [pltpu.roll(x, LANES - 1, 1) for x in here]
        left.append(pltpu.roll(east[strip, :], LANES - 1 - row, 1))
        right = [pltpu.roll(west[strip, :], (LANES - row) % LANES, 1)]
        right += [pltpu.roll(x, 1, 1) for x in here]
        for c, tile in enumerate(tiles):
            v = here[c]
            e = jnp.where(lane == LANES - 1, left[c + 1], left[c])
            w = jnp.where(lane == 0, right[c], right[c + 1])
            n = lat[0](t, strip, tile) if j == rows - 1 else field[t, j + 1, strip, tile]
            s = lat[1](t, strip, tile) if j == 0 else field[t, j - 1, strip, tile]
            moved = (
                v
                + courant_ref[0, j, strip, tile] * (e - v)
                + courant_ref[1, j, strip, tile] * (w - v)
                + courant_ref[2, j, strip, tile] * (n - v)
                + courant_ref[3, j, strip, tile] * (s - v)
            )
            store(strip, tile, mask[c] * moved)


def mask_row(mask_ref, j):
    wide = mask_ref.shape[1]
    return [mask_ref[j : j + 1, c : c + LANES].astype(jnp.float32) for c in range(0, wide, LANES)]


def beyond(halo_ref):
    read = lambda t, strip, tile: halo_ref[t, strip, tile]
    return read, read


def each_row(odd_ref, rows, inner, near, do):
    if inner:
        for j in range(1, rows - 1):
            do(j)
    for j in (0, rows - 1):
        pl.when((odd_ref[0] != 0) == ((j == 0) == near))(functools.partial(do, j))


def advance(levels, lat, field, courant_ref, mask_ref, hw, he, weight_ref, out_ref, state):
    tracers, rows, high, wide = field.shape
    for slot in range(state.shape[0]):
        state[slot, levels:high, :] = jnp.zeros((high - levels, wide), jnp.float32)

    def do(j):
        mask = mask_row(mask_ref, j)
        weight = weight_ref[j]
        for t in range(tracers):
            slot = (j * tracers + t) % state.shape[0]

            def store(strip, tile, value):
                state[slot, strip, tile] = value

            transported(t, j, levels, field, courant_ref, mask, lat, hw, he, store)
            for at in range(0, wide, 2 * LANES):
                out_ref[t, j, :, at : at + 2 * LANES] = vertical(weight, state[slot, :, at : at + 2 * LANES])

    return do


def body_kernel(levels, field, courant_ref, mask_ref, out_ref, none):
    none[...] = jnp.zeros_like(none)
    tracers, rows = field.shape[:2]
    for j in range(1, rows - 1):
        mask = mask_row(mask_ref, j)
        for t in range(tracers):

            def store(strip, tile, value):
                out_ref[t, j, strip, tile] = value

            transported(t, j, levels, field, courant_ref, mask, None, none, none, store)


def body(levels, field, courant, mask):
    tracers, rows, high, wide = field.shape
    return pl.pallas_call(
        functools.partial(body_kernel, levels),
        out_shape=jax.ShapeDtypeStruct((tracers, rows, levels, wide), jnp.float32),
        in_specs=[VMEM] * 3,
        out_specs=VMEM,
        scratch_shapes=[pltpu.VMEM((high, LANES), jnp.float32)],
        compiler_params=pltpu.CompilerParams(vmem_limit_bytes=LIMIT * MIB),
        cost_estimate=COST,
    )(field, courant, mask)


def patched(t, j, levels, body_ref, courant_ref, mask, hw, he, rows, store):
    wide = body_ref.shape[3]
    row = t * rows + j
    first, last = slice(0, LANES), slice(wide - LANES, wide)
    for at in range(0, levels, 8):
        count = min(8, levels - at)
        strip = slice(at, at + count)
        lane = lax.broadcasted_iota(jnp.int32, (count, LANES), 1)
        w = jnp.where(lane == 0, pltpu.roll(hw[strip, :], (LANES - row) % LANES, 1), 0.0)
        e = jnp.where(lane == LANES - 1, pltpu.roll(he[strip, :], LANES - 1 - row, 1), 0.0)
        store(strip, 0, body_ref[t, j, strip, first] + mask[0] * (courant_ref[1, j, strip, first] * w))
        store(strip, 1, body_ref[t, j, strip, last] + mask[-1] * (courant_ref[0, j, strip, last] * e))


def inner_kernel(levels, odd_ref, pair_ref, other_ref, field, courant_ref, mask_ref, weight_ref, near_in, body_ref,
                 out_ref, west, east, hw, he, state):
    ends_in_place(odd_ref, pair_ref, other_ref, hw, he)
    tracers, rows, high, wide = field.shape
    do = advance(levels, beyond(near_in), field, courant_ref, mask_ref, hw, he, weight_ref, out_ref, state)
    for j in range(1, rows - 1):
        mask = mask_row(mask_ref, j)
        for t in range(tracers):
            slot = (j * tracers + t) % state.shape[0]

            def store(strip, side, value):
                state[slot, strip, side * (wide - LANES) : side * (wide - LANES) + LANES] = value

            patched(t, j, levels, body_ref, courant_ref, mask, hw, he, rows, store)
            state[slot, :levels, LANES : wide - LANES] = body_ref[t, j, :, LANES : wide - LANES]
            for at in range(0, wide, 2 * LANES):
                out_ref[t, j, :, at : at + 2 * LANES] = vertical(weight_ref[j], state[slot, :, at : at + 2 * LANES])
    each_row(odd_ref, rows, False, True, do)
    for strip, first, last in collect_ends(range(1, rows - 1), out_ref, no_ends):
        west[strip, :] = first
        east[strip, :] = last


def edge_kernel(levels, odd_ref, pair_ref, other_ref, field, courant_ref, mask_ref, weight_ref, far_in,
                part_ref, west, east, out_ref, near_ref, far_ref, pair_out, other_out, hw, he, state):
    ends_in_place(odd_ref, pair_ref, other_ref, hw, he)
    rows = field.shape[1]
    do = advance(levels, beyond(far_in), field, courant_ref, mask_ref, hw, he, weight_ref, out_ref, state)
    each_row(odd_ref, rows, False, False, do)
    before = lambda strip: (west[strip, :], east[strip, :])
    hand_out(odd_ref, out_ref, (0, rows - 1), before, near_ref, far_ref, pair_out, other_out)


COST = pl.CostEstimate(flops=3_000_000_000, bytes_accessed=8_000_000, transcendentals=0)


def step(levels, odd, field, courant, mask, weight, halos):
    f32 = jnp.float32
    near, far, pair, other = halos
    tracers, rows, high, wide = field.shape
    field_shape, edge, _, end, _ = shapes_of(tracers, rows, high, wide)
    scratch = [pltpu.VMEM((high, LANES), f32)] * 2 + [pltpu.VMEM((2, high, wide), f32)]
    params = pltpu.CompilerParams(vmem_limit_bytes=LIMIT * MIB)
    part, west, east = pl.pallas_call(
        functools.partial(inner_kernel, levels),
        out_shape=(field_shape, end, end),
        in_specs=[SMEM] + [VMEM] * 8,
        out_specs=(VMEM,) * 3,
        scratch_shapes=scratch,
        compiler_params=params,
        cost_estimate=COST,
    )(odd, pair, other, field, courant, mask, weight, near, body(levels, field, courant, mask))
    return pl.pallas_call(
        functools.partial(edge_kernel, levels),
        out_shape=(field_shape, edge, edge, end, end),
        in_specs=[SMEM] + [VMEM] * 10,
        out_specs=(VMEM,) * 5,
        scratch_shapes=scratch,
        input_output_aliases={8: 0},
        compiler_params=params,
    )(odd, pair, other, field, courant, mask, weight, far, part, west, east)


def finish(levels, lat, field, courant_ref, mask_ref, hw, he, out_ref, state, sems, flying=None):
    tracers, rows = field.shape[:2]
    slots = state.shape[0]

    def do(j):
        started = []
        for t in range(tracers):
            slot = (j * tracers + t) % slots

            def store(strip, tile, value):
                state[slot, strip, tile] = value

            transported(t, j, levels, field, courant_ref, mask_row(mask_ref, j), lat, hw, he, store)
            copy = pltpu.make_async_copy(state.at[slot], out_ref.at[t, :, j, :], sems.at[slot])
            copy.start()
            started.append(copy)
        if flying is not None and 0 < j < rows - 1:
            flying.extend(started)
        else:
            for copy in started:
                copy.wait()

    return do


def final_inner_kernel(levels, odd_ref, pair_ref, other_ref, field, courant_ref, mask_ref, near_in, body_ref, out_ref,
                       hw, he, state, sems, sides, side_sems):
    tracers, rows, _, wide = field.shape
    middle = pl.ds(LANES, wide - 2 * LANES)
    flying = []
    for j in range(1, rows - 1):
        for t in range(tracers):
            flying.append(pltpu.make_async_copy(
                body_ref.at[t, j, :, middle], out_ref.at[t, :, j, middle], sems.at[j * tracers + t]
            ))
            flying[-1].start()
    ends_in_place(odd_ref, pair_ref, other_ref, hw, he)
    for j in range(1, rows - 1):
        mask = mask_row(mask_ref, j)
        for t in range(tracers):
            slot = j * tracers + t

            def store(strip, side, value):
                sides[slot, side, strip, :] = value

            patched(t, j, levels, body_ref, courant_ref, mask, hw, he, rows, store)
            for side in (0, 1):
                flying.append(pltpu.make_async_copy(
                    sides.at[slot, side],
                    out_ref.at[t, :, j, pl.ds(side * (wide - LANES), LANES)],
                    side_sems.at[slot * 2 + side],
                ))
                flying[-1].start()
    do = finish(levels, beyond(near_in), field, courant_ref, mask_ref, hw, he, out_ref, state, sems)
    each_row(odd_ref, rows, False, True, do)
    for copy in flying:
        copy.wait()


def final_edge_kernel(levels, odd_ref, pair_ref, other_ref, field, courant_ref, mask_ref, far_in, part_ref,
                      out_ref, hw, he, state, sems):
    ends_in_place(odd_ref, pair_ref, other_ref, hw, he)
    do = finish(levels, beyond(far_in), field, courant_ref, mask_ref, hw, he, out_ref, state, sems)
    each_row(odd_ref, field.shape[1], False, False, do)


def last_step(levels, odd, field, courant, mask, halos):
    f32 = jnp.float32
    near, far, pair, other = halos
    tracers, rows, high, wide = field.shape
    slots = tracers * rows
    scratch = [pltpu.VMEM((high, LANES), f32)] * 2 + [
        pltpu.VMEM((slots, levels, wide), f32),
        pltpu.SemaphoreType.DMA((slots,)),
    ]
    shape = jax.ShapeDtypeStruct((tracers, levels, rows, wide), f32)
    params = pltpu.CompilerParams(vmem_limit_bytes=LIMIT * MIB)
    part = pl.pallas_call(
        functools.partial(final_inner_kernel, levels),
        out_shape=shape,
        in_specs=[SMEM] + [VMEM] * 7,
        out_specs=HBM,
        scratch_shapes=scratch
        + [pltpu.VMEM((slots, 2, levels, LANES), f32), pltpu.SemaphoreType.DMA((2 * slots,))],
        compiler_params=params,
        cost_estimate=COST,
    )(odd, pair, other, field, courant, mask, near, body(levels, field, courant, mask))
    return pl.pallas_call(
        functools.partial(final_edge_kernel, levels),
        out_shape=shape,
        in_specs=[SMEM] + [VMEM] * 6 + [HBM],
        out_specs=HBM,
        scratch_shapes=scratch,
        input_output_aliases={7: 0},
        compiler_params=params,
    )(odd, pair, other, field, courant, mask, far, part)


def weights(inverse, high):
    rows, levels, _ = inverse.shape
    turned = jnp.swapaxes(inverse, 1, 2)
    pad = ((0, 0), (0, high - levels), (0, high - levels))
    whole = jnp.pad(lax.reduce_precision(turned, 8, 7), pad)
    rest = jnp.pad(turned, pad) - whole
    return jnp.concatenate(
        [jnp.concatenate([whole, whole], 2), jnp.concatenate([rest, rest], 2)], 1
    ).astype(jnp.bfloat16)


def exchange(near, far, pair, other):
    lat = lax.axis_size("lat")
    lon = lax.axis_size("lon")
    next_pair = [(i, i + 1 if i % 2 else i - 1) for i in range(1, lat - 1)]
    other = lax.ppermute(other, "lon", [(i, (i + 1 if i % 2 else i - 1) % lon) for i in range(lon)])
    pair = lax.ppermute(pair, "lon", [(i, i ^ 1) for i in range(lon)])
    far = lax.ppermute(far, "lat", next_pair)
    near = lax.ppermute(near, "lat", [(i, i ^ 1) for i in range(lat)])
    return near, far, pair, other


def local(terminal, courant, inverse, land_mask, obs_values, obs_owner, obs_cell):
    devices = lax.axis_size("lat") * lax.axis_size("lon")
    tracers, rows, levels, wide = terminal.shape
    high = padded_levels(levels)
    odd = jnp.stack([lax.axis_index("lat") % 2, lax.axis_index("lon") % 2]).astype(jnp.int32)
    send = pack(obs_owner, obs_cell, obs_values, levels, high, wide // LANES, devices)
    got = lax.all_to_all(send, ("lat", "lon"), split_axis=0, concat_axis=0, tiled=True)
    inputs = prepare(terminal, courant)
    weight = weights(inverse, high)
    field, *edges, courant = start(odd, got, weight, inputs, tracers, high, devices)
    for _ in range(STEPS - 1):
        field, *edges = step(levels, odd, field, courant, land_mask, weight, exchange(*edges))
    out = last_step(levels, odd, field, courant, land_mask, exchange(*edges))
    return jnp.swapaxes(out, 1, 2)


def solution(mesh):
    placed = (
        P(None, "lat", None, "lon"),
        P(None, "lat", None, "lon"),
        P("lat", None, None),
        P("lat", "lon"),
        P(("lat", "lon"), None),
        P(("lat", "lon"), None),
        P(("lat", "lon")),
    )
    return jax.shard_map(
        local, mesh=mesh, in_specs=placed, out_specs=P(None, "lat", None, "lon"), check_vma=False
    )
```
